32 devices in a mesh: dp: 16 (over z, x, core), lat: 2 (over y).
Axes of the slice: x: 2, y: 2, z: 4, core: 2. Of those that a mesh axis runs over, the one named last changes fastest.
Arguments:
- fields: bfloat16 [16, 48, 72, 641], P('dp', 'lat'), may hold values from -6 to 6
- noise_fields: bfloat16 [16, 2, 48, 576], P('dp', None, 'lat'), may hold values from -6 to 6
- step_counts: int32 [16], P('dp'), may hold values from 1 to 2, as said below
- spectral_flat: bfloat16 [2, 9986048], P('lat', 'dp'), may hold values from -0.25 to 0.25
- mlp_flat: bfloat16 [1650688], P(('dp', 'lat')), may hold values from -1.2 to 1.4
- cotangent: bfloat16 [16, 48, 72, 641], P('dp', 'lat'), may hold values from -6 to 6
Outputs:
- output_fields: bfloat16 [16, 48, 72, 641], P('dp', 'lat')
- fields_grad: bfloat16 [16, 48, 72, 641], P('dp', 'lat')
- spectral_grad: float32 [2, 9986048], P('lat', 'dp')
- mlp_grad: float32 [1650688], P(('dp', 'lat'))
The draws below stay inside these ranges and needn't reach their ends.
Inputs may be any that keep to these rules, and one draw needn't show every extreme that they name: `step_counts`: some date has 2 steps and some date has 1.
All inputs are finite; a program needn't handle non-finite values.
Results may differ from the reference program's by a relative error of at most 0.02.
Values may be sent and summed in bfloat16 or wider, within the bound.
A program may use at most 448 MiB of HBM per device.

```python
import math
import jax
import jax.numpy as jnp
import numpy as np
from jax import lax

D = 641
HID = 1282
NOISE = 8
NLAT = 48
NLON = 72
LDEG = 48
ORDERS = 36
STEPS = 2
CIN = 649
DATES = 16
DEG_DEV = 24
DEG_GROUPS = 2
SPEC_ROW = 9986048
MLP_PARAMS = 1648011
MLP_FLAT = 1650688


def draw_step_counts(key, part):
    key_one = jax.random.fold_in(key, 11)
    key_two = jax.random.fold_in(key, 12)
    key_three = jax.random.fold_in(key, 13)
    counts = jax.random.randint(key_one, (DATES,), 1, STEPS + 1)
    full_date = jax.random.randint(key_two, (), 0, DATES)
    short_date = (full_date + jax.random.randint(key_three, (), 1, DATES)) % DATES
    counts = counts.at[full_date].set(STEPS)
    counts = counts.at[short_date].set(1)
    return counts.astype(jnp.int32)


def draw_mlp_flat(key, part):
    keys_all = jax.random.split(jax.random.fold_in(key, 21), 9)

    def clipped(position, length, spread):
        return jnp.clip(jax.random.normal(keys_all[position], (length,), jnp.float32), -4.0, 4.0) * spread
    gain_one = jax.random.uniform(keys_all[0], (D,), jnp.float32, 0.6, 1.4)
    shift_one = clipped(1, D, 0.3)
    gain_two = jax.random.uniform(keys_all[2], (D,), jnp.float32, 0.6, 1.4)
    shift_two = clipped(3, D, 0.3)
    bias_hidden = clipped(4, HID, 0.3)
    bias_out = clipped(5, D, 0.1)
    w_in = clipped(6, D * HID, 1.0 / math.sqrt(D))
    w_out = clipped(7, HID * D, 1.0 / math.sqrt(HID))
    filler = clipped(8, MLP_FLAT - MLP_PARAMS, 0.05)
    joined = jnp.concatenate([gain_one, shift_one, gain_two, shift_two, bias_hidden, bias_out, w_in, w_out, filler])
    return joined.astype(jnp.bfloat16)


def block_scale(own_key, extent, cuts, low, largest):
    def one(dim, blocks):
        steps = jax.random.uniform(jax.random.fold_in(jax.random.fold_in(own_key, 6), dim), (blocks,), jnp.float32, low / len(cuts), largest / len(cuts))
        return jnp.repeat(jnp.exp(steps), extent[dim] // blocks).reshape((-1,) + (1,) * (len(extent) - dim - 1))

    factor_of = one(*cuts[0])
    for cut in cuts[1:]:
        factor_of = factor_of * one(*cut)
    return factor_of


def centred(key, shape, scale, limit, cuts=(), held_as=jnp.bfloat16):
    loudness = block_scale(key, shape, cuts, -0.22, 0.18) if cuts else 1.0
    drawn = jax.random.normal(key, shape, jnp.float32) * scale * loudness
    return jnp.minimum(jnp.maximum(drawn, -limit), limit).astype(held_as)


def setup_inputs(seed: int = 0) -> dict:
    arg_keys = jax.random.split(jax.random.key(seed), 7)
    fields = centred(arg_keys[0], (DATES, NLAT, NLON, D), 1.0, 6.0, ((0, 16), (1, 2)))
    noise_fields = centred(arg_keys[1], (DATES, STEPS, NLAT, NLON * NOISE), 1.0, 6.0, ((0, 16), (2, 2)))
    step_counts = draw_step_counts(jax.random.fold_in(arg_keys[6], 71), 0)
    spectral_flat = centred(arg_keys[3], (DEG_GROUPS, SPEC_ROW), CIN ** -0.5, 0.25, ((0, 2), (1, 16)))
    mlp_flat = draw_mlp_flat(jax.random.fold_in(arg_keys[6], 71), 0)
    cotangent = centred(arg_keys[5], (DATES, NLAT, NLON, D), 1.0, 6.0, ((0, 16), (1, 2)))
    return {"fields": fields, "noise_fields": noise_fields, "step_counts": step_counts, "spectral_flat": spectral_flat, "mlp_flat": mlp_flat, "cotangent": cotangent}


HIGHEST = lax.Precision.HIGHEST

@jax.custom_vjp
def low(v):
    return lax.optimization_barrier(v.astype(jnp.bfloat16)).astype(jnp.float32)

@jax.custom_vjp
def low_back(v):
    return v

def low_keep(v):
    return (low(v), None)

def low_pass(kept, grad):
    return (grad,)

def back_keep(v):
    return (v, None)

def back_low(kept, grad):
    return (low(grad),)
low.defvjp(low_keep, low_pass)
low_back.defvjp(back_keep, back_low)

def legendre_values(lat_total, degree_total, order_total):
    colatitude = np.pi * (np.arange(lat_total) + 0.5) / lat_total
    cosine = np.cos(colatitude)
    sine_part = np.sin(colatitude)
    legendre = np.zeros((lat_total, degree_total, order_total))
    diagonal = np.full(lat_total, 1.0 / math.sqrt(4.0 * math.pi))
    for column in range(order_total):
        if column > 0:
            diagonal = diagonal * math.sqrt((2.0 * column + 1.0) / (2.0 * column)) * sine_part
        legendre[:, column, column] = diagonal
        if column + 1 < degree_total:
            legendre[:, column + 1, column] = math.sqrt(2.0 * column + 3.0) * cosine * diagonal
        for degree in range(column + 2, degree_total):
            factor_one = math.sqrt((4.0 * degree * degree - 1.0) / (degree * degree - column * column))
            factor_two = math.sqrt(((degree - 1.0) ** 2 - column * column) / (4.0 * (degree - 1.0) ** 2 - 1.0))
            legendre[:, degree, column] = factor_one * (cosine * legendre[:, degree - 1, column] - factor_two * legendre[:, degree - 2, column])
    return (colatitude, legendre)

def spectral_tables(lat_total, lon_total, degree_total, order_total):
    colatitude, legendre = legendre_values(lat_total, degree_total, order_total)
    quadrature = np.sin(colatitude) * np.pi / lat_total
    angles = 2.0 * np.pi * np.outer(np.arange(lon_total), np.arange(order_total)) / lon_total
    fourier = np.concatenate([np.cos(angles), -np.sin(angles)], axis=1) * (2.0 * np.pi / lon_total)
    weights = np.where(np.arange(order_total) == 0, 1.0, 2.0)
    inverse = np.concatenate([np.cos(angles).T * weights[:, None], -np.sin(angles).T * weights[:, None]], axis=0)
    doubled = np.concatenate([legendre, legendre], axis=2)
    analysis = doubled * quadrature[:, None, None]
    return tuple((np.asarray(member, np.float32) for member in (fourier, inverse, analysis, doubled)))

def layer_norm(inputs, scale_gain, shift_vec):
    centered = inputs - lax.optimization_barrier(jnp.mean(inputs, axis=-1, keepdims=True))
    variance = lax.optimization_barrier(jnp.mean(centered * centered, axis=-1, keepdims=True))
    return centered * lax.rsqrt(variance + 1e-06) * scale_gain + shift_vec

def unpack_mlp(flat):
    pieces = []
    offset = 0
    for length in (D, D, D, D, HID, D):
        pieces.append(flat[offset:offset + length].astype(jnp.float32))
        offset = offset + length
    w_in = flat[offset:offset + D * HID].reshape(D, HID)
    offset = offset + D * HID
    w_out = flat[offset:offset + HID * D].reshape(HID, D)
    return (tuple(pieces), w_in, w_out)

def run_date(params, inputs):
    spectral, vectors, w_in, w_out = params
    gain_one, shift_one, gain_two, shift_two, bias_hidden, bias_out = vectors
    fourier, inverse, analysis, synthesis = [jnp.asarray(member) for member in spectral_tables(NLAT, NLON, LDEG, ORDERS)]
    current, noise_all, step_count = inputs
    for step_index in range(STEPS):
        step_mask = (step_index < step_count).astype(jnp.float32)
        normed = layer_norm(current, gain_one, shift_one)
        noise_step = noise_all[step_index].reshape(NLAT, NLON, NOISE)
        joined = jnp.concatenate([normed, noise_step], axis=-1)
        grid_modes = jnp.einsum('jnc,nk->jkc', joined, fourier, precision=HIGHEST)
        coeffs = low(low_back(jnp.einsum('jlk,jkc->lkc', analysis, grid_modes, precision=HIGHEST)))
        mixed_modes = low(low_back(jnp.einsum('lkc,lcd->lkd', coeffs, spectral, precision=HIGHEST)))
        lat_modes = jnp.einsum('jlk,lkd->jkd', synthesis, mixed_modes, precision=HIGHEST)
        branch = jnp.einsum('jkd,kn->jnd', lat_modes, inverse, precision=HIGHEST)
        middle = current + step_mask * branch
        hidden_in = low(layer_norm(middle, gain_two, shift_two))
        preactivation = low_back(jnp.einsum('jnd,dh->jnh', hidden_in, w_in, precision=HIGHEST) + bias_hidden)
        active = low(jax.nn.gelu(preactivation, approximate=False))
        result = low_back(jnp.einsum('jnh,hd->jnd', active, w_out, precision=HIGHEST) + bias_out)
        current = middle + step_mask * result
    return current

def reference(fields, noise_fields, step_counts, spectral_flat, mlp_flat, cotangent):
    noise_all = noise_fields.astype(jnp.float32)

    def forward(fields_in, spectral_in, mlp_in):
        spectral = spectral_in[:, :DEG_DEV * CIN * D].reshape(LDEG, CIN, D)
        vectors, w_in, w_out = unpack_mlp(mlp_in)
        params = (spectral, vectors, w_in, w_out)

        def one_date(inputs):
            return run_date(params, inputs)
        return lax.map(jax.checkpoint(one_date), (fields_in, noise_all, step_counts))
    outputs, pullback = jax.vjp(forward, fields.astype(jnp.float32), spectral_flat.astype(jnp.float32), mlp_flat.astype(jnp.float32))
    grad_fields, grad_spectral, grad_mlp = pullback(cotangent.astype(jnp.float32))
    return (outputs.astype(jnp.bfloat16), grad_fields.astype(jnp.bfloat16), grad_spectral, grad_mlp)
```

```python
from functools import partial
import math

import jax
import jax.numpy as jnp
import numpy as np
from jax import lax
from jax.experimental import pallas as pl
from jax.experimental.pallas import tpu as pltpu
from jax.sharding import PartitionSpec as P

D = 641
HID = 1282
NOISE = 8
NLAT = 48
NLON = 72
LDEG = 48
ORDERS = 36
STEPS = 2
CIN = D + NOISE

HIGHEST = lax.Precision.HIGHEST


def shortened(shard):
    return jax.tree.map(lambda a: a.astype(jnp.bfloat16) if a.dtype == jnp.float32 else a, shard)


def legendre_values(lat_total, degree_total, order_total):
    colatitude = np.pi * (np.arange(lat_total) + 0.5) / lat_total
    cosine = np.cos(colatitude)
    sine_part = np.sin(colatitude)
    legendre = np.zeros((lat_total, degree_total, order_total))
    diagonal = np.full(lat_total, 1.0 / math.sqrt(4.0 * math.pi))
    for column in range(order_total):
        if column > 0:
            diagonal = diagonal * math.sqrt((2.0 * column + 1.0) / (2.0 * column)) * sine_part
        legendre[:, column, column] = diagonal
        legendre[:, column + 1, column] = math.sqrt(2.0 * column + 3.0) * cosine * diagonal
        for degree in range(column + 2, degree_total):
            factor_one = math.sqrt(
                (4.0 * degree * degree - 1.0) / (degree * degree - column * column)
            )
            factor_two = math.sqrt(
                ((degree - 1.0) ** 2 - column * column) / (4.0 * (degree - 1.0) ** 2 - 1.0)
            )
            legendre[:, degree, column] = factor_one * (
                cosine * legendre[:, degree - 1, column]
                - factor_two * legendre[:, degree - 2, column]
            )
    return (colatitude, legendre)


def spectral_tables(lat_total, lon_total, degree_total, order_total):
    colatitude, legendre = legendre_values(lat_total, degree_total, order_total)
    quadrature = np.sin(colatitude) * np.pi / lat_total
    angles = 2.0 * np.pi * np.outer(np.arange(lon_total), np.arange(order_total)) / lon_total
    fourier = np.concatenate([np.cos(angles), -np.sin(angles)], axis=1) * (2.0 * np.pi / lon_total)
    weights = np.where(np.arange(order_total) == 0, 1.0, 2.0)
    inverse = np.concatenate(
        [np.cos(angles).T * weights[:, None], -np.sin(angles).T * weights[:, None]], axis=0
    )
    doubled = np.concatenate([legendre, legendre], axis=2)
    analysis = doubled * quadrature[:, None, None]
    return tuple(
        (np.asarray(member, np.float32) for member in (fourier, inverse, analysis, doubled))
    )


def normalize(values, scale_gain, shift_vec):
    centered = values - jnp.mean(values, axis=-1, keepdims=True)
    inverse_scale = lax.rsqrt(jnp.mean(centered * centered, axis=-1, keepdims=True) + 1e-06)
    unit = centered * inverse_scale
    return (unit * scale_gain + shift_vec, unit, inverse_scale)


def normalize_back(upstream, unit, inverse_scale, scale_gain):
    scaled = upstream * scale_gain
    mean_one = jnp.mean(scaled, axis=-1, keepdims=True)
    mean_two = jnp.mean(scaled * unit, axis=-1, keepdims=True)
    grad_input = inverse_scale * (scaled - mean_one - unit * mean_two)
    return (grad_input, jnp.sum(upstream * unit, axis=(0, 1, 2)), jnp.sum(upstream, axis=(0, 1, 2)))


def unpack_mlp(flat):
    pieces = []
    offset = 0
    for length in (D, D, D, D, HID, D):
        pieces.append(flat[offset : offset + length].astype(jnp.float32))
        offset = offset + length
    w_in = flat[offset : offset + D * HID].reshape(D, HID)
    offset = offset + D * HID
    w_out = flat[offset : offset + HID * D].reshape(HID, D)
    return (tuple(pieces), w_in, w_out)


def build_weights(spectral_whole, mlp_whole, degrees_here):
    count_all = degrees_here * (D + NOISE) * D
    spectral = spectral_whole[0, :count_all].reshape(degrees_here, D + NOISE, D)
    vectors, w_in, w_out = unpack_mlp(mlp_whole)
    return (spectral, vectors, w_in, w_out)


def forward_step(current, noise_step, step_mask, tables, weights):
    (
        fourier,
        inverse,
        analysis_here,
        synthesis_here,
        analysis_rows,
        synthesis_rows,
        analysis_degrees,
        synthesis_degrees,
    ) = tables
    spectral, vectors, w_in, w_out = weights
    gain_one, shift_one, gain_two, shift_two, bias_hidden, bias_out = vectors
    normed, unit_one, scale_one = normalize(current, gain_one, shift_one)
    joined = jnp.concatenate([normed, noise_step], axis=-1)
    grid_modes = jnp.einsum("bjnc,nk->bjkc", joined, fourier, precision=HIGHEST)
    by_order = lax.all_to_all(
        shortened(grid_modes), "lat", split_axis=2, concat_axis=1, tiled=True
    ).astype(grid_modes.dtype)
    coeffs = jnp.einsum("jlk,bjkc->blkc", analysis_here, by_order, precision=HIGHEST).astype(
        jnp.bfloat16
    )
    by_degree = lax.all_to_all(coeffs, "lat", split_axis=1, concat_axis=2, tiled=True)
    mixed_modes = jnp.einsum(
        "blkc,lcd->blkd", by_degree, spectral, preferred_element_type=jnp.float32
    ).astype(jnp.bfloat16)
    mixed_orders = lax.all_to_all(mixed_modes, "lat", split_axis=2, concat_axis=1, tiled=True)
    lat_modes = jnp.einsum(
        "jlk,blkd->bjkd", synthesis_here, mixed_orders.astype(jnp.float32), precision=HIGHEST
    )
    lat_rows = lax.all_to_all(
        shortened(lat_modes), "lat", split_axis=1, concat_axis=2, tiled=True
    ).astype(lat_modes.dtype)
    branch = jnp.einsum("bjkd,kn->bjnd", lat_rows, inverse, precision=HIGHEST)
    middle = current + step_mask * branch
    normed_two, unit_two, scale_two = normalize(middle, gain_two, shift_two)
    hidden_in = normed_two.astype(jnp.bfloat16)
    preactivation = (
        jnp.einsum("bjnd,dh->bjnh", hidden_in, w_in, preferred_element_type=jnp.float32)
        + bias_hidden
    )
    active = jax.nn.gelu(preactivation, approximate=False).astype(jnp.bfloat16)
    result = (
        jnp.einsum("bjnh,hd->bjnd", active, w_out, preferred_element_type=jnp.float32) + bias_out
    )
    kept_values = (
        unit_one,
        scale_one,
        by_degree,
        unit_two,
        scale_two,
        hidden_in,
        preactivation,
        active,
    )
    return (middle + step_mask * result, kept_values)


def backward_step(grad_state, step_mask, kept_values, tables, weights):
    (
        fourier,
        inverse,
        analysis_here,
        synthesis_here,
        analysis_rows,
        synthesis_rows,
        analysis_degrees,
        synthesis_degrees,
    ) = tables
    spectral, vectors, w_in, w_out = weights
    gain_one, shift_one, gain_two, shift_two, bias_hidden, bias_out = vectors
    unit_one, scale_one, by_degree, unit_two, scale_two, hidden_in, preactivation, active = (
        kept_values
    )
    grad_result = (step_mask * grad_state).astype(jnp.bfloat16)
    grad_bias_out = jnp.sum(grad_result.astype(jnp.float32), axis=(0, 1, 2))
    grad_w_out = jnp.einsum(
        "bjnh,bjnd->hd", active, grad_result, preferred_element_type=jnp.float32
    )
    grad_active = jnp.einsum(
        "bjnd,hd->bjnh", grad_result, w_out, preferred_element_type=jnp.float32
    )
    unused, gelu_back = jax.vjp(partial(jax.nn.gelu, approximate=False), preactivation)
    grad_preact = gelu_back(grad_active)[0].astype(jnp.bfloat16)
    grad_bias_hidden = jnp.sum(grad_preact.astype(jnp.float32), axis=(0, 1, 2))
    grad_w_in = jnp.einsum(
        "bjnd,bjnh->dh", hidden_in, grad_preact, preferred_element_type=jnp.float32
    )
    grad_hidden_in = jnp.einsum(
        "bjnh,dh->bjnd", grad_preact, w_in, preferred_element_type=jnp.float32
    )
    grad_norm_two, grad_gain_two, grad_shift_two = normalize_back(
        grad_hidden_in, unit_two, scale_two, gain_two
    )
    grad_middle = grad_state + grad_norm_two
    grad_branch = step_mask * grad_middle
    grad_rows = jnp.einsum("bjnd,kn->bjkd", grad_branch, inverse, precision=HIGHEST)
    grad_modes = lax.all_to_all(
        shortened(grad_rows), "lat", split_axis=2, concat_axis=1, tiled=True
    ).astype(grad_rows.dtype)
    grad_mixed = jnp.einsum("jlk,bjkd->blkd", synthesis_here, grad_modes, precision=HIGHEST).astype(
        jnp.bfloat16
    )
    grad_degree = lax.all_to_all(grad_mixed, "lat", split_axis=1, concat_axis=2, tiled=True)
    grad_spectral = jnp.einsum(
        "blkc,blkd->lcd", by_degree, grad_degree, preferred_element_type=jnp.float32
    )
    grad_coeffs = jnp.einsum(
        "blkd,lcd->blkc", grad_degree, spectral, preferred_element_type=jnp.float32
    ).astype(jnp.bfloat16)
    grad_coeff_orders = lax.all_to_all(grad_coeffs, "lat", split_axis=2, concat_axis=1, tiled=True)
    grad_grid = jnp.einsum(
        "jlk,blkc->bjkc", analysis_here, grad_coeff_orders.astype(jnp.float32), precision=HIGHEST
    )
    grad_lat = lax.all_to_all(
        shortened(grad_grid), "lat", split_axis=1, concat_axis=2, tiled=True
    ).astype(grad_grid.dtype)
    model_width = grad_state.shape[3]
    grad_normed = jnp.einsum(
        "bjkc,nk->bjnc", grad_lat[..., :model_width], fourier, precision=HIGHEST
    )
    grad_norm_one, grad_gain_one, grad_shift_one = normalize_back(
        grad_normed, unit_one, scale_one, gain_one
    )
    vectors_grad = (
        grad_gain_one,
        grad_shift_one,
        grad_gain_two,
        grad_shift_two,
        grad_bias_hidden,
        grad_bias_out,
    )
    return (grad_middle + grad_norm_one, (grad_spectral, vectors_grad, grad_w_in, grad_w_out))


def shards_general(fields, noise_fields, step_counts, spectral_flat, mlp_flat, cotangent):
    lat_count = lax.axis_size("lat")
    lat_index = lax.axis_index("lat")
    dates_here = fields.shape[0]
    rows_here = fields.shape[1]
    degrees_here = LDEG // lat_count
    orders_here = 2 * ORDERS // lat_count
    fourier, inverse, analysis, synthesis = [
        jnp.asarray(member) for member in spectral_tables(NLAT, NLON, LDEG, ORDERS)
    ]
    analysis_here = lax.dynamic_slice_in_dim(analysis, lat_index * orders_here, orders_here, 2)
    synthesis_here = lax.dynamic_slice_in_dim(synthesis, lat_index * orders_here, orders_here, 2)
    analysis_rows = lax.dynamic_slice_in_dim(analysis, lat_index * rows_here, rows_here, 0)
    synthesis_rows = lax.dynamic_slice_in_dim(synthesis, lat_index * rows_here, rows_here, 0)
    analysis_degrees = lax.dynamic_slice_in_dim(analysis, lat_index * degrees_here, degrees_here, 1)
    synthesis_degrees = lax.dynamic_slice_in_dim(
        synthesis, lat_index * degrees_here, degrees_here, 1
    )
    tables = (
        fourier,
        inverse,
        analysis_here,
        synthesis_here,
        analysis_rows,
        synthesis_rows,
        analysis_degrees,
        synthesis_degrees,
    )
    spectral_whole = lax.all_gather(spectral_flat, "dp", axis=1, tiled=True)
    mlp_whole = lax.all_gather(mlp_flat, ("dp", "lat"), axis=0, tiled=True)
    weights = build_weights(spectral_whole, mlp_whole, degrees_here)
    noise_steps = noise_fields.astype(jnp.float32).reshape(
        dates_here, STEPS, rows_here, NLON, NOISE
    )
    current = fields.astype(jnp.float32)
    kept_steps = []
    for step_index in range(STEPS):
        step_mask = (step_index < step_counts).astype(jnp.float32).reshape(dates_here, 1, 1, 1)
        current, kept_values = forward_step(
            current, noise_steps[:, step_index], step_mask, tables, weights
        )
        kept_steps.append((step_mask, kept_values))
    output_fields = current.astype(jnp.bfloat16)
    grad_state = cotangent.astype(jnp.float32)
    totals = None
    for step_index in reversed(range(STEPS)):
        step_mask, kept_values = kept_steps[step_index]
        grad_state, step_totals = backward_step(grad_state, step_mask, kept_values, tables, weights)
        totals = step_totals if totals is None else jax.tree.map(jnp.add, totals, step_totals)
    grad_spectral, grad_vectors, grad_w_in, grad_w_out = totals
    spectral_pad = jnp.zeros((spectral_whole.shape[1] - grad_spectral.size,), jnp.float32)
    spectral_pack = jnp.concatenate([grad_spectral.reshape(-1), spectral_pad]).reshape(1, -1)
    spectral_grad = lax.psum_scatter(
        spectral_pack.astype(jnp.bfloat16), "dp", scatter_dimension=1, tiled=True
    ).astype(jnp.float32)
    mlp_members = list(grad_vectors) + [grad_w_in.reshape(-1), grad_w_out.reshape(-1)]
    used_total = sum((member.size for member in mlp_members))
    mlp_pack = jnp.concatenate(
        mlp_members + [jnp.zeros((mlp_whole.shape[0] - used_total,), jnp.float32)]
    )
    mlp_grad = lax.psum_scatter(mlp_pack, ("dp", "lat"), scatter_dimension=0, tiled=True)
    return (output_fields, grad_state.astype(jnp.bfloat16), spectral_grad, mlp_grad)


ROWS = NLAT // 2
DEGS = LDEG // 2
CELLS = ROWS * NLON
DP = 768
HP = 1408
KP = 80
GROUPS = 5
GK = 16
WROWS = 672
BLK = 4
BC = BLK * NLON
WIN = 992
MAIN = 944
HEAD = 480
BF = jnp.bfloat16
F32 = jnp.float32
MB = 2**20


def params(limit=60, **more):
    return pltpu.CompilerParams(vmem_limit_bytes=limit * MB, **more)


def vspec():
    return pl.BlockSpec(memory_space=pltpu.VMEM)


def dot(a, b):
    return jnp.dot(a, b, preferred_element_type=F32)


def split_table(table):
    high = table.astype(BF).astype(np.float32)
    return np.concatenate([high, table - high, high], axis=1).astype(BF)


def split_dot(table, value):
    high = value.astype(BF).astype(F32)
    return dot(table, jnp.concatenate([high, high, value - high], axis=0).astype(BF))


def dot_nt(a, b):
    return lax.dot_general(a, b, (((1,), (1,)), ((), ())), preferred_element_type=F32)


def dot_tn(a, b):
    return lax.dot_general(a, b, (((0,), (0,)), ((), ())), preferred_element_type=F32)


def column_order():
    places = -np.ones(KP, np.int64)
    for group in range(GROUPS):
        for i in range(8):
            order = 8 * group + i
            if order < ORDERS:
                places[GK * group + i] = order
                places[GK * group + 8 + i] = ORDERS + order
    return places


def plan_tables():
    fourier, inverse, analysis, synthesis = spectral_tables(NLAT, NLON, LDEG, ORDERS)
    places = column_order()
    held = places >= 0
    take = np.where(held, places, 0)
    fourier = fourier[:, take] * held
    inverse = inverse[take, :] * held[:, None]
    analysis = analysis[:, :, take] * held
    synthesis = synthesis[:, :, take] * held
    eye = np.eye(GK, dtype=np.float32)

    def blocks(table):
        out = np.zeros((2, 2, GROUPS, 384, 384), np.float32)
        for own in range(2):
            for which in range(2):
                half = own if which == 0 else 1 - own
                for group in range(GROUPS):
                    part = table[24 * own : 24 * own + 24, 24 * half : 24 * half + 24]
                    part = part[:, :, GK * group : GK * group + GK]
                    full = np.einsum("pqi,ij->piqj", part, eye)
                    out[own, which, group] = full.reshape(384, 384)
        return out.astype(BF)

    by_degree = np.transpose
    return dict(
        fourier_t=split_table(fourier.T),
        fourier=split_table(fourier),
        inverse_t=split_table(inverse.T),
        inverse=split_table(inverse),
        analyse=blocks(by_degree(analysis, (1, 0, 2))),
        synthesize=blocks(synthesis),
        analyse_back=blocks(analysis),
        synthesize_back=blocks(by_degree(synthesis, (1, 0, 2))),
    )


def rows_out(flat_ref, start, offset, step, wide, tiles, tail, put, count, unroll=4):
    lane = lax.broadcasted_iota(jnp.int32, (8, 128), 1)

    def one(t, carry):
        shift = offset + step * t
        jump = shift // 128
        shift = shift - 128 * jump
        amount = (128 - shift) % 128
        low = lane + shift < 128
        pieces = [
            pltpu.roll(flat_ref[pl.ds(start + wide * t + jump + m, 8, stride=641), :], amount, 1)
            for m in range(tiles + 1)
        ]
        for m in range(tiles):
            piece = jnp.where(low, pieces[m], pieces[m + 1])
            if m == tiles - 1:
                piece = jnp.where(lane < tail, piece, 0.0)
            put(m, t, piece)
        return carry

    lax.fori_loop(0, count, one, 0, unroll=unroll)


def rows_in(flat_ref, start, offset, step, wide, tiles, get, count, unroll=2):
    lane = lax.broadcasted_iota(jnp.int32, (8, 128), 1)

    def one(t, carry):
        shift = offset + step * t
        jump = shift // 128
        shift = shift - 128 * jump
        high = lane >= shift
        pieces = [pltpu.roll(get(m, t), shift, 1) for m in range(tiles)]
        last = tiles + (1 if step > 1 else 0)
        for m in range(last):
            here = pieces[m] if m < tiles else jnp.zeros((8, 128), F32)
            before = pieces[m - 1] if m > 0 else jnp.zeros((8, 128), F32)
            piece = jnp.where(high, here, before)
            where = pl.ds(start + wide * t + jump + m, 8, stride=641)
            if m == 0 or m >= tiles - 1:
                flat_ref[where, :] = flat_ref[where, :] + piece
            else:
                flat_ref[where, :] = piece
        return carry

    lax.fori_loop(0, count, one, 0, unroll=unroll)


def shard_place(shard, length):
    first = (shard * length) // D
    base = (first // 16) * 16
    start = D * base - length * shard + 128 * 88
    return base, start // 128, start % 128


def window_kernel(length, shard_ref, flat_ref, main_ref, side_ref, flat, tiles, extra):
    chunks = length // 128
    base, start, offset = shard_place(shard_ref[0], length)
    flat[0:88, :] = jnp.zeros((88, 128), F32)
    flat[88 + chunks :, :] = jnp.zeros((flat.shape[0] - 88 - chunks, 128), F32)

    def load(i, carry):
        piece = flat_ref[:, pl.ds(pl.multiple_of(1024 * i, 1024), 1024)]
        flat[pl.ds(pl.multiple_of(88 + 8 * i, 8), 8), :] = piece.astype(F32).reshape(8, 128)
        return carry

    lax.fori_loop(0, chunks // 8, load, 0, unroll=7)
    rest = chunks % 8
    if rest:
        piece = flat_ref[:, 128 * (chunks - rest) :].astype(F32).reshape(rest, 128)
        flat[88 + chunks - rest : 88 + chunks, :] = piece
    lane = lax.broadcasted_iota(jnp.int32, (8, 128), 1)
    extra[...] = jnp.zeros_like(extra)

    def put(m, t, piece):
        if m < 5:
            tiles[m, pl.ds(t, 8, stride=128), :] = piece
        else:
            extra[...] = jnp.where(lane == t, piece[:, 0:1], extra[...])

    rows_out(flat, start, offset, 1, 5, 6, 1, put, 128)
    side_ref[48:64, :] = jnp.zeros((16, 640), BF)
    side_ref[48:64, 0:128] = jnp.concatenate([extra[...], jnp.zeros((8, 128), F32)], axis=0).astype(BF)
    for m in range(5):
        at = slice(128 * m, 128 * m + 128)
        main_ref[:, at] = tiles[m, 16 : 16 + MAIN, :].astype(BF)
        side_ref[0:16, at] = tiles[m, 0:16, :].astype(BF)
        side_ref[16:48, at] = tiles[m, 16 + MAIN : WIN, :].astype(BF)


def spectral_window(shard, flat):
    length = flat.shape[1]
    return pl.pallas_call(
        partial(window_kernel, length),
        out_shape=(jax.ShapeDtypeStruct((MAIN, 640), BF), jax.ShapeDtypeStruct((64, 640), BF)),
        in_specs=[pl.BlockSpec(memory_space=pltpu.SMEM), vspec()],
        out_specs=(vspec(), vspec()),
        scratch_shapes=[
            pltpu.VMEM((5256, 128), F32),
            pltpu.VMEM((5, 1024, 128), F32),
            pltpu.VMEM((8, 128), F32),
        ],
        compiler_params=params(),
    )(shard, flat)


VECTORS = ((0, D), (D, D), (2 * D, D), (3 * D, D), (4 * D, HID), (4 * D + HID, D))
IN_AT = 5 * D + HID
OUT_AT = IN_AT + D * HID


def mlp_kernel(flat_ref, in_ref, out_ref, vec_ref, flat, tin, tout):
    count = flat_ref.shape[0]
    flat[0:count, :] = flat_ref[...].astype(F32)
    lane = lax.broadcasted_iota(jnp.int32, (1, 128), 1)
    vec_ref[...] = jnp.zeros_like(vec_ref)
    for row, (place, length) in enumerate(VECTORS):
        first, shift = place // 128, place % 128
        for m in range(-(-length // 128)):
            one = flat[first + m : first + m + 1, :]
            two = flat[first + m + 1 : first + m + 2, :]
            if shift:
                one = pltpu.roll(one, 128 - shift, 1)
                two = pltpu.roll(two, 128 - shift, 1)
            piece = jnp.where(lane + shift < 128, one, two)
            piece = jnp.where(lane + 128 * m < length, piece, 0.0)
            vec_ref[row : row + 1, 128 * m : 128 * m + 128] = piece
    for part in range(2):

        def put_in(m, t, piece, part=part):
            tin[m, pl.ds(t + 512 * part, 8, stride=64), :] = piece

        rows_out(flat, IN_AT // 128 + 641 * 8 * part, IN_AT % 128, 2, 10, 11, 2, put_in, 64, 2)

        def put_out(m, t, piece, part=part):
            tout[m, pl.ds(t + 1024 * part, 8, stride=128), :] = piece

        rows_out(flat, OUT_AT // 128 + 641 * 8 * part, OUT_AT % 128, 1, 5, 6, 1, put_out, 128, 4)
    keep = lax.broadcasted_iota(jnp.int32, (DP, 128), 0) < D
    for m in range(11):
        in_ref[:, 128 * m : 128 * m + 128] = jnp.where(keep, tin[m, :DP, :], 0.0).astype(BF)
    keep = lax.broadcasted_iota(jnp.int32, (HP, 128), 0) < HID
    for m in range(6):
        out_ref[:, 128 * m : 128 * m + 128] = jnp.where(keep, tout[m, :HP, :], 0.0).astype(BF)


def mlp_weights(flat):
    return pl.pallas_call(
        mlp_kernel,
        out_shape=(
            jax.ShapeDtypeStruct((DP, HP), BF),
            jax.ShapeDtypeStruct((HP, DP), BF),
            jax.ShapeDtypeStruct((8, HP), F32),
        ),
        in_specs=[vspec()],
        out_specs=(vspec(), vspec(), vspec()),
        scratch_shapes=[
            pltpu.VMEM((16776, 128), F32),
            pltpu.VMEM((11, 1024, 128), F32),
            pltpu.VMEM((6, 2048, 128), F32),
        ],
        compiler_params=params(),
    )(flat)


ALL_ROWS = 15584
CHIPS = 8


def cuts(length, count):
    return [((s * length) // D) // 16 * 16 for s in range(count)] + [ALL_ROWS]


def gather_kernel(length, main_ref, side_ref, w_ref, column_ref, sides, edges, line, ring, over, arrive, local):
    dp = lax.axis_index("dp")
    lat = lax.axis_index("lat")
    core = dp % 2
    chip = dp // 2
    z = chip // 2
    x = chip % 2
    place = z + x * (7 - 2 * z)
    home = lat == core
    count = 2 * CHIPS

    def chip_at(p):
        p = (p + CHIPS) % CHIPS
        back = p // 4
        return ((1 - back) * p + back * (7 - p)) * 2 + back

    def device(p, which):
        return (chip_at(p) * 2 + which, lat)

    def shard(p, which):
        return chip_at(p) * 2 + which

    across = (dp, 1 - lat)
    partner = (dp + 1 - 2 * core, lat)
    barrier = pltpu.get_barrier_semaphore()
    for who in (device(place + 1, core), device(place - 1, core), across, partner):
        pl.semaphore_signal(barrier, inc=1, device_id=who, device_id_type=pl.DeviceIdType.MESH)
    pl.semaphore_wait(barrier, 4)

    def rows_of(s, first, size):
        start = ((s * length) // D) // 16 * 16 + 16 + first
        return w_ref.at[pl.ds(pl.multiple_of(start, 16), size)]

    def remote(src, dst, send, recv, who):
        return pltpu.make_async_remote_copy(
            src_ref=src, dst_ref=dst, send_sem=send, recv_sem=recv, device_id=who,
            device_id_type=pl.DeviceIdType.MESH,
        )

    first = core
    second = 1 - core
    hops = {1: [(0, 0), (0, 1), (1, 0), (1, 1), (2, 0), (2, 1), (3, 0)],
            -1: [(0, 0), (0, 1), (1, 0), (1, 1), (2, 0), (2, 1), (3, 1)]}
    coming = [(way, d, w) for d in (1, 2, 3) for w in (0, 1) for way in (1, -1)] + [(1, 4, 0), (-1, 4, 1)]

    def named(way, d, w):
        which = first if w == 0 else second
        return shard(place - way * d, which)

    def wait_part(kind, s, size):
        remote(rows_of(s, 0, size), rows_of(s, 0, size), local.at[0], arrive.at[kind, s], across).wait_recv()

    def wait_side(s):
        remote(sides.at[s], sides.at[s], local.at[0], arrive.at[2, s], across).wait_recv()

    own = dp

    @pl.when(home)
    def _():
        keep = pltpu.make_async_copy(main_ref, rows_of(own, 0, MAIN), local.at[0])
        keep.start()
        keep_side = pltpu.make_async_copy(side_ref, sides.at[own], local.at[1])
        keep_side.start()
        sent = []

        def send(way, hop, s, main, side):
            to = device(place + way, core)
            lane = 0 if way == 1 else 1
            copies = (
                remote(main, rows_of(s, 0, MAIN), ring.at[lane, hop], arrive.at[0, s], to),
                remote(side, sides.at[s], ring.at[lane + 2, hop], arrive.at[2, s], to),
            )
            for copy in copies:
                copy.start()
                sent.append(copy)

        def cross(index, s, main, side):
            copies = [remote(main(0, HEAD), rows_of(s, 0, HEAD), over.at[0, index], arrive.at[1, s], across)]
            copies.append(remote(side, sides.at[s], over.at[1, index], arrive.at[2, s], across))
            if index < 2:
                copies.insert(
                    0,
                    remote(
                        main(HEAD, MAIN - HEAD), rows_of(s, HEAD, MAIN - HEAD), over.at[2, index],
                        arrive.at[0, s], across,
                    ),
                )
            for copy in copies:
                copy.start()
                sent.append(copy)

        send(1, 0, own, main_ref, side_ref)
        send(-1, 0, own, main_ref, side_ref)
        cross(0, own, lambda at, size: main_ref.at[pl.ds(at, size)], side_ref)
        mate = dp + 1 - 2 * core
        wait_part(0, mate, MAIN)
        wait_side(mate)
        held = lambda s: (lambda at, size: rows_of(s, at, size))
        send(1, 1, mate, rows_of(mate, 0, MAIN), sides.at[mate])
        send(-1, 1, mate, rows_of(mate, 0, MAIN), sides.at[mate])
        cross(1, mate, held(mate), sides.at[mate])
        for index, (way, d, w) in enumerate(coming):
            s = named(way, d, w)
            wait_part(0, s, MAIN)
            wait_side(s)
            if (d, w) in hops[way]:
                send(way, hops[way].index((d, w)), s, rows_of(s, 0, MAIN), sides.at[s])
            cross(2 + index, s, held(s), sides.at[s])
        for copy in sent:
            copy.wait_send()
        keep.wait()
        keep_side.wait()

    @pl.when(jnp.logical_not(home))
    def _():
        sent = [
            remote(main_ref, rows_of(own, 0, MAIN), ring.at[4, 0], arrive.at[0, own], partner),
            remote(side_ref, sides.at[own], ring.at[4, 1], arrive.at[2, own], partner),
        ]
        for copy in sent:
            copy.start()
        size = MAIN - HEAD

        def send(way, hop, s):
            lane = 0 if way == 1 else 1
            copy = remote(
                rows_of(s, HEAD, size), rows_of(s, HEAD, size), ring.at[lane, hop], arrive.at[0, s],
                device(place + way, core),
            )
            copy.start()
            sent.append(copy)

        mate = dp + 1 - 2 * core
        wait_part(0, own, size)
        send(1, 0, own)
        send(-1, 0, own)
        wait_part(0, mate, size)
        send(1, 1, mate)
        send(-1, 1, mate)
        for way, d, w in coming:
            s = named(way, d, w)
            wait_part(0, s, size)
            if (d, w) in hops[way]:
                send(way, hops[way].index((d, w)), s)
        for s in [own, mate] + [named(*one) for one in coming]:
            wait_part(1, s, HEAD)
            wait_side(s)
        for copy in sent:
            copy.wait_send()

    places = cuts(length, count)
    copies = []
    for s in range(count):
        span = places[s + 1] - places[s]
        edge = sides[s, 0:16, :]
        if s:
            before = places[s] - places[s - 1] - 16 - MAIN
            edge = edge + sides[s - 1, 16 + before : 32 + before, :]
        edges[s] = edge
        copies.append(pltpu.make_async_copy(edges.at[s], w_ref.at[pl.ds(places[s], 16)], local.at[2 + s]))
        left = span - 16 - MAIN
        if left:
            copies.append(
                pltpu.make_async_copy(
                    sides.at[s, pl.ds(16, left)], w_ref.at[pl.ds(places[s] + 16 + MAIN, left)],
                    local.at[2 + count + s],
                )
            )
    for copy in copies:
        copy.start()
    lane = lax.broadcasted_iota(jnp.int32, (8, 128), 1)
    line[...] = jnp.zeros_like(line)
    for s in range(count):
        a, b = places[s] // 128, places[s] % 128
        piece = sides[s, 48:64, 0:128].astype(F32)[:8]
        if b:
            piece = pltpu.roll(piece, b, 1)
        line[a : a + 8, :] += jnp.where(lane >= b, piece, 0.0)
        line[a + 1 : a + 9, :] += jnp.where(lane < b, piece, 0.0)
    lane = lax.broadcasted_iota(jnp.int32, (1, 128), 1)
    for degree in range(DEGS):
        a, b = CIN * degree // 128, CIN * degree % 128
        piece = line[a : a + 8, :]
        if b:
            piece = pltpu.roll(piece, 128 - b, 1)
        for m in range(6):
            one = jnp.where(lane + b < 128, piece[m : m + 1], piece[m + 1 : m + 2])
            one = jnp.where(lane + 128 * m < CIN, one, 0.0)
            column_ref[degree : degree + 1, 128 * m : 128 * m + 128] = one
    for copy in copies:
        copy.wait()


def gather_rows(length, main, side):
    count = 2 * CHIPS
    return pl.pallas_call(
        partial(gather_kernel, length),
        out_shape=(jax.ShapeDtypeStruct((ALL_ROWS, 640), BF), jax.ShapeDtypeStruct((DEGS, DP), F32)),
        in_specs=[vspec(), vspec()],
        out_specs=(pl.BlockSpec(memory_space=pl.ANY), vspec()),
        scratch_shapes=[
            pltpu.VMEM((count, 64, 640), BF),
            pltpu.VMEM((count, 16, 640), BF),
            pltpu.VMEM((136, 128), F32),
            pltpu.SemaphoreType.DMA((5, 7)),
            pltpu.SemaphoreType.DMA((3, count)),
            pltpu.SemaphoreType.DMA((3, count)),
            pltpu.SemaphoreType.DMA((2 + 2 * count,)),
        ],
        compiler_params=params(30, collective_id=0, has_side_effects=True),
    )(main, side)


def lane_mask():
    return (lax.broadcasted_iota(jnp.int32, (1, DP), 1) < D).astype(F32)


def unit_of(values, mask):
    mean = jnp.sum(values, axis=-1, keepdims=True) * (1.0 / D)
    centred = (values - mean) * mask
    square = jnp.sum(centred * centred, axis=-1, keepdims=True) * (1.0 / D)
    scale = lax.rsqrt(square + 1e-06)
    return centred * scale, scale


def norm_back(upstream, unit, scale, gain):
    scaled = upstream * gain
    mean_one = jnp.sum(scaled, axis=-1, keepdims=True) * (1.0 / D)
    mean_two = jnp.sum(scaled * unit, axis=-1, keepdims=True) * (1.0 / D)
    return scale * (scaled - mean_one * lane_mask() - unit * mean_two)


def modes_kernel(state_ref, noise_ref, vec_ref, table_ref, out_ref):
    unit, scale = unit_of(state_ref[...].astype(F32), lane_mask())
    normed = unit * vec_ref[0:1, :DP] + vec_ref[1:2, :DP]
    joined = jnp.concatenate(
        [normed[:, :640], normed[:, 640:] + noise_ref[...].astype(F32)], axis=1
    )
    for j in range(BLK):
        piece = joined[NLON * j : NLON * j + NLON, :]
        out_ref[j] = split_dot(table_ref[...], piece).astype(BF)


def modes(state, noise, vectors, table):
    return pl.pallas_call(
        modes_kernel,
        grid=(ROWS // BLK,),
        out_shape=jax.ShapeDtypeStruct((ROWS, KP, DP), BF),
        in_specs=[
            pl.BlockSpec((BC, DP), lambda i: (i, 0)),
            pl.BlockSpec((BC, 128), lambda i: (i, 0)),
            pl.BlockSpec((8, HP), lambda i: (0, 0)),
            pl.BlockSpec((KP, 3 * NLON), lambda i: (0, 0)),
        ],
        out_specs=pl.BlockSpec((BLK, KP, DP), lambda i: (i, 0, 0)),
        compiler_params=params(),
    )(state, noise, vectors, table)


def legendre(table_ref, own_ref, other_ref, out_ref):
    for group in range(GROUPS):
        at = slice(GK * group, GK * group + GK)
        total = dot(table_ref[0, 0, group], own_ref[:, at, :].reshape(384, DP))
        total = total + dot(table_ref[0, 1, group], other_ref[:, at, :].reshape(384, DP))
        out_ref[:, at, :] = total.astype(out_ref.dtype).reshape(24, GK, DP)


def fetch(w_ref, w_buf, sem, degree, slot):
    first = pl.multiple_of((CIN * degree) // 16 * 16, 16)
    return pltpu.make_async_copy(w_ref.at[pl.ds(first, WROWS)], w_buf.at[slot], sem.at[slot])


def mix_kernel(half_ref, own_ref, other_ref, table_ref, column_ref, w_ref, coeff_ref, mixed_ref, w_buf, sem):
    fetch(w_ref, w_buf, sem, 0, 0).start()
    legendre(table_ref, own_ref, other_ref, coeff_ref)
    lane = lax.broadcasted_iota(jnp.int32, (KP, 128), 1)

    def one(degree, carry):
        slot = degree % 2

        @pl.when(degree + 1 < DEGS)
        def _():
            fetch(w_ref, w_buf, sem, degree + 1, 1 - slot).start()

        fetch(w_ref, w_buf, sem, degree, slot).wait()
        coeffs = coeff_ref[degree].astype(F32)
        moved = pltpu.roll(coeffs, (CIN * degree) % 16, 1)
        mixed = dot(moved[:, :WROWS].astype(BF), w_buf[slot])
        mixed_ref[degree, :, :640] = mixed.astype(BF)
        last = jnp.sum(coeffs * column_ref[pl.ds(degree, 1), :], axis=1, keepdims=True)
        mixed_ref[degree, :, 640:] = jnp.where(lane < 1, last, 0.0).astype(BF)
        return carry

    lax.fori_loop(0, DEGS, one, 0)


def mix_back_kernel(half_ref, own_ref, other_ref, table_ref, column_ref, w_ref, grad_ref, out_ref, w_buf, wide, sem):
    fetch(w_ref, w_buf, sem, 0, 0).start()
    legendre(table_ref, own_ref, other_ref, grad_ref)
    keep = lax.broadcasted_iota(jnp.int32, (KP, DP), 1) < CIN
    wide[...] = jnp.zeros_like(wide)

    def one(degree, carry):
        slot = degree % 2

        @pl.when(degree + 1 < DEGS)
        def _():
            fetch(w_ref, w_buf, sem, degree + 1, 1 - slot).start()

        fetch(w_ref, w_buf, sem, degree, slot).wait()
        wide[:, :WROWS] = dot_nt(grad_ref[degree, :, :640], w_buf[slot])
        back = pltpu.roll(wide[...], DP - (CIN * degree) % 16, 1)
        last = grad_ref[degree, :, 640:].astype(F32)[:, 0:1]
        back = back + last * column_ref[pl.ds(degree, 1), :]
        out_ref[degree] = jnp.where(keep, back, 0.0).astype(BF)
        return carry

    lax.fori_loop(0, DEGS, one, 0)


def mix(half, own, other, table, weights, column, back):
    whole = pl.BlockSpec((24, KP, DP), lambda i, h: (0, 0, 0))
    scratch = [pltpu.VMEM((2, WROWS, 640), BF)]
    if back:
        scratch.append(pltpu.VMEM((KP, DP), F32))
    scratch.append(pltpu.SemaphoreType.DMA((2,)))
    return pl.pallas_call(
        mix_back_kernel if back else mix_kernel,
        grid_spec=pltpu.PrefetchScalarGridSpec(
            num_scalar_prefetch=1,
            grid=(1,),
            in_specs=[
                whole,
                whole,
                pl.BlockSpec((1, 2, GROUPS, 384, 384), lambda i, h: (h[0], 0, 0, 0, 0)),
                pl.BlockSpec((DEGS, DP), lambda i, h: (0, 0)),
                pl.BlockSpec(memory_space=pl.ANY),
            ],
            out_specs=(whole, whole),
            scratch_shapes=scratch,
        ),
        out_shape=(jax.ShapeDtypeStruct((24, KP, DP), BF),) * 2,
        compiler_params=params(),
    )(half, own, other, table, column, weights)


HID_PARTS = ((0, 256), (256, 256), (512, 256), (768, 256), (1024, 256), (1280, 128))


def feed_kernel(
    half_ref, mask_ref, own_ref, other_ref, table_ref, inverse_ref, state_ref, vec_ref, in_ref, out_ref,
    next_ref, middle_ref, hidden_ref, active_ref, slope_ref, lat,
):
    i = pl.program_id(0)

    @pl.when(i == 0)
    def _():
        legendre(table_ref, own_ref, other_ref, lat)

    mask = mask_ref[0]
    parts = [split_dot(inverse_ref[...], lat[BLK * i + j]) for j in range(BLK)]
    middle = state_ref[...].astype(F32) + mask * jnp.concatenate(parts, axis=0)
    middle_ref[...] = middle
    unit, scale = unit_of(middle, lane_mask())
    hidden = (unit * vec_ref[2:3, :DP] + vec_ref[3:4, :DP]).astype(BF)
    hidden_ref[...] = hidden
    for first, width in HID_PARTS:
        at = slice(first, first + width)
        pre = dot(hidden, in_ref[:, at]) + vec_ref[4:5, at]
        bell = 0.5 * (1.0 + lax.erf(pre * (1.0 / math.sqrt(2.0))))
        active_ref[:, at] = (pre * bell).astype(BF)
        slope = bell + pre * (jnp.exp(-0.5 * pre * pre) * (1.0 / math.sqrt(2.0 * math.pi)))
        slope_ref[:, at] = slope.astype(BF)
    result = dot(active_ref[...], out_ref[...]) + vec_ref[5:6, :DP]
    next_ref[...] = (middle + mask * result).astype(next_ref.dtype)


def cell_spec(width):
    return pl.BlockSpec((BC, width), lambda i, *h: (i, 0))


def fixed(*shape):
    return pl.BlockSpec(shape, lambda i, *h: (0,) * len(shape))


def table_spec():
    return pl.BlockSpec((1, 2, GROUPS, 384, 384), lambda i, h, *m: (h[0], 0, 0, 0, 0))


def feed(half, mask, own, other, table, inverse_t, state, vectors, w_in, w_out, last):
    cells = lambda width, kind: jax.ShapeDtypeStruct((CELLS, width), kind)
    return pl.pallas_call(
        feed_kernel,
        grid_spec=pltpu.PrefetchScalarGridSpec(
            num_scalar_prefetch=2,
            grid=(ROWS // BLK,),
            in_specs=[
                fixed(24, KP, DP), fixed(24, KP, DP), table_spec(), fixed(NLON, 3 * KP), cell_spec(DP),
                fixed(8, HP), fixed(DP, HP), fixed(HP, DP),
            ],
            out_specs=(cell_spec(DP), cell_spec(DP), cell_spec(DP), cell_spec(HP), cell_spec(HP)),
            scratch_shapes=[pltpu.VMEM((24, KP, DP), F32)],
        ),
        out_shape=(
            cells(DP, BF if last else F32), cells(DP, F32), cells(DP, BF), cells(HP, BF), cells(HP, BF),
        ),
        compiler_params=params(),
    )(half, mask, own, other, table, inverse_t, state, vectors, w_in, w_out)


def feed_back_kernel(
    mask_ref, grad_ref, slope_ref, middle_ref, vec_ref, in_ref, out_ref, inverse_ref,
    result_ref, pre_ref, gm_ref, modes_ref, sums_ref,
):
    i = pl.program_id(0)

    @pl.when(i == 0)
    def _():
        sums_ref[...] = jnp.zeros_like(sums_ref)

    mask = mask_ref[0]
    grad = grad_ref[...].astype(F32)
    result = (mask * grad).astype(BF)
    result_ref[...] = result
    sums_ref[5:6, :DP] += jnp.sum(result.astype(F32), axis=0, keepdims=True)
    for first, width in HID_PARTS:
        at = slice(first, first + width)
        active = dot_nt(result, out_ref[at, :])
        pre = (active * slope_ref[:, at].astype(F32)).astype(BF)
        pre_ref[:, at] = pre
        sums_ref[4:5, at] += jnp.sum(pre.astype(F32), axis=0, keepdims=True)
    upstream = dot_nt(pre_ref[...], in_ref[...])
    unit, scale = unit_of(middle_ref[...], lane_mask())
    sums_ref[2:3, :DP] += jnp.sum(upstream * unit, axis=0, keepdims=True)
    sums_ref[3:4, :DP] += jnp.sum(upstream, axis=0, keepdims=True)
    total = grad + norm_back(upstream, unit, scale, vec_ref[2:3, :DP])
    gm_ref[...] = total
    total = mask * total
    for j in range(BLK):
        piece = total[NLON * j : NLON * j + NLON, :]
        modes_ref[j] = split_dot(inverse_ref[...], piece).astype(BF)


def feed_back(mask, grad, slope, middle, vectors, w_in, w_out, inverse):
    cells = lambda width, kind: jax.ShapeDtypeStruct((CELLS, width), kind)
    return pl.pallas_call(
        feed_back_kernel,
        grid_spec=pltpu.PrefetchScalarGridSpec(
            num_scalar_prefetch=1,
            grid=(ROWS // BLK,),
            in_specs=[
                cell_spec(DP), cell_spec(HP), cell_spec(DP), fixed(8, HP), fixed(DP, HP), fixed(HP, DP),
                fixed(KP, 3 * NLON),
            ],
            out_specs=(
                cell_spec(DP), cell_spec(HP), cell_spec(DP),
                pl.BlockSpec((BLK, KP, DP), lambda i, *h: (i, 0, 0)), fixed(8, HP),
            ),
        ),
        out_shape=(
            cells(DP, BF), cells(HP, BF), cells(DP, F32), jax.ShapeDtypeStruct((ROWS, KP, DP), BF),
            jax.ShapeDtypeStruct((8, HP), F32),
        ),
        compiler_params=params(),
    )(mask, grad, slope, middle, vectors, w_in, w_out, inverse)


def first_back_kernel(
    half_ref, own_ref, other_ref, table_ref, fourier_ref, state_ref, gm_ref, vec_ref, out_ref, sums_ref, lat,
):
    i = pl.program_id(0)

    @pl.when(i == 0)
    def _():
        legendre(table_ref, own_ref, other_ref, lat)
        sums_ref[...] = jnp.zeros_like(sums_ref)

    parts = [split_dot(fourier_ref[...], lat[BLK * i + j]) for j in range(BLK)]
    upstream = jnp.concatenate(parts, axis=0)
    unit, scale = unit_of(state_ref[...].astype(F32), lane_mask())
    sums_ref[0:1, :] += jnp.sum(upstream * unit, axis=0, keepdims=True)
    sums_ref[1:2, :] += jnp.sum(upstream, axis=0, keepdims=True)
    total = gm_ref[...] + norm_back(upstream, unit, scale, vec_ref[0:1, :DP])
    out_ref[...] = total.astype(out_ref.dtype)


def first_back(half, own, other, table, fourier, state, gm, vectors, last):
    return pl.pallas_call(
        first_back_kernel,
        grid_spec=pltpu.PrefetchScalarGridSpec(
            num_scalar_prefetch=1,
            grid=(ROWS // BLK,),
            in_specs=[
                fixed(24, KP, DP), fixed(24, KP, DP), table_spec(), fixed(NLON, 3 * KP), cell_spec(DP),
                cell_spec(DP), fixed(8, HP),
            ],
            out_specs=(cell_spec(DP), fixed(8, DP)),
            scratch_shapes=[pltpu.VMEM((24, KP, DP), F32)],
        ),
        out_shape=(
            jax.ShapeDtypeStruct((CELLS, DP), BF if last else F32), jax.ShapeDtypeStruct((8, DP), F32),
        ),
        compiler_params=params(),
    )(half, own, other, table, fourier, state, gm, vectors)


def mlp_grad_kernel(h0, h1, p0, p1, a0, a1, r0, r1, tin, tout, turned):
    for step, ref in enumerate((h0, h1)):
        turned[:, CELLS * step : CELLS * step + CELLS] = ref[...].T
    for first, width in HID_PARTS:
        at = slice(first, first + width)
        part = dot(turned[:, :CELLS], p0[:, at]) + dot(turned[:, CELLS:], p1[:, at])
        for m in range(width // 128):
            tin[first // 128 + m] = part[:, 128 * m : 128 * m + 128]
        part = dot_tn(a0[:, at], r0[...]) + dot_tn(a1[:, at], r1[...])
        for m in range(6):
            tout[m, at, :] = part[:, 128 * m : 128 * m + 128]


def mlp_flat_kernel(gin, gout, feed_sums, first_sums, flat_ref, tin, tout):
    tin[:, :DP, :] = gin[...]
    tout[:, :HP, :] = gout[...]
    tin[:, DP:, :] = jnp.zeros((11, 1024 - DP, 128), F32)
    tout[:, HP:, :] = jnp.zeros((6, 2048 - HP, 128), F32)
    flat_ref[...] = jnp.zeros_like(flat_ref)
    lane = lax.broadcasted_iota(jnp.int32, (1, 128), 1)
    sums = feed_sums[...]
    for row, (place, length) in enumerate(VECTORS):
        first, shift = place // 128, place % 128
        for m in range(-(-length // 128)):
            at = slice(128 * m, 128 * m + 128)
            piece = first_sums[row : row + 1, at] if row < 2 else sums[row : row + 1, at]
            piece = jnp.where(lane + 128 * m < length, piece, 0.0)
            if shift:
                piece = pltpu.roll(piece, shift, 1)
            flat_ref[first + m : first + m + 1, :] += jnp.where(lane >= shift, piece, 0.0)
            flat_ref[first + m + 1 : first + m + 2, :] += jnp.where(lane < shift, piece, 0.0)
    for part in range(2):

        def get_in(m, t, part=part):
            return tin[m, pl.ds(t + 512 * part, 8, stride=64), :]

        rows_in(flat_ref, IN_AT // 128 + 641 * 8 * part, IN_AT % 128, 2, 10, 11, get_in, 64, 1)

    for part in range(2):

        def get_out(m, t, part=part):
            return tout[m, pl.ds(t + 1024 * part, 8, stride=128), :]

        rows_in(flat_ref, OUT_AT // 128 + 641 * 8 * part, OUT_AT % 128, 1, 5, 6, get_out, 128, 2)


FLAT_ROWS = 16784


def mlp_grads(hidden, pre, active, result, feed_sums, first_sums):
    gin, gout = pl.pallas_call(
        mlp_grad_kernel,
        out_shape=(jax.ShapeDtypeStruct((11, DP, 128), F32), jax.ShapeDtypeStruct((6, HP, 128), F32)),
        in_specs=[vspec()] * 8,
        out_specs=(vspec(), vspec()),
        scratch_shapes=[pltpu.VMEM((DP, 2 * CELLS), BF)],
        compiler_params=params(62),
    )(*hidden, *pre, *active, *result)
    return pl.pallas_call(
        mlp_flat_kernel,
        out_shape=jax.ShapeDtypeStruct((FLAT_ROWS, 128), F32),
        in_specs=[vspec()] * 4,
        out_specs=vspec(),
        scratch_shapes=[pltpu.VMEM((11, 1024, 128), F32), pltpu.VMEM((6, 2048, 128), F32)],
        compiler_params=params(62),
    )(gin, gout, feed_sums, first_sums)


def spectral_grad_kernel(c0, c1, g0, g1, tiles_ref, head_ref):
    rows = 16 * KP
    tiles_ref[:, 0:16, :] = jnp.zeros((6, 16, 128), F32)
    for e in range(2):
        total = dot_tn(c0[:, e].reshape(rows, DP), g0[:, e].reshape(rows, DP))
        total = total + dot_tn(c1[:, e].reshape(rows, DP), g1[:, e].reshape(rows, DP))
        if e == 0:
            head_ref[...] = total[0:8, :]
        for m in range(6):
            tiles_ref[m, 16 + CIN * e : 16 + CIN * e + CIN, :] = total[:CIN, 128 * m : 128 * m + 128]
    tiles_ref[:, 16 + 2 * CIN :, :] = jnp.zeros((6, 1384 - 16 - 2 * CIN, 128), F32)


def spectral_grads(coeffs, grads):
    return pl.pallas_call(
        spectral_grad_kernel,
        out_shape=(jax.ShapeDtypeStruct((6, 1384, 128), F32), jax.ShapeDtypeStruct((8, DP), F32)),
        in_specs=[vspec()] * 4,
        out_specs=(vspec(), vspec()),
        compiler_params=params(),
    )(*coeffs, *grads)


def flatten_kernel(length, shard_ref, tiles_ref, next_ref, out_ref, tiles, flat):
    chunks = length // 128
    shard = shard_ref[0]
    base, start, offset = shard_place(shard, length)
    move = base - CIN * ((3 * shard) // 2) + 16
    tiles[...] = tiles_ref[...]
    for m in range(6):
        tiles[m, 16 + 2 * CIN : 24 + 2 * CIN, :] = next_ref[:, 128 * m : 128 * m + 128]
    flat[...] = jnp.zeros_like(flat)

    def get(m, t):
        return tiles[m, pl.ds(t + move, 8, stride=128), :]

    rows_in(flat, start, offset, 1, 5, 6, get, 128)

    def save(i, carry):
        piece = flat[pl.ds(pl.multiple_of(88 + 8 * i, 8), 8), :].reshape(1, 1024)
        out_ref[:, pl.ds(pl.multiple_of(1024 * i, 1024), 1024)] = piece
        return carry

    lax.fori_loop(0, chunks // 8, save, 0, unroll=7)
    rest = chunks % 8
    if rest:
        piece = flat[88 + chunks - rest : 88 + chunks, :].reshape(1, 128 * rest)
        out_ref[:, 128 * (chunks - rest) :] = piece


def flatten(shard, tiles, after, length):
    return pl.pallas_call(
        partial(flatten_kernel, length),
        out_shape=jax.ShapeDtypeStruct((1, length), F32),
        in_specs=[pl.BlockSpec(memory_space=pltpu.SMEM), vspec(), vspec()],
        out_specs=vspec(),
        scratch_shapes=[pltpu.VMEM((6, 1384, 128), F32), pltpu.VMEM((5256, 128), F32)],
        compiler_params=params(),
    )(shard, tiles, after)


def wide(block):
    flat = block.reshape(CELLS, D)
    return jnp.pad(flat, ((0, 0), (0, DP - D)))


def shards_paired(fields, noise_fields, step_counts, spectral_flat, mlp_flat, cotangent):
    axes = ("dp", "lat")
    dp_count = lax.axis_size("dp")
    dp_index = lax.axis_index("dp")
    core = dp_index % 2
    lat_index = lax.axis_index("lat")
    length = spectral_flat.shape[1]
    places = [(d, y) for d in range(dp_count) for y in range(2)]
    number = lambda d, y: 2 * d + y
    mirror = [(number(d, y), number(d - d % 2 + y, d % 2)) for d, y in places]
    other_core = [(number(d, y), number(d + 1 - 2 * (d % 2), y)) for d, y in places]
    same_core = [[number(d, y) for d, y in places if d % 2 == c] for c in range(2)]
    mirrored = lambda a: lax.ppermute(a, axes, mirror)
    swapped = lambda a: lax.ppermute(a, axes, other_core)
    half = core.astype(jnp.int32).reshape(1)
    tables = {name: jnp.asarray(value) for name, value in plan_tables().items()}

    main, side = spectral_window(dp_index.astype(jnp.int32).reshape(1), spectral_flat)
    weights, column = gather_rows(length, main, side)
    mlp_whole = lax.all_gather(mlp_flat, axes, axis=0, tiled=True)
    state = mirrored(wide(fields))
    noise = jnp.pad(
        noise_fields.reshape(STEPS, CELLS, NOISE), ((0, 0), (0, 0), (1, 128 - 1 - NOISE))
    )
    noise = mirrored(noise)
    counts = mirrored(step_counts)
    grad = mirrored(wide(cotangent))
    w_in, w_out, vectors = mlp_weights(mlp_whole.reshape(-1, 128))

    kept = []
    for step in range(STEPS):
        mask = (step < counts).astype(F32)
        lon_modes = modes(state, noise[step], vectors, tables["fourier_t"])
        coeffs, mixed = mix(half, lon_modes, swapped(lon_modes), tables["analyse"], weights, column, False)
        following, middle, hidden, active, slope = feed(
            half, mask, mixed, swapped(mixed), tables["synthesize"], tables["inverse_t"], state, vectors,
            w_in, w_out, step == STEPS - 1,
        )
        kept.append((mask, state, coeffs, middle, hidden, active, slope))
        state = following
    output = mirrored(state)

    owners = dp_count
    pairs = np.array([[(3 * s) // 2, (3 * s) // 2 + 1] for s in range(owners)])

    def to_owners(block):
        parts = jnp.concatenate([block[a : b + 1] for a, b in pairs], axis=0)
        parts = parts.reshape(owners, 2, KP, DP)
        return lax.all_to_all(
            parts, axes, split_axis=0, concat_axis=0, tiled=True, axis_index_groups=same_core
        )

    coeff_parts = [to_owners(kept[step][2]) for step in range(STEPS)]
    grad_parts = [None] * STEPS
    results = [None] * STEPS
    pres = [None] * STEPS
    feed_sums = first_sums = 0.0
    for step in reversed(range(STEPS)):
        mask, state, coeffs, middle, hidden, active, slope = kept[step]
        results[step], pres[step], gm, grad_modes, sums = feed_back(
            mask, grad, slope, middle, vectors, w_in, w_out, tables["inverse"]
        )
        feed_sums = feed_sums + sums
        grad_mixed, grad_coeffs = mix(
            half, grad_modes, swapped(grad_modes), tables["synthesize_back"], weights, column, True
        )
        grad_parts[step] = to_owners(grad_mixed)
        grad, sums = first_back(
            half, grad_coeffs, swapped(grad_coeffs), tables["analyse_back"], tables["fourier"], state, gm,
            vectors, step == 0,
        )
        first_sums = first_sums + sums
    fields_grad = mirrored(grad)
    mlp_pack = mlp_grads(
        [k[4] for k in kept], pres, [k[5] for k in kept], results, feed_sums, first_sums
    )
    mlp_pack = mlp_pack[: mlp_whole.shape[0] // 128].reshape(-1)
    mlp_grad = lax.psum_scatter(mlp_pack, axes, scatter_dimension=0, tiled=True)

    owner = (dp_index - core + lat_index).astype(jnp.int32).reshape(1)
    tiles, head = spectral_grads(coeff_parts, grad_parts)
    spot = lambda s, c: number(s - s % 2 + c, s % 2)
    earlier = [(spot(s, c), spot(s - 1, c)) for s in range(1, owners) for c in range(2)]
    after = lax.ppermute(head, axes, earlier)
    spectral_grad = mirrored(flatten(owner, tiles, after, length))
    narrow = lambda a: a[:, :D].reshape(1, ROWS, NLON, D)
    return narrow(output), narrow(fields_grad), spectral_grad, mlp_grad


def solution(mesh):
    paired = mesh.shape["lat"] == 2 and mesh.shape["dp"] == 16
    return jax.shard_map(
        shards_paired if paired else shards_general,
        mesh=mesh,
        in_specs=(
            P("dp", "lat", None, None),
            P("dp", None, "lat", None),
            P("dp"),
            P("lat", "dp"),
            P(("dp", "lat")),
            P("dp", "lat", None, None),
        ),
        out_specs=(
            P("dp", "lat", None, None),
            P("dp", "lat", None, None),
            P("lat", "dp"),
            P(("dp", "lat")),
        ),
        check_vma=False,
    )
```

```python
from functools import partial
import math

import jax
import jax.numpy as jnp
import numpy as np
from jax import lax
from jax.experimental import pallas as pl
from jax.experimental.pallas import tpu as pltpu
from jax.sharding import PartitionSpec as P

D = 641
HID = 1282
NOISE = 8
NLAT = 48
NLON = 72
LDEG = 48
ORDERS = 36
STEPS = 2
CIN = D + NOISE

HIGHEST = lax.Precision.HIGHEST


def shortened(shard):
    return jax.tree.map(lambda a: a.astype(jnp.bfloat16) if a.dtype == jnp.float32 else a, shard)


def legendre_values(lat_total, degree_total, order_total):
    colatitude = np.pi * (np.arange(lat_total) + 0.5) / lat_total
    cosine = np.cos(colatitude)
    sine_part = np.sin(colatitude)
    legendre = np.zeros((lat_total, degree_total, order_total))
    diagonal = np.full(lat_total, 1.0 / math.sqrt(4.0 * math.pi))
    for column in range(order_total):
        if column > 0:
            diagonal = diagonal * math.sqrt((2.0 * column + 1.0) / (2.0 * column)) * sine_part
        legendre[:, column, column] = diagonal
        legendre[:, column + 1, column] = math.sqrt(2.0 * column + 3.0) * cosine * diagonal
        for degree in range(column + 2, degree_total):
            factor_one = math.sqrt(
                (4.0 * degree * degree - 1.0) / (degree * degree - column * column)
            )
            factor_two = math.sqrt(
                ((degree - 1.0) ** 2 - column * column) / (4.0 * (degree - 1.0) ** 2 - 1.0)
            )
            legendre[:, degree, column] = factor_one * (
                cosine * legendre[:, degree - 1, column]
                - factor_two * legendre[:, degree - 2, column]
            )
    return (colatitude, legendre)


def spectral_tables(lat_total, lon_total, degree_total, order_total):
    colatitude, legendre = legendre_values(lat_total, degree_total, order_total)
    quadrature = np.sin(colatitude) * np.pi / lat_total
    angles = 2.0 * np.pi * np.outer(np.arange(lon_total), np.arange(order_total)) / lon_total
    fourier = np.concatenate([np.cos(angles), -np.sin(angles)], axis=1) * (2.0 * np.pi / lon_total)
    weights = np.where(np.arange(order_total) == 0, 1.0, 2.0)
    inverse = np.concatenate(
        [np.cos(angles).T * weights[:, None], -np.sin(angles).T * weights[:, None]], axis=0
    )
    doubled = np.concatenate([legendre, legendre], axis=2)
    analysis = doubled * quadrature[:, None, None]
    return tuple(
        (np.asarray(member, np.float32) for member in (fourier, inverse, analysis, doubled))
    )


def normalize(values, scale_gain, shift_vec):
    centered = values - jnp.mean(values, axis=-1, keepdims=True)
    inverse_scale = lax.rsqrt(jnp.mean(centered * centered, axis=-1, keepdims=True) + 1e-06)
    unit = centered * inverse_scale
    return (unit * scale_gain + shift_vec, unit, inverse_scale)


def normalize_back(upstream, unit, inverse_scale, scale_gain):
    scaled = upstream * scale_gain
    mean_one = jnp.mean(scaled, axis=-1, keepdims=True)
    mean_two = jnp.mean(scaled * unit, axis=-1, keepdims=True)
    grad_input = inverse_scale * (scaled - mean_one - unit * mean_two)
    return (grad_input, jnp.sum(upstream * unit, axis=(0, 1, 2)), jnp.sum(upstream, axis=(0, 1, 2)))


def unpack_mlp(flat):
    pieces = []
    offset = 0
    for length in (D, D, D, D, HID, D):
        pieces.append(flat[offset : offset + length].astype(jnp.float32))
        offset = offset + length
    w_in = flat[offset : offset + D * HID].reshape(D, HID)
    offset = offset + D * HID
    w_out = flat[offset : offset + HID * D].reshape(HID, D)
    return (tuple(pieces), w_in, w_out)


def build_weights(spectral_whole, mlp_whole, degrees_here):
    count_all = degrees_here * (D + NOISE) * D
    spectral = spectral_whole[0, :count_all].reshape(degrees_here, D + NOISE, D)
    vectors, w_in, w_out = unpack_mlp(mlp_whole)
    return (spectral, vectors, w_in, w_out)


def forward_step(current, noise_step, step_mask, tables, weights):
    (
        fourier,
        inverse,
        analysis_here,
        synthesis_here,
        analysis_rows,
        synthesis_rows,
        analysis_degrees,
        synthesis_degrees,
    ) = tables
    spectral, vectors, w_in, w_out = weights
    gain_one, shift_one, gain_two, shift_two, bias_hidden, bias_out = vectors
    normed, unit_one, scale_one = normalize(current, gain_one, shift_one)
    joined = jnp.concatenate([normed, noise_step], axis=-1)
    grid_modes = jnp.einsum("bjnc,nk->bjkc", joined, fourier, precision=HIGHEST)
    by_order = lax.all_to_all(
        shortened(grid_modes), "lat", split_axis=2, concat_axis=1, tiled=True
    ).astype(grid_modes.dtype)
    coeffs = jnp.einsum("jlk,bjkc->blkc", analysis_here, by_order, precision=HIGHEST).astype(
        jnp.bfloat16
    )
    by_degree = lax.all_to_all(coeffs, "lat", split_axis=1, concat_axis=2, tiled=True)
    mixed_modes = jnp.einsum(
        "blkc,lcd->blkd", by_degree, spectral, preferred_element_type=jnp.float32
    ).astype(jnp.bfloat16)
    mixed_orders = lax.all_to_all(mixed_modes, "lat", split_axis=2, concat_axis=1, tiled=True)
    lat_modes = jnp.einsum(
        "jlk,blkd->bjkd", synthesis_here, mixed_orders.astype(jnp.float32), precision=HIGHEST
    )
    lat_rows = lax.all_to_all(
        shortened(lat_modes), "lat", split_axis=1, concat_axis=2, tiled=True
    ).astype(lat_modes.dtype)
    branch = jnp.einsum("bjkd,kn->bjnd", lat_rows, inverse, precision=HIGHEST)
    middle = current + step_mask * branch
    normed_two, unit_two, scale_two = normalize(middle, gain_two, shift_two)
    hidden_in = normed_two.astype(jnp.bfloat16)
    preactivation = (
        jnp.einsum("bjnd,dh->bjnh", hidden_in, w_in, preferred_element_type=jnp.float32)
        + bias_hidden
    )
    active = jax.nn.gelu(preactivation, approximate=False).astype(jnp.bfloat16)
    result = (
        jnp.einsum("bjnh,hd->bjnd", active, w_out, preferred_element_type=jnp.float32) + bias_out
    )
    kept_values = (
        unit_one,
        scale_one,
        by_degree,
        unit_two,
        scale_two,
        hidden_in,
        preactivation,
        active,
    )
    return (middle + step_mask * result, kept_values)


def backward_step(grad_state, step_mask, kept_values, tables, weights):
    (
        fourier,
        inverse,
        analysis_here,
        synthesis_here,
        analysis_rows,
        synthesis_rows,
        analysis_degrees,
        synthesis_degrees,
    ) = tables
    spectral, vectors, w_in, w_out = weights
    gain_one, shift_one, gain_two, shift_two, bias_hidden, bias_out = vectors
    unit_one, scale_one, by_degree, unit_two, scale_two, hidden_in, preactivation, active = (
        kept_values
    )
    grad_result = (step_mask * grad_state).astype(jnp.bfloat16)
    grad_bias_out = jnp.sum(grad_result.astype(jnp.float32), axis=(0, 1, 2))
    grad_w_out = jnp.einsum(
        "bjnh,bjnd->hd", active, grad_result, preferred_element_type=jnp.float32
    )
    grad_active = jnp.einsum(
        "bjnd,hd->bjnh", grad_result, w_out, preferred_element_type=jnp.float32
    )
    unused, gelu_back = jax.vjp(partial(jax.nn.gelu, approximate=False), preactivation)
    grad_preact = gelu_back(grad_active)[0].astype(jnp.bfloat16)
    grad_bias_hidden = jnp.sum(grad_preact.astype(jnp.float32), axis=(0, 1, 2))
    grad_w_in = jnp.einsum(
        "bjnd,bjnh->dh", hidden_in, grad_preact, preferred_element_type=jnp.float32
    )
    grad_hidden_in = jnp.einsum(
        "bjnh,dh->bjnd", grad_preact, w_in, preferred_element_type=jnp.float32
    )
    grad_norm_two, grad_gain_two, grad_shift_two = normalize_back(
        grad_hidden_in, unit_two, scale_two, gain_two
    )
    grad_middle = grad_state + grad_norm_two
    grad_branch = step_mask * grad_middle
    grad_rows = jnp.einsum("bjnd,kn->bjkd", grad_branch, inverse, precision=HIGHEST)
    grad_modes = lax.all_to_all(
        shortened(grad_rows), "lat", split_axis=2, concat_axis=1, tiled=True
    ).astype(grad_rows.dtype)
    grad_mixed = jnp.einsum("jlk,bjkd->blkd", synthesis_here, grad_modes, precision=HIGHEST).astype(
        jnp.bfloat16
    )
    grad_degree = lax.all_to_all(grad_mixed, "lat", split_axis=1, concat_axis=2, tiled=True)
    grad_spectral = jnp.einsum(
        "blkc,blkd->lcd", by_degree, grad_degree, preferred_element_type=jnp.float32
    )
    grad_coeffs = jnp.einsum(
        "blkd,lcd->blkc", grad_degree, spectral, preferred_element_type=jnp.float32
    ).astype(jnp.bfloat16)
    grad_coeff_orders = lax.all_to_all(grad_coeffs, "lat", split_axis=2, concat_axis=1, tiled=True)
    grad_grid = jnp.einsum(
        "jlk,blkc->bjkc", analysis_here, grad_coeff_orders.astype(jnp.float32), precision=HIGHEST
    )
    grad_lat = lax.all_to_all(
        shortened(grad_grid), "lat", split_axis=1, concat_axis=2, tiled=True
    ).astype(grad_grid.dtype)
    model_width = grad_state.shape[3]
    grad_normed = jnp.einsum(
        "bjkc,nk->bjnc", grad_lat[..., :model_width], fourier, precision=HIGHEST
    )
    grad_norm_one, grad_gain_one, grad_shift_one = normalize_back(
        grad_normed, unit_one, scale_one, gain_one
    )
    vectors_grad = (
        grad_gain_one,
        grad_shift_one,
        grad_gain_two,
        grad_shift_two,
        grad_bias_hidden,
        grad_bias_out,
    )
    return (grad_middle + grad_norm_one, (grad_spectral, vectors_grad, grad_w_in, grad_w_out))


def shards_general(fields, noise_fields, step_counts, spectral_flat, mlp_flat, cotangent):
    lat_count = lax.axis_size("lat")
    lat_index = lax.axis_index("lat")
    dates_here = fields.shape[0]
    rows_here = fields.shape[1]
    degrees_here = LDEG // lat_count
    orders_here = 2 * ORDERS // lat_count
    fourier, inverse, analysis, synthesis = [
        jnp.asarray(member) for member in spectral_tables(NLAT, NLON, LDEG, ORDERS)
    ]
    analysis_here = lax.dynamic_slice_in_dim(analysis, lat_index * orders_here, orders_here, 2)
    synthesis_here = lax.dynamic_slice_in_dim(synthesis, lat_index * orders_here, orders_here, 2)
    analysis_rows = lax.dynamic_slice_in_dim(analysis, lat_index * rows_here, rows_here, 0)
    synthesis_rows = lax.dynamic_slice_in_dim(synthesis, lat_index * rows_here, rows_here, 0)
    analysis_degrees = lax.dynamic_slice_in_dim(analysis, lat_index * degrees_here, degrees_here, 1)
    synthesis_degrees = lax.dynamic_slice_in_dim(
        synthesis, lat_index * degrees_here, degrees_here, 1
    )
    tables = (
        fourier,
        inverse,
        analysis_here,
        synthesis_here,
        analysis_rows,
        synthesis_rows,
        analysis_degrees,
        synthesis_degrees,
    )
    spectral_whole = lax.all_gather(spectral_flat, "dp", axis=1, tiled=True)
    mlp_whole = lax.all_gather(mlp_flat, ("dp", "lat"), axis=0, tiled=True)
    weights = build_weights(spectral_whole, mlp_whole, degrees_here)
    noise_steps = noise_fields.astype(jnp.float32).reshape(
        dates_here, STEPS, rows_here, NLON, NOISE
    )
    current = fields.astype(jnp.float32)
    kept_steps = []
    for step_index in range(STEPS):
        step_mask = (step_index < step_counts).astype(jnp.float32).reshape(dates_here, 1, 1, 1)
        current, kept_values = forward_step(
            current, noise_steps[:, step_index], step_mask, tables, weights
        )
        kept_steps.append((step_mask, kept_values))
    output_fields = current.astype(jnp.bfloat16)
    grad_state = cotangent.astype(jnp.float32)
    totals = None
    for step_index in reversed(range(STEPS)):
        step_mask, kept_values = kept_steps[step_index]
        grad_state, step_totals = backward_step(grad_state, step_mask, kept_values, tables, weights)
        totals = step_totals if totals is None else jax.tree.map(jnp.add, totals, step_totals)
    grad_spectral, grad_vectors, grad_w_in, grad_w_out = totals
    spectral_pad = jnp.zeros((spectral_whole.shape[1] - grad_spectral.size,), jnp.float32)
    spectral_pack = jnp.concatenate([grad_spectral.reshape(-1), spectral_pad]).reshape(1, -1)
    spectral_grad = lax.psum_scatter(
        spectral_pack.astype(jnp.bfloat16), "dp", scatter_dimension=1, tiled=True
    ).astype(jnp.float32)
    mlp_members = list(grad_vectors) + [grad_w_in.reshape(-1), grad_w_out.reshape(-1)]
    used_total = sum((member.size for member in mlp_members))
    mlp_pack = jnp.concatenate(
        mlp_members + [jnp.zeros((mlp_whole.shape[0] - used_total,), jnp.float32)]
    )
    mlp_grad = lax.psum_scatter(mlp_pack, ("dp", "lat"), scatter_dimension=0, tiled=True)
    return (output_fields, grad_state.astype(jnp.bfloat16), spectral_grad, mlp_grad)


ROWS = NLAT // 2
DEGS = LDEG // 2
CELLS = ROWS * NLON
DP = 768
HP = 1408
KP = 72
GROUPS = 9
GK = 8
DEPTH = 8
WROWS = 672
BLK = 4
BC = BLK * NLON
WIN = 992
MAIN = 944
HEAD = 416
BF = jnp.bfloat16
F32 = jnp.float32
MB = 2**20


def params(limit=60, **more):
    return pltpu.CompilerParams(vmem_limit_bytes=limit * MB, **more)


LIGHT = pl.CostEstimate(flops=1, bytes_accessed=1, transcendentals=0)


def vspec():
    return pl.BlockSpec(memory_space=pltpu.VMEM)


def dot(a, b):
    return jnp.dot(a, b, preferred_element_type=F32)


def split_table(table):
    high = table.astype(BF).astype(np.float32)
    return np.concatenate([high, table - high, high], axis=1).astype(BF)


def split_dot(table, value):
    high = value.astype(BF).astype(F32)
    return dot(table, jnp.concatenate([high, high, value - high], axis=0).astype(BF))


def dot_nt(a, b):
    return lax.dot_general(a, b, (((1,), (1,)), ((), ())), preferred_element_type=F32)


def dot_tn(a, b):
    return lax.dot_general(a, b, (((0,), (0,)), ((), ())), preferred_element_type=F32)


def column_order():
    places = np.zeros(KP, np.int64)
    for group in range(GROUPS):
        for i in range(4):
            places[GK * group + i] = 4 * group + i
            places[GK * group + 4 + i] = ORDERS + 4 * group + i
    return places


def plan_tables():
    fourier, inverse, analysis, synthesis = spectral_tables(NLAT, NLON, LDEG, ORDERS)
    take = column_order()
    fourier = fourier[:, take]
    inverse = inverse[take, :]
    analysis = analysis[:, :, take]
    synthesis = synthesis[:, :, take]
    eye = np.eye(GK, dtype=np.float32)

    def blocks(table):
        out = np.zeros((2, GROUPS, 192, 384), np.float32)
        for own in range(2):
            for which in range(2):
                half = own if which == 0 else 1 - own
                for group in range(GROUPS):
                    part = table[24 * own : 24 * own + 24, 24 * half : 24 * half + 24]
                    part = part[:, :, GK * group : GK * group + GK]
                    full = np.einsum("pqi,ij->piqj", part, eye)
                    out[own, group, :, 192 * which : 192 * which + 192] = full.reshape(192, 192)
        return out.astype(BF)

    by_degree = np.transpose
    return dict(
        fourier_t=split_table(fourier.T),
        fourier=split_table(fourier),
        inverse_t=split_table(inverse.T),
        inverse=split_table(inverse),
        analyse=blocks(by_degree(analysis, (1, 0, 2))),
        synthesize=blocks(synthesis),
        analyse_back=blocks(analysis),
        synthesize_back=blocks(by_degree(synthesis, (1, 0, 2))),
    )


def rows_out(flat_ref, start, offset, step, wide, tiles, tail, put, count, unroll=4):
    lane = lax.broadcasted_iota(jnp.int32, (8, 128), 1)

    def one(t, carry):
        shift = offset + step * t
        jump = shift // 128
        shift = shift - 128 * jump
        amount = (128 - shift) % 128
        low = lane + shift < 128
        pieces = [
            pltpu.roll(flat_ref[pl.ds(start + wide * t + jump + m, 8, stride=641), :], amount, 1)
            for m in range(tiles + 1)
        ]
        for m in range(tiles):
            piece = jnp.where(low, pieces[m], pieces[m + 1])
            if m == tiles - 1:
                piece = jnp.where(lane < tail, piece, 0.0)
            put(m, t, piece)
        return carry

    lax.fori_loop(0, count, one, 0, unroll=unroll)


def rows_in(flat_ref, start, offset, step, wide, tiles, get, count, unroll=2):
    lane = lax.broadcasted_iota(jnp.int32, (8, 128), 1)

    def one(t, carry):
        shift = offset + step * t
        jump = shift // 128
        shift = shift - 128 * jump
        high = lane >= shift
        pieces = [pltpu.roll(get(m, t), shift, 1) for m in range(tiles)]
        last = tiles + (1 if step > 1 else 0)
        for m in range(last):
            here = pieces[m] if m < tiles else jnp.zeros((8, 128), F32)
            before = pieces[m - 1] if m > 0 else jnp.zeros((8, 128), F32)
            piece = jnp.where(high, here, before)
            where = pl.ds(start + wide * t + jump + m, 8, stride=641)
            if m == 0 or m >= tiles - 1:
                flat_ref[where, :] = flat_ref[where, :] + piece
            else:
                flat_ref[where, :] = piece
        return carry

    lax.fori_loop(0, count, one, 0, unroll=unroll)


def shard_place(shard, length):
    first = (shard * length) // D
    base = (first // 16) * 16
    start = D * base - length * shard + 128 * 88
    return base, start // 128, start % 128


def window_kernel(length, shard_ref, flat_ref, main_ref, side_ref, flat, tiles, extra):
    chunks = length // 128
    base, start, offset = shard_place(shard_ref[0], length)
    flat[0:88, :] = jnp.zeros((88, 128), F32)
    flat[88 + chunks :, :] = jnp.zeros((flat.shape[0] - 88 - chunks, 128), F32)

    def load(i, carry):
        piece = flat_ref[:, pl.ds(pl.multiple_of(1024 * i, 1024), 1024)]
        flat[pl.ds(pl.multiple_of(88 + 8 * i, 8), 8), :] = piece.astype(F32).reshape(8, 128)
        return carry

    lax.fori_loop(0, chunks // 8, load, 0, unroll=7)
    rest = chunks % 8
    if rest:
        piece = flat_ref[:, 128 * (chunks - rest) :].astype(F32).reshape(rest, 128)
        flat[88 + chunks - rest : 88 + chunks, :] = piece
    lane = lax.broadcasted_iota(jnp.int32, (8, 128), 1)
    extra[...] = jnp.zeros_like(extra)

    def put(m, t, piece):
        if m < 5:
            tiles[m, pl.ds(t, 8, stride=128), :] = piece
        else:
            extra[...] = jnp.where(lane == t, piece[:, 0:1], extra[...])

    rows_out(flat, start, offset, 1, 5, 6, 1, put, 128)
    side_ref[48:64, :] = jnp.zeros((16, 640), BF)
    side_ref[48:64, 0:128] = jnp.concatenate([extra[...], jnp.zeros((8, 128), F32)], axis=0).astype(BF)
    for m in range(5):
        at = slice(128 * m, 128 * m + 128)
        main_ref[:, at] = tiles[m, 16 : 16 + MAIN, :].astype(BF)
        side_ref[0:16, at] = tiles[m, 0:16, :].astype(BF)
        side_ref[16:48, at] = tiles[m, 16 + MAIN : WIN, :].astype(BF)


def spectral_window(shard, flat):
    length = flat.shape[1]
    return pl.pallas_call(
        partial(window_kernel, length),
        out_shape=(jax.ShapeDtypeStruct((MAIN, 640), BF), jax.ShapeDtypeStruct((64, 640), BF)),
        in_specs=[pl.BlockSpec(memory_space=pltpu.SMEM), vspec()],
        out_specs=(vspec(), vspec()),
        scratch_shapes=[
            pltpu.VMEM((5256, 128), F32),
            pltpu.VMEM((5, 1024, 128), F32),
            pltpu.VMEM((8, 128), F32),
        ],
        cost_estimate=LIGHT,
        compiler_params=params(),
    )(shard, flat)


VECTORS = ((0, D), (D, D), (2 * D, D), (3 * D, D), (4 * D, HID), (4 * D + HID, D))
IN_AT = 5 * D + HID
OUT_AT = IN_AT + D * HID


def mlp_kernel(flat_ref, in_ref, out_ref, vec_ref, flat, tin, tout):
    count, rows, _ = flat_ref.shape
    for k in range(count):
        flat[rows * k : rows * k + rows, :] = flat_ref[k].astype(F32)
    lane = lax.broadcasted_iota(jnp.int32, (1, 128), 1)
    vec_ref[...] = jnp.zeros_like(vec_ref)
    for row, (place, length) in enumerate(VECTORS):
        first, shift = place // 128, place % 128
        for m in range(-(-length // 128)):
            one = flat[first + m : first + m + 1, :]
            two = flat[first + m + 1 : first + m + 2, :]
            if shift:
                one = pltpu.roll(one, 128 - shift, 1)
                two = pltpu.roll(two, 128 - shift, 1)
            piece = jnp.where(lane + shift < 128, one, two)
            piece = jnp.where(lane + 128 * m < length, piece, 0.0)
            vec_ref[row : row + 1, 128 * m : 128 * m + 128] = piece
    for part in range(2):

        def put_in(m, t, piece, part=part):
            tin[m, pl.ds(t + 512 * part, 8, stride=64), :] = piece

        rows_out(flat, IN_AT // 128 + 641 * 8 * part, IN_AT % 128, 2, 10, 11, 2, put_in, 64, 2)

        def put_out(m, t, piece, part=part):
            tout[m, pl.ds(t + 1024 * part, 8, stride=128), :] = piece

        rows_out(flat, OUT_AT // 128 + 641 * 8 * part, OUT_AT % 128, 1, 5, 6, 1, put_out, 128, 4)
    keep = lax.broadcasted_iota(jnp.int32, (DP, 128), 0) < D
    for m in range(11):
        in_ref[:, 128 * m : 128 * m + 128] = jnp.where(keep, tin[m, :DP, :], 0.0).astype(BF)
    keep = lax.broadcasted_iota(jnp.int32, (HP, 128), 0) < HID
    for m in range(6):
        out_ref[:, 128 * m : 128 * m + 128] = jnp.where(keep, tout[m, :HP, :], 0.0).astype(BF)


def mlp_weights(flat):
    return pl.pallas_call(
        mlp_kernel,
        out_shape=(
            jax.ShapeDtypeStruct((DP, HP), BF),
            jax.ShapeDtypeStruct((HP, DP), BF),
            jax.ShapeDtypeStruct((8, HP), F32),
        ),
        in_specs=[vspec()],
        out_specs=(vspec(), vspec(), vspec()),
        scratch_shapes=[
            pltpu.VMEM((16776, 128), F32),
            pltpu.VMEM((11, 1024, 128), F32),
            pltpu.VMEM((6, 2048, 128), F32),
        ],
        cost_estimate=LIGHT,
        compiler_params=params(),
    )(flat)


ALL_ROWS = 15584
CHIPS = 8


def cuts(length, count):
    return [((s * length) // D) // 16 * 16 for s in range(count)] + [ALL_ROWS]


def gather_kernel(length, main_ref, side_ref, w_ref, column_ref, sides, edges, line, ring, over, arrive, local):
    dp = lax.axis_index("dp")
    lat = lax.axis_index("lat")
    core = dp % 2
    chip = dp // 2
    z = chip // 2
    x = chip % 2
    place = z + x * (7 - 2 * z)
    home = lat == core
    count = 2 * CHIPS

    def chip_at(p):
        p = (p + CHIPS) % CHIPS
        back = p // 4
        return ((1 - back) * p + back * (7 - p)) * 2 + back

    def device(p, which):
        return (chip_at(p) * 2 + which, lat)

    def shard(p, which):
        return chip_at(p) * 2 + which

    across = (dp, 1 - lat)
    partner = (dp + 1 - 2 * core, lat)
    barrier = pltpu.get_barrier_semaphore()
    for who in (device(place + 1, core), device(place - 1, core), across, partner):
        pl.semaphore_signal(barrier, inc=1, device_id=who, device_id_type=pl.DeviceIdType.MESH)
    pl.semaphore_wait(barrier, 4)

    def rows_of(s, first, size):
        start = ((s * length) // D) // 16 * 16 + 16 + first
        return w_ref.at[pl.ds(pl.multiple_of(start, 16), size)]

    def remote(src, dst, send, recv, who):
        return pltpu.make_async_remote_copy(
            src_ref=src, dst_ref=dst, send_sem=send, recv_sem=recv, device_id=who,
            device_id_type=pl.DeviceIdType.MESH,
        )

    first = core
    second = 1 - core
    hops = {1: [(0, 0), (0, 1), (1, 0), (1, 1), (2, 0), (2, 1), (3, 0)],
            -1: [(0, 0), (0, 1), (1, 0), (1, 1), (2, 0), (2, 1), (3, 1)]}
    coming = [(way, d, w) for d in (1, 2, 3) for w in (0, 1) for way in (1, -1)] + [(1, 4, 0), (-1, 4, 1)]

    def named(way, d, w):
        which = first if w == 0 else second
        return shard(place - way * d, which)

    def wait_part(kind, s, size):
        remote(rows_of(s, 0, size), rows_of(s, 0, size), local.at[0], arrive.at[kind, s], across).wait_recv()

    def wait_side(s):
        remote(sides.at[s], sides.at[s], local.at[0], arrive.at[2, s], across).wait_recv()

    own = dp

    @pl.when(home)
    def _():
        keep = pltpu.make_async_copy(main_ref, rows_of(own, 0, MAIN), local.at[0])
        keep.start()
        keep_side = pltpu.make_async_copy(side_ref, sides.at[own], local.at[1])
        keep_side.start()
        sent = []

        def send(way, hop, s, main, side):
            to = device(place + way, core)
            lane = 0 if way == 1 else 1
            copies = (
                remote(main, rows_of(s, 0, MAIN), ring.at[lane, hop], arrive.at[0, s], to),
                remote(side, sides.at[s], ring.at[lane + 2, hop], arrive.at[2, s], to),
            )
            for copy in copies:
                copy.start()
                sent.append(copy)

        def cross(index, s, main, side):
            copies = [remote(main(0, HEAD), rows_of(s, 0, HEAD), over.at[0, index], arrive.at[1, s], across)]
            copies.append(remote(side, sides.at[s], over.at[1, index], arrive.at[2, s], across))
            if index < 2:
                copies.insert(
                    0,
                    remote(
                        main(HEAD, MAIN - HEAD), rows_of(s, HEAD, MAIN - HEAD), over.at[2, index],
                        arrive.at[0, s], across,
                    ),
                )
            for copy in copies:
                copy.start()
                sent.append(copy)

        send(1, 0, own, main_ref, side_ref)
        send(-1, 0, own, main_ref, side_ref)
        cross(0, own, lambda at, size: main_ref.at[pl.ds(at, size)], side_ref)
        mate = dp + 1 - 2 * core
        wait_part(0, mate, MAIN)
        wait_side(mate)
        held = lambda s: (lambda at, size: rows_of(s, at, size))
        send(1, 1, mate, rows_of(mate, 0, MAIN), sides.at[mate])
        send(-1, 1, mate, rows_of(mate, 0, MAIN), sides.at[mate])
        cross(1, mate, held(mate), sides.at[mate])
        for index, (way, d, w) in enumerate(coming):
            s = named(way, d, w)
            wait_part(0, s, MAIN)
            wait_side(s)
            if (d, w) in hops[way]:
                send(way, hops[way].index((d, w)), s, rows_of(s, 0, MAIN), sides.at[s])
            cross(2 + index, s, held(s), sides.at[s])
        for copy in sent:
            copy.wait_send()
        keep.wait()
        keep_side.wait()

    @pl.when(jnp.logical_not(home))
    def _():
        sent = [
            remote(main_ref, rows_of(own, 0, MAIN), ring.at[4, 0], arrive.at[0, own], partner),
            remote(side_ref, sides.at[own], ring.at[4, 1], arrive.at[2, own], partner),
        ]
        for copy in sent:
            copy.start()
        size = MAIN - HEAD

        def send(way, hop, s):
            lane = 0 if way == 1 else 1
            copy = remote(
                rows_of(s, HEAD, size), rows_of(s, HEAD, size), ring.at[lane, hop], arrive.at[0, s],
                device(place + way, core),
            )
            copy.start()
            sent.append(copy)

        mate = dp + 1 - 2 * core
        wait_part(0, own, size)
        send(1, 0, own)
        send(-1, 0, own)
        wait_part(0, mate, size)
        send(1, 1, mate)
        send(-1, 1, mate)
        for way, d, w in coming:
            s = named(way, d, w)
            wait_part(0, s, size)
            if (d, w) in hops[way]:
                send(way, hops[way].index((d, w)), s)
        for s in [own, mate] + [named(*one) for one in coming]:
            wait_part(1, s, HEAD)
            wait_side(s)
        for copy in sent:
            copy.wait_send()

    places = cuts(length, count)
    copies = []
    for s in range(count):
        span = places[s + 1] - places[s]
        edge = sides[s, 0:16, :]
        if s:
            before = places[s] - places[s - 1] - 16 - MAIN
            edge = edge + sides[s - 1, 16 + before : 32 + before, :]
        edges[s] = edge
        copies.append(pltpu.make_async_copy(edges.at[s], w_ref.at[pl.ds(places[s], 16)], local.at[2 + s]))
        left = span - 16 - MAIN
        if left:
            copies.append(
                pltpu.make_async_copy(
                    sides.at[s, pl.ds(16, left)], w_ref.at[pl.ds(places[s] + 16 + MAIN, left)],
                    local.at[2 + count + s],
                )
            )
    for copy in copies:
        copy.start()
    lane = lax.broadcasted_iota(jnp.int32, (8, 128), 1)
    line[...] = jnp.zeros_like(line)
    for s in range(count):
        a, b = places[s] // 128, places[s] % 128
        piece = sides[s, 48:64, 0:128].astype(F32)[:8]
        if b:
            piece = pltpu.roll(piece, b, 1)
        line[a : a + 8, :] += jnp.where(lane >= b, piece, 0.0)
        line[a + 1 : a + 9, :] += jnp.where(lane < b, piece, 0.0)
    lane = lax.broadcasted_iota(jnp.int32, (1, 128), 1)
    for degree in range(DEGS):
        a, b = CIN * degree // 128, CIN * degree % 128
        piece = line[a : a + 8, :]
        if b:
            piece = pltpu.roll(piece, 128 - b, 1)
        for m in range(6):
            one = jnp.where(lane + b < 128, piece[m : m + 1], piece[m + 1 : m + 2])
            one = jnp.where(lane + 128 * m < CIN, one, 0.0)
            column_ref[degree : degree + 1, 128 * m : 128 * m + 128] = one
    for copy in copies:
        copy.wait()


def gather_rows(length, main, side):
    count = 2 * CHIPS
    return pl.pallas_call(
        partial(gather_kernel, length),
        out_shape=(jax.ShapeDtypeStruct((ALL_ROWS, 640), BF), jax.ShapeDtypeStruct((DEGS, DP), F32)),
        in_specs=[vspec(), vspec()],
        out_specs=(pl.BlockSpec(memory_space=pl.ANY), vspec()),
        scratch_shapes=[
            pltpu.VMEM((count, 64, 640), BF),
            pltpu.VMEM((count, 16, 640), BF),
            pltpu.VMEM((136, 128), F32),
            pltpu.SemaphoreType.DMA((5, 7)),
            pltpu.SemaphoreType.DMA((3, count)),
            pltpu.SemaphoreType.DMA((3, count)),
            pltpu.SemaphoreType.DMA((2 + 2 * count,)),
        ],
        cost_estimate=LIGHT,
        compiler_params=params(30, collective_id=0, has_side_effects=True),
    )(main, side)


def lane_mask():
    return (lax.broadcasted_iota(jnp.int32, (1, DP), 1) < D).astype(F32)


def unit_of(values, mask):
    mean = jnp.sum(values, axis=-1, keepdims=True) * (1.0 / D)
    centred = (values - mean) * mask
    square = jnp.sum(centred * centred, axis=-1, keepdims=True) * (1.0 / D)
    scale = lax.rsqrt(square + 1e-06)
    return centred * scale, scale


def norm_back(upstream, unit, scale, gain):
    scaled = upstream * gain
    mean_one = jnp.sum(scaled, axis=-1, keepdims=True) * (1.0 / D)
    mean_two = jnp.sum(scaled * unit, axis=-1, keepdims=True) * (1.0 / D)
    return scale * (scaled - mean_one * lane_mask() - unit * mean_two)


def modes_kernel(state_ref, noise_ref, vec_ref, table_ref, out_ref):
    unit, scale = unit_of(state_ref[...].astype(F32), lane_mask())
    normed = unit * vec_ref[0:1, :DP] + vec_ref[1:2, :DP]
    joined = jnp.concatenate(
        [normed[:, :640], normed[:, 640:] + noise_ref[...].astype(F32)], axis=1
    )
    for j in range(BLK):
        piece = joined[NLON * j : NLON * j + NLON, :]
        out_ref[j] = split_dot(table_ref[...], piece).astype(BF).reshape(GROUPS, GK, DP)


def modes(state, noise, vectors, table):
    return pl.pallas_call(
        modes_kernel,
        grid=(ROWS // BLK,),
        out_shape=jax.ShapeDtypeStruct((ROWS, GROUPS, GK, DP), BF),
        in_specs=[
            pl.BlockSpec((BC, DP), lambda i: (i, 0)),
            pl.BlockSpec((BC, 128), lambda i: (i, 0)),
            pl.BlockSpec((8, HP), lambda i: (0, 0)),
            pl.BlockSpec((KP, 3 * NLON), lambda i: (0, 0)),
        ],
        out_specs=pl.BlockSpec((BLK, GROUPS, GK, DP), lambda i: (i, 0, 0, 0)),
        cost_estimate=LIGHT,
        compiler_params=params(),
    )(state, noise, vectors, table)


def legendre(table_ref, own_ref, other_ref, out_ref):
    for group in range(GROUPS):
        both = jnp.concatenate(
            [own_ref[:, group].reshape(192, DP), other_ref[:, group].reshape(192, DP)], axis=0
        )
        total = dot(table_ref[0, group], both)
        out_ref[:, group] = total.astype(out_ref.dtype).reshape(24, GK, DP)


def fetch(w_ref, w_buf, sem, degree):
    slot = degree % DEPTH
    first = pl.multiple_of((CIN * degree) // 16 * 16, 16)
    return pltpu.make_async_copy(w_ref.at[pl.ds(first, WROWS)], w_buf.at[slot], sem.at[slot])


def fetch_next(w_ref, w_buf, sem, degree):
    fetch(w_ref, w_buf, sem, degree).wait()


def fetch_ahead(w_ref, w_buf, sem, degree):
    @pl.when(degree + DEPTH < DEGS)
    def _():
        fetch(w_ref, w_buf, sem, degree + DEPTH).start()


C_TILES = 9
G_TILES = 11
OWNERS = 16


def owner_degrees(owner):
    first = 3 * (owner // 2)
    return first + 2 * (owner % 2), first + 1


def pack_tiles(block_ref, parts_ref, middle_tiles):
    lane = lax.broadcasted_iota(jnp.int32, (KP, 128), 1)
    for owner in range(OWNERS):
        own, middle = owner_degrees(owner)
        for m in range(5):
            at = slice(128 * m, 128 * m + 128)
            parts_ref[owner, m] = block_ref[own, :, :, at].reshape(KP, 128)
        for n, m in enumerate(middle_tiles[owner % 2]):
            at = slice(128 * m, 128 * m + 128)
            parts_ref[owner, 5 + n] = block_ref[middle, :, :, at].reshape(KP, 128)
        one = block_ref[own, :, :, 640:].reshape(KP, 128).astype(F32)
        two = block_ref[middle, :, :, 640:].reshape(KP, 128).astype(F32)
        two = pltpu.roll(two, 16, 1)
        last = parts_ref.shape[1] - 1
        parts_ref[owner, last] = jnp.where(lane < 16, one, two).astype(BF)


def mix_kernel(
    half_ref, own_ref, other_ref, table_ref, column_ref, w_ref, parts_ref, mixed_ref, coeff_ref, w_buf, sem,
):
    for degree in range(DEPTH):
        fetch(w_ref, w_buf, sem, degree).start()
    legendre(table_ref, own_ref, other_ref, coeff_ref)
    pack_tiles(coeff_ref, parts_ref, ((0, 1, 2), (2, 3, 4)))
    lane = lax.broadcasted_iota(jnp.int32, (KP, 128), 1)

    def one(degree, carry):
        fetch_next(w_ref, w_buf, sem, degree)
        coeffs = coeff_ref[degree].reshape(KP, DP).astype(F32)
        moved = pltpu.roll(coeffs, (CIN * degree) % 16, 1)
        mixed = dot(moved[:, :WROWS].astype(BF), w_buf[degree % DEPTH])
        last = jnp.sum(coeffs * column_ref[pl.ds(degree, 1), :], axis=1, keepdims=True)
        mixed = jnp.concatenate([mixed, jnp.where(lane < 1, last, 0.0)], axis=1)
        mixed_ref[degree] = mixed.astype(BF).reshape(GROUPS, GK, DP)
        fetch_ahead(w_ref, w_buf, sem, degree)
        return carry

    lax.fori_loop(0, DEGS, one, 0)


def mix_back_kernel(
    half_ref, own_ref, other_ref, table_ref, column_ref, w_ref, parts_ref, out_ref, grad_ref, w_buf, wide, sem,
):
    for degree in range(DEPTH):
        fetch(w_ref, w_buf, sem, degree).start()
    legendre(table_ref, own_ref, other_ref, grad_ref)
    every = (0, 1, 2, 3, 4)
    pack_tiles(grad_ref, parts_ref, (every, every))
    keep = lax.broadcasted_iota(jnp.int32, (KP, DP), 1) < CIN
    wide[...] = jnp.zeros_like(wide)

    def one(degree, carry):
        fetch_next(w_ref, w_buf, sem, degree)
        grad = grad_ref[degree].reshape(KP, DP)
        wide[:, :WROWS] = dot_nt(grad[:, :640], w_buf[degree % DEPTH])
        back = pltpu.roll(wide[...], DP - (CIN * degree) % 16, 1)
        last = grad[:, 640:].astype(F32)[:, 0:1]
        back = back + last * column_ref[pl.ds(degree, 1), :]
        out_ref[degree] = jnp.where(keep, back, 0.0).astype(BF).reshape(GROUPS, GK, DP)
        fetch_ahead(w_ref, w_buf, sem, degree)
        return carry

    lax.fori_loop(0, DEGS, one, 0)


def mix(half, own, other, table, weights, column, back):
    whole = fixed(24, GROUPS, GK, DP)
    tiles = G_TILES if back else C_TILES
    scratch = [pltpu.VMEM((24, GROUPS, GK, DP), BF), pltpu.VMEM((DEPTH, WROWS, 640), BF)]
    if back:
        scratch.append(pltpu.VMEM((KP, DP), F32))
    scratch.append(pltpu.SemaphoreType.DMA((DEPTH,)))
    return pl.pallas_call(
        mix_back_kernel if back else mix_kernel,
        grid_spec=pltpu.PrefetchScalarGridSpec(
            num_scalar_prefetch=1,
            grid=(1,),
            in_specs=[
                whole,
                whole,
                table_spec(),
                fixed(DEGS, DP),
                pl.BlockSpec(memory_space=pl.ANY),
            ],
            out_specs=(fixed(OWNERS, tiles, KP, 128), whole),
            scratch_shapes=scratch,
        ),
        out_shape=(
            jax.ShapeDtypeStruct((OWNERS, tiles, KP, 128), BF),
            jax.ShapeDtypeStruct((24, GROUPS, GK, DP), BF),
        ),
        cost_estimate=LIGHT,
        compiler_params=params(),
    )(half, own, other, table, column, weights)


HID_PARTS = ((0, 256), (256, 256), (512, 256), (768, 256), (1024, 256), (1280, 128))


def feed_kernel(
    half_ref, mask_ref, own_ref, other_ref, table_ref, inverse_ref, state_ref, vec_ref, in_ref, out_ref,
    next_ref, middle_ref, hidden_ref, active_ref, slope_ref, lat,
):
    i = pl.program_id(0)

    @pl.when(i == 0)
    def _():
        legendre(table_ref, own_ref, other_ref, lat)

    mask = mask_ref[0]
    parts = [split_dot(inverse_ref[...], lat[BLK * i + j].reshape(KP, DP)) for j in range(BLK)]
    middle = state_ref[...].astype(F32) + mask * jnp.concatenate(parts, axis=0)
    middle_ref[...] = middle
    unit, scale = unit_of(middle, lane_mask())
    hidden = (unit * vec_ref[2:3, :DP] + vec_ref[3:4, :DP]).astype(BF)
    hidden_ref[...] = hidden
    for first, width in HID_PARTS:
        at = slice(first, first + width)
        pre = dot(hidden, in_ref[:, at]) + vec_ref[4:5, at]
        bell = 0.5 * (1.0 + lax.erf(pre * (1.0 / math.sqrt(2.0))))
        active_ref[:, at] = (pre * bell).astype(BF)
        slope = bell + pre * (jnp.exp(-0.5 * pre * pre) * (1.0 / math.sqrt(2.0 * math.pi)))
        slope_ref[:, at] = slope.astype(BF)
    result = dot(active_ref[...], out_ref[...]) + vec_ref[5:6, :DP]
    next_ref[...] = (middle + mask * result).astype(next_ref.dtype)


def cell_spec(width):
    return pl.BlockSpec((BC, width), lambda i, *h: (i, 0))


def fixed(*shape):
    return pl.BlockSpec(shape, lambda i, *h: (0,) * len(shape))


def table_spec():
    return pl.BlockSpec((1, GROUPS, 192, 384), lambda i, h, *m: (h[0], 0, 0, 0))


def feed(half, mask, own, other, table, inverse_t, state, vectors, w_in, w_out, last):
    cells = lambda width, kind: jax.ShapeDtypeStruct((CELLS, width), kind)
    return pl.pallas_call(
        feed_kernel,
        grid_spec=pltpu.PrefetchScalarGridSpec(
            num_scalar_prefetch=2,
            grid=(ROWS // BLK,),
            in_specs=[
                fixed(24, GROUPS, GK, DP), fixed(24, GROUPS, GK, DP), table_spec(), fixed(NLON, 3 * KP), cell_spec(DP),
                fixed(8, HP), fixed(DP, HP), fixed(HP, DP),
            ],
            out_specs=(cell_spec(DP), cell_spec(DP), cell_spec(DP), cell_spec(HP), cell_spec(HP)),
            scratch_shapes=[pltpu.VMEM((24, GROUPS, GK, DP), F32)],
        ),
        out_shape=(
            cells(DP, BF if last else F32), cells(DP, F32), cells(DP, BF), cells(HP, BF), cells(HP, BF),
        ),
        cost_estimate=LIGHT,
        compiler_params=params(),
    )(half, mask, own, other, table, inverse_t, state, vectors, w_in, w_out)


def feed_back_kernel(
    mask_ref, grad_ref, slope_ref, middle_ref, vec_ref, in_ref, out_ref, inverse_ref,
    result_ref, pre_ref, gm_ref, modes_ref, sums_ref,
):
    i = pl.program_id(0)

    @pl.when(i == 0)
    def _():
        sums_ref[...] = jnp.zeros_like(sums_ref)

    mask = mask_ref[0]
    grad = grad_ref[...].astype(F32)
    result = (mask * grad).astype(BF)
    result_ref[...] = result
    sums_ref[5:6, :DP] += jnp.sum(result.astype(F32), axis=0, keepdims=True)
    for first, width in HID_PARTS:
        at = slice(first, first + width)
        active = dot_nt(result, out_ref[at, :])
        pre = (active * slope_ref[:, at].astype(F32)).astype(BF)
        pre_ref[:, at] = pre
        sums_ref[4:5, at] += jnp.sum(pre.astype(F32), axis=0, keepdims=True)
    upstream = dot_nt(pre_ref[...], in_ref[...])
    unit, scale = unit_of(middle_ref[...], lane_mask())
    sums_ref[2:3, :DP] += jnp.sum(upstream * unit, axis=0, keepdims=True)
    sums_ref[3:4, :DP] += jnp.sum(upstream, axis=0, keepdims=True)
    total = grad + norm_back(upstream, unit, scale, vec_ref[2:3, :DP])
    gm_ref[...] = total
    total = mask * total
    for j in range(BLK):
        piece = total[NLON * j : NLON * j + NLON, :]
        modes_ref[j] = split_dot(inverse_ref[...], piece).astype(BF).reshape(GROUPS, GK, DP)


def feed_back(mask, grad, slope, middle, vectors, w_in, w_out, inverse):
    cells = lambda width, kind: jax.ShapeDtypeStruct((CELLS, width), kind)
    return pl.pallas_call(
        feed_back_kernel,
        grid_spec=pltpu.PrefetchScalarGridSpec(
            num_scalar_prefetch=1,
            grid=(ROWS // BLK,),
            in_specs=[
                cell_spec(DP), cell_spec(HP), cell_spec(DP), fixed(8, HP), fixed(DP, HP), fixed(HP, DP),
                fixed(KP, 3 * NLON),
            ],
            out_specs=(
                cell_spec(DP), cell_spec(HP), cell_spec(DP),
                pl.BlockSpec((BLK, GROUPS, GK, DP), lambda i, *h: (i, 0, 0, 0)), fixed(8, HP),
            ),
        ),
        out_shape=(
            cells(DP, BF), cells(HP, BF), cells(DP, F32), jax.ShapeDtypeStruct((ROWS, GROUPS, GK, DP), BF),
            jax.ShapeDtypeStruct((8, HP), F32),
        ),
        cost_estimate=LIGHT,
        compiler_params=params(),
    )(mask, grad, slope, middle, vectors, w_in, w_out, inverse)


def first_back_kernel(
    half_ref, own_ref, other_ref, table_ref, fourier_ref, state_ref, gm_ref, vec_ref, out_ref, sums_ref, lat,
):
    i = pl.program_id(0)

    @pl.when(i == 0)
    def _():
        legendre(table_ref, own_ref, other_ref, lat)
        sums_ref[...] = jnp.zeros_like(sums_ref)

    parts = [split_dot(fourier_ref[...], lat[BLK * i + j].reshape(KP, DP)) for j in range(BLK)]
    upstream = jnp.concatenate(parts, axis=0)
    unit, scale = unit_of(state_ref[...].astype(F32), lane_mask())
    sums_ref[0:1, :] += jnp.sum(upstream * unit, axis=0, keepdims=True)
    sums_ref[1:2, :] += jnp.sum(upstream, axis=0, keepdims=True)
    total = gm_ref[...] + norm_back(upstream, unit, scale, vec_ref[0:1, :DP])
    out_ref[...] = total.astype(out_ref.dtype)


def first_back(half, own, other, table, fourier, state, gm, vectors, last):
    return pl.pallas_call(
        first_back_kernel,
        grid_spec=pltpu.PrefetchScalarGridSpec(
            num_scalar_prefetch=1,
            grid=(ROWS // BLK,),
            in_specs=[
                fixed(24, GROUPS, GK, DP), fixed(24, GROUPS, GK, DP), table_spec(), fixed(NLON, 3 * KP), cell_spec(DP),
                cell_spec(DP), fixed(8, HP),
            ],
            out_specs=(cell_spec(DP), fixed(8, DP)),
            scratch_shapes=[pltpu.VMEM((24, GROUPS, GK, DP), F32)],
        ),
        out_shape=(
            jax.ShapeDtypeStruct((CELLS, DP), BF if last else F32), jax.ShapeDtypeStruct((8, DP), F32),
        ),
        cost_estimate=LIGHT,
        compiler_params=params(),
    )(half, own, other, table, fourier, state, gm, vectors)


def mlp_grad_kernel(h0, h1, p0, p1, a0, a1, r0, r1, tin, tout, turned):
    for step, ref in enumerate((h0, h1)):
        turned[:, CELLS * step : CELLS * step + CELLS] = ref[...].T
    for first, width in HID_PARTS:
        at = slice(first, first + width)
        part = dot(turned[:, :CELLS], p0[:, at]) + dot(turned[:, CELLS:], p1[:, at])
        for m in range(width // 128):
            tin[first // 128 + m] = part[:, 128 * m : 128 * m + 128]
        part = dot_tn(a0[:, at], r0[...]) + dot_tn(a1[:, at], r1[...])
        for m in range(6):
            tout[m, at, :] = part[:, 128 * m : 128 * m + 128]


def mlp_flat_kernel(gin, gout, feed_sums, first_sums, pack_ref, tin, tout, flat_ref):
    tin[:, :DP, :] = gin[...]
    tout[:, :HP, :] = gout[...]
    tin[:, DP:, :] = jnp.zeros((11, 1024 - DP, 128), F32)
    tout[:, HP:, :] = jnp.zeros((6, 2048 - HP, 128), F32)
    flat_ref[...] = jnp.zeros_like(flat_ref)
    lane = lax.broadcasted_iota(jnp.int32, (1, 128), 1)
    sums = feed_sums[...]
    for row, (place, length) in enumerate(VECTORS):
        first, shift = place // 128, place % 128
        for m in range(-(-length // 128)):
            at = slice(128 * m, 128 * m + 128)
            piece = first_sums[row : row + 1, at] if row < 2 else sums[row : row + 1, at]
            piece = jnp.where(lane + 128 * m < length, piece, 0.0)
            if shift:
                piece = pltpu.roll(piece, shift, 1)
            flat_ref[first + m : first + m + 1, :] += jnp.where(lane >= shift, piece, 0.0)
            flat_ref[first + m + 1 : first + m + 2, :] += jnp.where(lane < shift, piece, 0.0)
    for part in range(2):

        def get_in(m, t, part=part):
            return tin[m, pl.ds(t + 512 * part, 8, stride=64), :]

        rows_in(flat_ref, IN_AT // 128 + 641 * 8 * part, IN_AT % 128, 2, 10, 11, get_in, 64, 1)

    for part in range(2):

        def get_out(m, t, part=part):
            return tout[m, pl.ds(t + 1024 * part, 8, stride=128), :]

        rows_in(flat_ref, OUT_AT // 128 + 641 * 8 * part, OUT_AT % 128, 1, 5, 6, get_out, 128, 2)
    for k in range(32):
        piece = flat_ref[SHARD_ROWS * k : SHARD_ROWS * k + SHARD_ROWS, :]
        piece = jnp.concatenate([piece, jnp.zeros((416 - SHARD_ROWS, 128), F32)], axis=0)
        pack_ref[(k // 2) % 2, (k // 4) * 2 + k % 2] = piece.astype(BF)


FLAT_ROWS = 16784
SHARD_ROWS = 403


def mlp_grads(hidden, pre, active, result, feed_sums, first_sums):
    gin, gout = pl.pallas_call(
        mlp_grad_kernel,
        out_shape=(jax.ShapeDtypeStruct((11, DP, 128), F32), jax.ShapeDtypeStruct((6, HP, 128), F32)),
        in_specs=[vspec()] * 8,
        out_specs=(vspec(), vspec()),
        scratch_shapes=[pltpu.VMEM((DP, 2 * CELLS), BF)],
        cost_estimate=LIGHT,
        compiler_params=params(62),
    )(*hidden, *pre, *active, *result)
    return pl.pallas_call(
        mlp_flat_kernel,
        out_shape=jax.ShapeDtypeStruct((2, 16, 416, 128), BF),
        in_specs=[vspec()] * 4,
        out_specs=vspec(),
        scratch_shapes=[
            pltpu.VMEM((11, 1024, 128), F32),
            pltpu.VMEM((6, 2048, 128), F32),
            pltpu.VMEM((FLAT_ROWS, 128), F32),
        ],
        cost_estimate=LIGHT,
        compiler_params=params(62),
    )(gin, gout, feed_sums, first_sums)


def spectral_grad_kernel(odd_ref, c0, c1, g0, g1, tiles_ref, head_ref):
    rows = OWNERS * KP
    lane = lax.broadcasted_iota(jnp.int32, (DP, 128), 1)
    tiles_ref[:, 0:16, :] = jnp.zeros((6, 16, 128), F32)
    tiles_ref[:, 16 + 2 * CIN :, :] = jnp.zeros((6, 1384 - 16 - 2 * CIN, 128), F32)

    def side(ref, first, count):
        take = [ref[:, m].reshape(rows, 128) for m in list(range(first, first + count)) + [ref.shape[1] - 1]]
        return jnp.concatenate(take, axis=1)

    def product(c_first, c_count, g_first):
        total = dot_tn(side(c0, c_first, c_count), side(g0, g_first, 5))
        return total + dot_tn(side(c1, c_first, c_count), side(g1, g_first, 5))

    def save(start, part, first, count, column):
        for m in range(6):
            piece = part[first : first + count, 128 * m : 128 * m + 128]
            if m == 5:
                if column:
                    piece = pltpu.roll(piece, 128 - column, 1)
                piece = jnp.where(lane[:count] < 1, piece, 0.0)
            tiles_ref[m, start : start + count, :] = piece

    own = product(0, 5, 0)
    head_ref[...] = jnp.concatenate(
        [own[0:8, :640], jnp.where(lane[:8] < 1, own[0:8, 640:], 0.0)], axis=1
    )
    middle = product(5, 3, 5)

    @pl.when(odd_ref[0] == 0)
    def _():
        save(16, own, 0, CIN, 0)
        save(16 + CIN, middle, 0, 384, 16)
        tiles_ref[:, 16 + CIN + 384 : 16 + 2 * CIN, :] = jnp.zeros((6, CIN - 384, 128), F32)

    @pl.when(odd_ref[0] == 1)
    def _():
        tiles_ref[:, 16 : 16 + 256, :] = jnp.zeros((6, 256, 128), F32)
        save(16 + 256, middle, 0, 384, 16)
        save(16 + 640, middle, 400, 9, 16)
        save(16 + CIN, own, 0, CIN, 0)


def spectral_grads(odd, coeffs, grads):
    return pl.pallas_call(
        spectral_grad_kernel,
        out_shape=(jax.ShapeDtypeStruct((6, 1384, 128), F32), jax.ShapeDtypeStruct((8, DP), F32)),
        in_specs=[pl.BlockSpec(memory_space=pltpu.SMEM)] + [vspec()] * 4,
        out_specs=(vspec(), vspec()),
        cost_estimate=LIGHT,
        compiler_params=params(),
    )(odd, *coeffs, *grads)


def flatten_kernel(length, shard_ref, tiles_ref, next_ref, out_ref, tiles, flat):
    chunks = length // 128
    shard = shard_ref[0]
    base, start, offset = shard_place(shard, length)
    move = base - CIN * ((3 * shard) // 2) + 16
    tiles[...] = tiles_ref[...]
    for m in range(6):
        tiles[m, 16 + 2 * CIN : 24 + 2 * CIN, :] = next_ref[:, 128 * m : 128 * m + 128]
    flat[...] = jnp.zeros_like(flat)

    def get(m, t):
        return tiles[m, pl.ds(t + move, 8, stride=128), :]

    rows_in(flat, start, offset, 1, 5, 6, get, 128)

    def save(i, carry):
        piece = flat[pl.ds(pl.multiple_of(88 + 8 * i, 8), 8), :].reshape(1, 1024)
        out_ref[:, pl.ds(pl.multiple_of(1024 * i, 1024), 1024)] = piece
        return carry

    lax.fori_loop(0, chunks // 8, save, 0, unroll=7)
    rest = chunks % 8
    if rest:
        piece = flat[88 + chunks - rest : 88 + chunks, :].reshape(1, 128 * rest)
        out_ref[:, 128 * (chunks - rest) :] = piece


def flatten(shard, tiles, after, length):
    return pl.pallas_call(
        partial(flatten_kernel, length),
        out_shape=jax.ShapeDtypeStruct((1, length), F32),
        in_specs=[pl.BlockSpec(memory_space=pltpu.SMEM), vspec(), vspec()],
        out_specs=vspec(),
        scratch_shapes=[pltpu.VMEM((6, 1384, 128), F32), pltpu.VMEM((5256, 128), F32)],
        cost_estimate=LIGHT,
        compiler_params=params(),
    )(shard, tiles, after)


def wide(block):
    flat = block.reshape(CELLS, D)
    return jnp.pad(flat, ((0, 0), (0, DP - D)))


def shards_paired(fields, noise_fields, step_counts, spectral_flat, mlp_flat, cotangent):
    axes = ("dp", "lat")
    dp_count = lax.axis_size("dp")
    dp_index = lax.axis_index("dp")
    core = dp_index % 2
    lat_index = lax.axis_index("lat")
    length = spectral_flat.shape[1]
    places = [(d, y) for d in range(dp_count) for y in range(2)]
    number = lambda d, y: 2 * d + y
    mirror = [(number(d, y), number(d - d % 2 + y, d % 2)) for d, y in places]
    other_core = [(number(d, y), number(d + 1 - 2 * (d % 2), y)) for d, y in places]
    same_core = [[number(d, y) for d, y in places if d % 2 == c] for c in range(2)]
    stays = core == lat_index

    def mirrored(block):
        moved = lax.ppermute(block, axes, [pair for pair in mirror if pair[0] != pair[1]])
        return jnp.where(stays, block, moved)

    swapped = lambda a: lax.ppermute(a, axes, other_core)
    half = core.astype(jnp.int32).reshape(1)
    tables = {name: jnp.asarray(value) for name, value in plan_tables().items()}

    main, side = spectral_window(dp_index.astype(jnp.int32).reshape(1), spectral_flat)
    weights, column = gather_rows(length, main, side)
    mlp_whole = lax.all_gather(mlp_flat.reshape(-1, 128), axes, axis=0, tiled=False)
    mlp_whole, weights = lax.optimization_barrier((mlp_whole, weights))
    state = mirrored(wide(fields))
    noise = mirrored(noise_fields).reshape(STEPS, CELLS, NOISE)
    noise = jnp.pad(noise, ((0, 0), (0, 0), (1, 128 - 1 - NOISE)))
    counts = mirrored(step_counts)
    later, weights = lax.optimization_barrier((cotangent, weights))
    grad = mirrored(wide(later))
    w_in, w_out, vectors = mlp_weights(mlp_whole)

    kept = []
    for step in range(STEPS):
        mask = (step < counts).astype(F32)
        lon_modes = modes(state, noise[step], vectors, tables["fourier_t"])
        parts, mixed = mix(half, lon_modes, swapped(lon_modes), tables["analyse"], weights, column, False)
        following, middle, hidden, active, slope = feed(
            half, mask, mixed, swapped(mixed), tables["synthesize"], tables["inverse_t"], state, vectors,
            w_in, w_out, step == STEPS - 1,
        )
        kept.append((mask, state, parts, middle, hidden, active, slope))
        state = following
    output = mirrored(state)

    def to_owners(parts):
        return lax.all_to_all(
            parts, axes, split_axis=0, concat_axis=0, tiled=True, axis_index_groups=same_core
        )

    coeff_parts = [to_owners(kept[step][2]) for step in range(STEPS)]
    grad_parts = [None] * STEPS
    results = [None] * STEPS
    pres = [None] * STEPS
    feed_sums = first_sums = 0.0
    for step in reversed(range(STEPS)):
        mask, state, parts, middle, hidden, active, slope = kept[step]
        results[step], pres[step], gm, grad_modes, sums = feed_back(
            mask, grad, slope, middle, vectors, w_in, w_out, tables["inverse"]
        )
        feed_sums = feed_sums + sums
        parts, grad_coeffs = mix(
            half, grad_modes, swapped(grad_modes), tables["synthesize_back"], weights, column, True
        )
        grad_parts[step] = to_owners(parts)
        grad, sums = first_back(
            half, grad_coeffs, swapped(grad_coeffs), tables["analyse_back"], tables["fourier"], state, gm,
            vectors, step == 0,
        )
        first_sums = first_sums + sums
    fields_grad = mirrored(grad)
    mlp_pack = mlp_grads(
        [k[4] for k in kept], pres, [k[5] for k in kept], results, feed_sums, first_sums
    )
    own = lax.dynamic_index_in_dim(mlp_pack, core, 0, keepdims=False)
    give = lax.dynamic_index_in_dim(mlp_pack, 1 - core, 0, keepdims=False)
    pair = (own.astype(F32) + swapped(give).astype(F32)).astype(BF)
    pair = lax.all_to_all(
        pair, axes, split_axis=0, concat_axis=0, tiled=True, axis_index_groups=same_core
    )
    mlp_grad = jnp.sum(pair.astype(F32), axis=0)[: mlp_flat.shape[0] // 128].reshape(-1)

    owner = (dp_index - core + lat_index).astype(jnp.int32).reshape(1)
    odd = lat_index.astype(jnp.int32).reshape(1)
    tiles, head = spectral_grads(odd, coeff_parts, grad_parts)
    spot = lambda s, c: number(s - s % 2 + c, s % 2)
    earlier = [(spot(s, c), spot(s - 1, c)) for s in range(1, dp_count) for c in range(2)]
    after = lax.ppermute(head, axes, earlier)
    spectral_grad = mirrored(flatten(owner, tiles, after, length))
    narrow = lambda a: a[:, :D].reshape(1, ROWS, NLON, D)
    return narrow(output), narrow(fields_grad), spectral_grad, mlp_grad


def solution(mesh):
    paired = mesh.shape["lat"] == 2 and mesh.shape["dp"] == 16
    return jax.shard_map(
        shards_paired if paired else shards_general,
        mesh=mesh,
        in_specs=(
            P("dp", "lat", None, None),
            P("dp", None, "lat", None),
            P("dp"),
            P("lat", "dp"),
            P(("dp", "lat")),
            P("dp", "lat", None, None),
        ),
        out_specs=(
            P("dp", "lat", None, None),
            P("dp", "lat", None, None),
            P("lat", "dp"),
            P(("dp", "lat")),
        ),
        check_vma=False,
    )
```

```python
from functools import partial
import math

import jax
import jax.numpy as jnp
import numpy as np
from jax import lax
from jax.experimental import pallas as pl
from jax.experimental.pallas import tpu as pltpu
from jax.sharding import PartitionSpec as P

D = 641
HID = 1282
NOISE = 8
NLAT = 48
NLON = 72
LDEG = 48
ORDERS = 36
STEPS = 2
CIN = D + NOISE

HIGHEST = lax.Precision.HIGHEST


def shortened(shard):
    return jax.tree.map(lambda a: a.astype(jnp.bfloat16) if a.dtype == jnp.float32 else a, shard)


def legendre_values(lat_total, degree_total, order_total):
    colatitude = np.pi * (np.arange(lat_total) + 0.5) / lat_total
    cosine = np.cos(colatitude)
    sine_part = np.sin(colatitude)
    legendre = np.zeros((lat_total, degree_total, order_total))
    diagonal = np.full(lat_total, 1.0 / math.sqrt(4.0 * math.pi))
    for column in range(order_total):
        if column > 0:
            diagonal = diagonal * math.sqrt((2.0 * column + 1.0) / (2.0 * column)) * sine_part
        legendre[:, column, column] = diagonal
        legendre[:, column + 1, column] = math.sqrt(2.0 * column + 3.0) * cosine * diagonal
        for degree in range(column + 2, degree_total):
            factor_one = math.sqrt(
                (4.0 * degree * degree - 1.0) / (degree * degree - column * column)
            )
            factor_two = math.sqrt(
                ((degree - 1.0) ** 2 - column * column) / (4.0 * (degree - 1.0) ** 2 - 1.0)
            )
            legendre[:, degree, column] = factor_one * (
                cosine * legendre[:, degree - 1, column]
                - factor_two * legendre[:, degree - 2, column]
            )
    return (colatitude, legendre)


def spectral_tables(lat_total, lon_total, degree_total, order_total):
    colatitude, legendre = legendre_values(lat_total, degree_total, order_total)
    quadrature = np.sin(colatitude) * np.pi / lat_total
    angles = 2.0 * np.pi * np.outer(np.arange(lon_total), np.arange(order_total)) / lon_total
    fourier = np.concatenate([np.cos(angles), -np.sin(angles)], axis=1) * (2.0 * np.pi / lon_total)
    weights = np.where(np.arange(order_total) == 0, 1.0, 2.0)
    inverse = np.concatenate(
        [np.cos(angles).T * weights[:, None], -np.sin(angles).T * weights[:, None]], axis=0
    )
    doubled = np.concatenate([legendre, legendre], axis=2)
    analysis = doubled * quadrature[:, None, None]
    return tuple(
        (np.asarray(member, np.float32) for member in (fourier, inverse, analysis, doubled))
    )


def normalize(values, scale_gain, shift_vec):
    centered = values - jnp.mean(values, axis=-1, keepdims=True)
    inverse_scale = lax.rsqrt(jnp.mean(centered * centered, axis=-1, keepdims=True) + 1e-06)
    unit = centered * inverse_scale
    return (unit * scale_gain + shift_vec, unit, inverse_scale)


def normalize_back(upstream, unit, inverse_scale, scale_gain):
    scaled = upstream * scale_gain
    mean_one = jnp.mean(scaled, axis=-1, keepdims=True)
    mean_two = jnp.mean(scaled * unit, axis=-1, keepdims=True)
    grad_input = inverse_scale * (scaled - mean_one - unit * mean_two)
    return (grad_input, jnp.sum(upstream * unit, axis=(0, 1, 2)), jnp.sum(upstream, axis=(0, 1, 2)))


def unpack_mlp(flat):
    pieces = []
    offset = 0
    for length in (D, D, D, D, HID, D):
        pieces.append(flat[offset : offset + length].astype(jnp.float32))
        offset = offset + length
    w_in = flat[offset : offset + D * HID].reshape(D, HID)
    offset = offset + D * HID
    w_out = flat[offset : offset + HID * D].reshape(HID, D)
    return (tuple(pieces), w_in, w_out)


def build_weights(spectral_whole, mlp_whole, degrees_here):
    count_all = degrees_here * (D + NOISE) * D
    spectral = spectral_whole[0, :count_all].reshape(degrees_here, D + NOISE, D)
    vectors, w_in, w_out = unpack_mlp(mlp_whole)
    return (spectral, vectors, w_in, w_out)


def forward_step(current, noise_step, step_mask, tables, weights):
    (
        fourier,
        inverse,
        analysis_here,
        synthesis_here,
        analysis_rows,
        synthesis_rows,
        analysis_degrees,
        synthesis_degrees,
    ) = tables
    spectral, vectors, w_in, w_out = weights
    gain_one, shift_one, gain_two, shift_two, bias_hidden, bias_out = vectors
    normed, unit_one, scale_one = normalize(current, gain_one, shift_one)
    joined = jnp.concatenate([normed, noise_step], axis=-1)
    grid_modes = jnp.einsum("bjnc,nk->bjkc", joined, fourier, precision=HIGHEST)
    by_order = lax.all_to_all(
        shortened(grid_modes), "lat", split_axis=2, concat_axis=1, tiled=True
    ).astype(grid_modes.dtype)
    coeffs = jnp.einsum("jlk,bjkc->blkc", analysis_here, by_order, precision=HIGHEST).astype(
        jnp.bfloat16
    )
    by_degree = lax.all_to_all(coeffs, "lat", split_axis=1, concat_axis=2, tiled=True)
    mixed_modes = jnp.einsum(
        "blkc,lcd->blkd", by_degree, spectral, preferred_element_type=jnp.float32
    ).astype(jnp.bfloat16)
    mixed_orders = lax.all_to_all(mixed_modes, "lat", split_axis=2, concat_axis=1, tiled=True)
    lat_modes = jnp.einsum(
        "jlk,blkd->bjkd", synthesis_here, mixed_orders.astype(jnp.float32), precision=HIGHEST
    )
    lat_rows = lax.all_to_all(
        shortened(lat_modes), "lat", split_axis=1, concat_axis=2, tiled=True
    ).astype(lat_modes.dtype)
    branch = jnp.einsum("bjkd,kn->bjnd", lat_rows, inverse, precision=HIGHEST)
    middle = current + step_mask * branch
    normed_two, unit_two, scale_two = normalize(middle, gain_two, shift_two)
    hidden_in = normed_two.astype(jnp.bfloat16)
    preactivation = (
        jnp.einsum("bjnd,dh->bjnh", hidden_in, w_in, preferred_element_type=jnp.float32)
        + bias_hidden
    )
    active = jax.nn.gelu(preactivation, approximate=False).astype(jnp.bfloat16)
    result = (
        jnp.einsum("bjnh,hd->bjnd", active, w_out, preferred_element_type=jnp.float32) + bias_out
    )
    kept_values = (
        unit_one,
        scale_one,
        by_degree,
        unit_two,
        scale_two,
        hidden_in,
        preactivation,
        active,
    )
    return (middle + step_mask * result, kept_values)


def backward_step(grad_state, step_mask, kept_values, tables, weights):
    (
        fourier,
        inverse,
        analysis_here,
        synthesis_here,
        analysis_rows,
        synthesis_rows,
        analysis_degrees,
        synthesis_degrees,
    ) = tables
    spectral, vectors, w_in, w_out = weights
    gain_one, shift_one, gain_two, shift_two, bias_hidden, bias_out = vectors
    unit_one, scale_one, by_degree, unit_two, scale_two, hidden_in, preactivation, active = (
        kept_values
    )
    grad_result = (step_mask * grad_state).astype(jnp.bfloat16)
    grad_bias_out = jnp.sum(grad_result.astype(jnp.float32), axis=(0, 1, 2))
    grad_w_out = jnp.einsum(
        "bjnh,bjnd->hd", active, grad_result, preferred_element_type=jnp.float32
    )
    grad_active = jnp.einsum(
        "bjnd,hd->bjnh", grad_result, w_out, preferred_element_type=jnp.float32
    )
    unused, gelu_back = jax.vjp(partial(jax.nn.gelu, approximate=False), preactivation)
    grad_preact = gelu_back(grad_active)[0].astype(jnp.bfloat16)
    grad_bias_hidden = jnp.sum(grad_preact.astype(jnp.float32), axis=(0, 1, 2))
    grad_w_in = jnp.einsum(
        "bjnd,bjnh->dh", hidden_in, grad_preact, preferred_element_type=jnp.float32
    )
    grad_hidden_in = jnp.einsum(
        "bjnh,dh->bjnd", grad_preact, w_in, preferred_element_type=jnp.float32
    )
    grad_norm_two, grad_gain_two, grad_shift_two = normalize_back(
        grad_hidden_in, unit_two, scale_two, gain_two
    )
    grad_middle = grad_state + grad_norm_two
    grad_branch = step_mask * grad_middle
    grad_rows = jnp.einsum("bjnd,kn->bjkd", grad_branch, inverse, precision=HIGHEST)
    grad_modes = lax.all_to_all(
        shortened(grad_rows), "lat", split_axis=2, concat_axis=1, tiled=True
    ).astype(grad_rows.dtype)
    grad_mixed = jnp.einsum("jlk,bjkd->blkd", synthesis_here, grad_modes, precision=HIGHEST).astype(
        jnp.bfloat16
    )
    grad_degree = lax.all_to_all(grad_mixed, "lat", split_axis=1, concat_axis=2, tiled=True)
    grad_spectral = jnp.einsum(
        "blkc,blkd->lcd", by_degree, grad_degree, preferred_element_type=jnp.float32
    )
    grad_coeffs = jnp.einsum(
        "blkd,lcd->blkc", grad_degree, spectral, preferred_element_type=jnp.float32
    ).astype(jnp.bfloat16)
    grad_coeff_orders = lax.all_to_all(grad_coeffs, "lat", split_axis=2, concat_axis=1, tiled=True)
    grad_grid = jnp.einsum(
        "jlk,blkc->bjkc", analysis_here, grad_coeff_orders.astype(jnp.float32), precision=HIGHEST
    )
    grad_lat = lax.all_to_all(
        shortened(grad_grid), "lat", split_axis=1, concat_axis=2, tiled=True
    ).astype(grad_grid.dtype)
    model_width = grad_state.shape[3]
    grad_normed = jnp.einsum(
        "bjkc,nk->bjnc", grad_lat[..., :model_width], fourier, precision=HIGHEST
    )
    grad_norm_one, grad_gain_one, grad_shift_one = normalize_back(
        grad_normed, unit_one, scale_one, gain_one
    )
    vectors_grad = (
        grad_gain_one,
        grad_shift_one,
        grad_gain_two,
        grad_shift_two,
        grad_bias_hidden,
        grad_bias_out,
    )
    return (grad_middle + grad_norm_one, (grad_spectral, vectors_grad, grad_w_in, grad_w_out))


def shards_general(fields, noise_fields, step_counts, spectral_flat, mlp_flat, cotangent):
    lat_count = lax.axis_size("lat")
    lat_index = lax.axis_index("lat")
    dates_here = fields.shape[0]
    rows_here = fields.shape[1]
    degrees_here = LDEG // lat_count
    orders_here = 2 * ORDERS // lat_count
    fourier, inverse, analysis, synthesis = [
        jnp.asarray(member) for member in spectral_tables(NLAT, NLON, LDEG, ORDERS)
    ]
    analysis_here = lax.dynamic_slice_in_dim(analysis, lat_index * orders_here, orders_here, 2)
    synthesis_here = lax.dynamic_slice_in_dim(synthesis, lat_index * orders_here, orders_here, 2)
    analysis_rows = lax.dynamic_slice_in_dim(analysis, lat_index * rows_here, rows_here, 0)
    synthesis_rows = lax.dynamic_slice_in_dim(synthesis, lat_index * rows_here, rows_here, 0)
    analysis_degrees = lax.dynamic_slice_in_dim(analysis, lat_index * degrees_here, degrees_here, 1)
    synthesis_degrees = lax.dynamic_slice_in_dim(
        synthesis, lat_index * degrees_here, degrees_here, 1
    )
    tables = (
        fourier,
        inverse,
        analysis_here,
        synthesis_here,
        analysis_rows,
        synthesis_rows,
        analysis_degrees,
        synthesis_degrees,
    )
    spectral_whole = lax.all_gather(spectral_flat, "dp", axis=1, tiled=True)
    mlp_whole = lax.all_gather(mlp_flat, ("dp", "lat"), axis=0, tiled=True)
    weights = build_weights(spectral_whole, mlp_whole, degrees_here)
    noise_steps = noise_fields.astype(jnp.float32).reshape(
        dates_here, STEPS, rows_here, NLON, NOISE
    )
    current = fields.astype(jnp.float32)
    kept_steps = []
    for step_index in range(STEPS):
        step_mask = (step_index < step_counts).astype(jnp.float32).reshape(dates_here, 1, 1, 1)
        current, kept_values = forward_step(
            current, noise_steps[:, step_index], step_mask, tables, weights
        )
        kept_steps.append((step_mask, kept_values))
    output_fields = current.astype(jnp.bfloat16)
    grad_state = cotangent.astype(jnp.float32)
    totals = None
    for step_index in reversed(range(STEPS)):
        step_mask, kept_values = kept_steps[step_index]
        grad_state, step_totals = backward_step(grad_state, step_mask, kept_values, tables, weights)
        totals = step_totals if totals is None else jax.tree.map(jnp.add, totals, step_totals)
    grad_spectral, grad_vectors, grad_w_in, grad_w_out = totals
    spectral_pad = jnp.zeros((spectral_whole.shape[1] - grad_spectral.size,), jnp.float32)
    spectral_pack = jnp.concatenate([grad_spectral.reshape(-1), spectral_pad]).reshape(1, -1)
    spectral_grad = lax.psum_scatter(
        spectral_pack.astype(jnp.bfloat16), "dp", scatter_dimension=1, tiled=True
    ).astype(jnp.float32)
    mlp_members = list(grad_vectors) + [grad_w_in.reshape(-1), grad_w_out.reshape(-1)]
    used_total = sum((member.size for member in mlp_members))
    mlp_pack = jnp.concatenate(
        mlp_members + [jnp.zeros((mlp_whole.shape[0] - used_total,), jnp.float32)]
    )
    mlp_grad = lax.psum_scatter(mlp_pack, ("dp", "lat"), scatter_dimension=0, tiled=True)
    return (output_fields, grad_state.astype(jnp.bfloat16), spectral_grad, mlp_grad)


ROWS = NLAT // 2
DEGS = LDEG // 2
CELLS = ROWS * NLON
DP = 768
HP = 1408
KP = 72
GROUPS = 9
GK = 8
DEPTH = 8
WROWS = 672
BLK = 4
BC = BLK * NLON
WIN = 992
MAIN = 944
TROWS = 1392
HEAD = 352
BF = jnp.bfloat16
F32 = jnp.float32
MB = 2**20


def params(limit=60, **more):
    return pltpu.CompilerParams(vmem_limit_bytes=limit * MB, **more)


LIGHT = pl.CostEstimate(flops=1, bytes_accessed=1, transcendentals=0)


def vspec():
    return pl.BlockSpec(memory_space=pltpu.VMEM)


def dot(a, b):
    return jnp.dot(a, b, preferred_element_type=F32)


def split_table(table):
    high = table.astype(BF).astype(np.float32)
    return np.concatenate([high, table - high, high], axis=1).astype(BF)


def split_dot(table, value):
    high = value.astype(BF).astype(F32)
    return dot(table, jnp.concatenate([high, high, value - high], axis=0).astype(BF))


def dot_nt(a, b):
    return lax.dot_general(a, b, (((1,), (1,)), ((), ())), preferred_element_type=F32)


def dot_tn(a, b):
    return lax.dot_general(a, b, (((0,), (0,)), ((), ())), preferred_element_type=F32)


def column_order():
    places = np.zeros(KP, np.int64)
    for group in range(GROUPS):
        for i in range(4):
            places[GK * group + i] = 4 * group + i
            places[GK * group + 4 + i] = ORDERS + 4 * group + i
    return places


def plan_tables():
    fourier, inverse, analysis, synthesis = spectral_tables(NLAT, NLON, LDEG, ORDERS)
    take = column_order()
    fourier = fourier[:, take]
    inverse = inverse[take, :]
    analysis = analysis[:, :, take]
    synthesis = synthesis[:, :, take]
    eye = np.eye(GK, dtype=np.float32)

    def blocks(table):
        out = np.zeros((2, GROUPS, 192, 384), np.float32)
        for own in range(2):
            for which in range(2):
                half = own if which == 0 else 1 - own
                for group in range(GROUPS):
                    part = table[24 * own : 24 * own + 24, 24 * half : 24 * half + 24]
                    part = part[:, :, GK * group : GK * group + GK]
                    full = np.einsum("pqi,ij->piqj", part, eye)
                    out[own, group, :, 192 * which : 192 * which + 192] = full.reshape(192, 192)
        return out.astype(BF)

    by_degree = np.transpose
    return dict(
        fourier_t=split_table(fourier.T),
        fourier=split_table(fourier),
        inverse_t=split_table(inverse.T),
        inverse=split_table(inverse),
        analyse=blocks(by_degree(analysis, (1, 0, 2))),
        synthesize=blocks(synthesis),
        analyse_back=blocks(analysis),
        synthesize_back=blocks(by_degree(synthesis, (1, 0, 2))),
    )


def rows_out(flat_ref, start, offset, step, wide, tiles, tail, put, count, unroll=4):
    lane = lax.broadcasted_iota(jnp.int32, (8, 128), 1)

    def one(t, carry):
        shift = offset + step * t
        jump = shift // 128
        shift = shift - 128 * jump
        amount = (128 - shift) % 128
        low = lane + shift < 128
        pieces = [
            pltpu.roll(flat_ref[pl.ds(start + wide * t + jump + m, 8, stride=641), :], amount, 1)
            for m in range(tiles + 1)
        ]
        for m in range(tiles):
            piece = jnp.where(low, pieces[m], pieces[m + 1])
            if m == tiles - 1:
                piece = jnp.where(lane < tail, piece, 0.0)
            put(m, t, piece)
        return carry

    lax.fori_loop(0, count, one, 0, unroll=unroll)


def rows_in(flat_ref, start, offset, step, wide, tiles, get, count, unroll=2):
    lane = lax.broadcasted_iota(jnp.int32, (8, 128), 1)

    def one(t, carry):
        shift = offset + step * t
        jump = shift // 128
        shift = shift - 128 * jump
        high = lane >= shift
        pieces = [pltpu.roll(get(m, t), shift, 1) for m in range(tiles)]
        last = tiles + (1 if step > 1 else 0)
        for m in range(last):
            here = pieces[m] if m < tiles else jnp.zeros((8, 128), F32)
            before = pieces[m - 1] if m > 0 else jnp.zeros((8, 128), F32)
            piece = jnp.where(high, here, before)
            where = pl.ds(start + wide * t + jump + m, 8, stride=641)
            if m == 0 or m >= tiles - 1:
                flat_ref[where, :] = flat_ref[where, :] + piece
            else:
                flat_ref[where, :] = piece
        return carry

    lax.fori_loop(0, count, one, 0, unroll=unroll)


def shard_place(shard, length):
    first = (shard * length) // D
    base = (first // 16) * 16
    start = D * base - length * shard + 128 * 88
    return base, start // 128, start % 128


def window_kernel(length, shard_ref, flat_ref, main_ref, side_ref, flat, tiles, extra):
    chunks = length // 128
    base, start, offset = shard_place(shard_ref[0], length)
    flat[0:88, :] = jnp.zeros((88, 128), F32)
    flat[88 + chunks :, :] = jnp.zeros((flat.shape[0] - 88 - chunks, 128), F32)

    def load(i, carry):
        piece = flat_ref[:, pl.ds(pl.multiple_of(1024 * i, 1024), 1024)]
        flat[pl.ds(pl.multiple_of(88 + 8 * i, 8), 8), :] = piece.astype(F32).reshape(8, 128)
        return carry

    lax.fori_loop(0, chunks // 8, load, 0, unroll=7)
    rest = chunks % 8
    if rest:
        piece = flat_ref[:, 128 * (chunks - rest) :].astype(F32).reshape(rest, 128)
        flat[88 + chunks - rest : 88 + chunks, :] = piece
    lane = lax.broadcasted_iota(jnp.int32, (8, 128), 1)
    extra[...] = jnp.zeros_like(extra)

    def put(m, t, piece):
        if m < 5:
            tiles[m, pl.ds(t, 8, stride=128), :] = piece
        else:
            extra[...] = jnp.where(lane == t, piece[:, 0:1], extra[...])

    rows_out(flat, start, offset, 1, 5, 6, 1, put, 128)
    side_ref[48:64, :] = jnp.zeros((16, 640), BF)
    side_ref[48:64, 0:128] = jnp.concatenate([extra[...], jnp.zeros((8, 128), F32)], axis=0).astype(BF)
    for m in range(5):
        at = slice(128 * m, 128 * m + 128)
        main_ref[:, at] = tiles[m, 16 : 16 + MAIN, :].astype(BF)
        side_ref[0:16, at] = tiles[m, 0:16, :].astype(BF)
        side_ref[16:48, at] = tiles[m, 16 + MAIN : WIN, :].astype(BF)


def spectral_window(shard, flat):
    length = flat.shape[1]
    return pl.pallas_call(
        partial(window_kernel, length),
        out_shape=(jax.ShapeDtypeStruct((MAIN, 640), BF), jax.ShapeDtypeStruct((64, 640), BF)),
        in_specs=[pl.BlockSpec(memory_space=pltpu.SMEM), vspec()],
        out_specs=(vspec(), vspec()),
        scratch_shapes=[
            pltpu.VMEM((5256, 128), F32),
            pltpu.VMEM((5, 1024, 128), F32),
            pltpu.VMEM((8, 128), F32),
        ],
        cost_estimate=LIGHT,
        compiler_params=params(),
    )(shard, flat)


VECTORS = ((0, D), (D, D), (2 * D, D), (3 * D, D), (4 * D, HID), (4 * D + HID, D))
IN_AT = 5 * D + HID
OUT_AT = IN_AT + D * HID


def mlp_kernel(flat_ref, in_ref, out_ref, vec_ref, flat, tin, tout):
    count, rows, _ = flat_ref.shape
    for k in range(count):
        flat[rows * k : rows * k + rows, :] = flat_ref[k].astype(F32)
    lane = lax.broadcasted_iota(jnp.int32, (1, 128), 1)
    vec_ref[...] = jnp.zeros_like(vec_ref)
    for row, (place, length) in enumerate(VECTORS):
        first, shift = place // 128, place % 128
        for m in range(-(-length // 128)):
            one = flat[first + m : first + m + 1, :]
            two = flat[first + m + 1 : first + m + 2, :]
            if shift:
                one = pltpu.roll(one, 128 - shift, 1)
                two = pltpu.roll(two, 128 - shift, 1)
            piece = jnp.where(lane + shift < 128, one, two)
            piece = jnp.where(lane + 128 * m < length, piece, 0.0)
            vec_ref[row : row + 1, 128 * m : 128 * m + 128] = piece
    for part in range(2):

        def put_in(m, t, piece, part=part):
            tin[m, pl.ds(t + 512 * part, 8, stride=64), :] = piece

        rows_out(flat, IN_AT // 128 + 641 * 8 * part, IN_AT % 128, 2, 10, 11, 2, put_in, 64, 2)

        def put_out(m, t, piece, part=part):
            tout[m, pl.ds(t + 1024 * part, 8, stride=128), :] = piece

        rows_out(flat, OUT_AT // 128 + 641 * 8 * part, OUT_AT % 128, 1, 5, 6, 1, put_out, 128, 4)
    keep = lax.broadcasted_iota(jnp.int32, (DP, 128), 0) < D
    for m in range(11):
        in_ref[:, 128 * m : 128 * m + 128] = jnp.where(keep, tin[m, :DP, :], 0.0).astype(BF)
    keep = lax.broadcasted_iota(jnp.int32, (HP, 128), 0) < HID
    for m in range(6):
        out_ref[:, 128 * m : 128 * m + 128] = jnp.where(keep, tout[m, :HP, :], 0.0).astype(BF)


def mlp_weights(flat):
    return pl.pallas_call(
        mlp_kernel,
        out_shape=(
            jax.ShapeDtypeStruct((DP, HP), BF),
            jax.ShapeDtypeStruct((HP, DP), BF),
            jax.ShapeDtypeStruct((8, HP), F32),
        ),
        in_specs=[vspec()],
        out_specs=(vspec(), vspec(), vspec()),
        scratch_shapes=[
            pltpu.VMEM((16776, 128), F32),
            pltpu.VMEM((11, 1024, 128), F32),
            pltpu.VMEM((6, 2048, 128), F32),
        ],
        cost_estimate=LIGHT,
        compiler_params=params(),
    )(flat)


ALL_ROWS = 15584
CHIPS = 8


def cuts(length, count):
    return [((s * length) // D) // 16 * 16 for s in range(count)] + [ALL_ROWS]


def gather_kernel(length, main_ref, side_ref, w_ref, column_ref, sides, edges, line, ring, over, arrive, local):
    dp = lax.axis_index("dp")
    lat = lax.axis_index("lat")
    core = dp % 2
    chip = dp // 2
    z = chip // 2
    x = chip % 2
    place = z + x * (7 - 2 * z)
    home = lat == core
    count = 2 * CHIPS

    def chip_at(p):
        p = (p + CHIPS) % CHIPS
        back = p // 4
        return ((1 - back) * p + back * (7 - p)) * 2 + back

    def device(p, which):
        return (chip_at(p) * 2 + which, lat)

    def shard(p, which):
        return chip_at(p) * 2 + which

    across = (dp, 1 - lat)
    partner = (dp + 1 - 2 * core, lat)
    barrier = pltpu.get_barrier_semaphore()
    for who in (device(place + 1, core), device(place - 1, core), across, partner):
        pl.semaphore_signal(barrier, inc=1, device_id=who, device_id_type=pl.DeviceIdType.MESH)
    pl.semaphore_wait(barrier, 4)

    def rows_of(s, first, size):
        start = ((s * length) // D) // 16 * 16 + 16 + first
        return w_ref.at[pl.ds(pl.multiple_of(start, 16), size)]

    def remote(src, dst, send, recv, who):
        return pltpu.make_async_remote_copy(
            src_ref=src, dst_ref=dst, send_sem=send, recv_sem=recv, device_id=who,
            device_id_type=pl.DeviceIdType.MESH,
        )

    first = core
    second = 1 - core
    hops = {1: [(0, 0), (0, 1), (1, 0), (1, 1), (2, 0), (2, 1), (3, 0)],
            -1: [(0, 0), (0, 1), (1, 0), (1, 1), (2, 0), (2, 1), (3, 1)]}
    coming = [(way, d, w) for d in (1, 2, 3) for w in (0, 1) for way in (1, -1)] + [(1, 4, 0), (-1, 4, 1)]

    def named(way, d, w):
        which = first if w == 0 else second
        return shard(place - way * d, which)

    def wait_part(kind, s, size):
        remote(rows_of(s, 0, size), rows_of(s, 0, size), local.at[0], arrive.at[kind, s], across).wait_recv()

    def wait_side(s):
        remote(sides.at[s], sides.at[s], local.at[0], arrive.at[2, s], across).wait_recv()

    own = dp

    @pl.when(home)
    def _():
        keep = pltpu.make_async_copy(main_ref, rows_of(own, 0, MAIN), local.at[0])
        keep.start()
        keep_side = pltpu.make_async_copy(side_ref, sides.at[own], local.at[1])
        keep_side.start()
        sent = []

        def send(way, hop, s, main, side):
            to = device(place + way, core)
            lane = 0 if way == 1 else 1
            copies = (
                remote(main, rows_of(s, 0, MAIN), ring.at[lane, hop], arrive.at[0, s], to),
                remote(side, sides.at[s], ring.at[lane + 2, hop], arrive.at[2, s], to),
            )
            for copy in copies:
                copy.start()
                sent.append(copy)

        def cross(index, s, main, side):
            copies = [remote(main(0, HEAD), rows_of(s, 0, HEAD), over.at[0, index], arrive.at[1, s], across)]
            copies.append(remote(side, sides.at[s], over.at[1, index], arrive.at[2, s], across))
            if index < 2:
                copies.insert(
                    0,
                    remote(
                        main(HEAD, MAIN - HEAD), rows_of(s, HEAD, MAIN - HEAD), over.at[2, index],
                        arrive.at[0, s], across,
                    ),
                )
            for copy in copies:
                copy.start()
                sent.append(copy)

        send(1, 0, own, main_ref, side_ref)
        send(-1, 0, own, main_ref, side_ref)
        cross(0, own, lambda at, size: main_ref.at[pl.ds(at, size)], side_ref)
        mate = dp + 1 - 2 * core
        wait_part(0, mate, MAIN)
        wait_side(mate)
        held = lambda s: (lambda at, size: rows_of(s, at, size))
        send(1, 1, mate, rows_of(mate, 0, MAIN), sides.at[mate])
        send(-1, 1, mate, rows_of(mate, 0, MAIN), sides.at[mate])
        cross(1, mate, held(mate), sides.at[mate])
        for index, (way, d, w) in enumerate(coming):
            s = named(way, d, w)
            wait_part(0, s, MAIN)
            wait_side(s)
            if (d, w) in hops[way]:
                send(way, hops[way].index((d, w)), s, rows_of(s, 0, MAIN), sides.at[s])
            cross(2 + index, s, held(s), sides.at[s])
        for copy in sent:
            copy.wait_send()
        keep.wait()
        keep_side.wait()

    @pl.when(jnp.logical_not(home))
    def _():
        sent = [
            remote(main_ref, rows_of(own, 0, MAIN), ring.at[4, 0], arrive.at[0, own], partner),
            remote(side_ref, sides.at[own], ring.at[4, 1], arrive.at[2, own], partner),
        ]
        for copy in sent:
            copy.start()
        size = MAIN - HEAD

        def send(way, hop, s):
            lane = 0 if way == 1 else 1
            copy = remote(
                rows_of(s, HEAD, size), rows_of(s, HEAD, size), ring.at[lane, hop], arrive.at[0, s],
                device(place + way, core),
            )
            copy.start()
            sent.append(copy)

        mate = dp + 1 - 2 * core
        wait_part(0, own, size)
        send(1, 0, own)
        send(-1, 0, own)
        wait_part(0, mate, size)
        send(1, 1, mate)
        send(-1, 1, mate)
        for way, d, w in coming:
            s = named(way, d, w)
            wait_part(0, s, size)
            if (d, w) in hops[way]:
                send(way, hops[way].index((d, w)), s)
        for s in [own, mate] + [named(*one) for one in coming]:
            wait_part(1, s, HEAD)
            wait_side(s)
        for copy in sent:
            copy.wait_send()

    places = cuts(length, count)
    copies = []
    for s in range(count):
        span = places[s + 1] - places[s]
        edge = sides[s, 0:16, :]
        if s:
            before = places[s] - places[s - 1] - 16 - MAIN
            edge = edge + sides[s - 1, 16 + before : 32 + before, :]
        edges[s] = edge
        copies.append(pltpu.make_async_copy(edges.at[s], w_ref.at[pl.ds(places[s], 16)], local.at[2 + s]))
        left = span - 16 - MAIN
        if left:
            copies.append(
                pltpu.make_async_copy(
                    sides.at[s, pl.ds(16, left)], w_ref.at[pl.ds(places[s] + 16 + MAIN, left)],
                    local.at[2 + count + s],
                )
            )
    for copy in copies:
        copy.start()
    lane = lax.broadcasted_iota(jnp.int32, (8, 128), 1)
    line[...] = jnp.zeros_like(line)
    for s in range(count):
        a, b = places[s] // 128, places[s] % 128
        piece = sides[s, 48:64, 0:128].astype(F32)[:8]
        if b:
            piece = pltpu.roll(piece, b, 1)
        line[a : a + 8, :] += jnp.where(lane >= b, piece, 0.0)
        line[a + 1 : a + 9, :] += jnp.where(lane < b, piece, 0.0)
    lane = lax.broadcasted_iota(jnp.int32, (1, 128), 1)
    for degree in range(DEGS):
        a, b = CIN * degree // 128, CIN * degree % 128
        piece = line[a : a + 8, :]
        if b:
            piece = pltpu.roll(piece, 128 - b, 1)
        for m in range(6):
            one = jnp.where(lane + b < 128, piece[m : m + 1], piece[m + 1 : m + 2])
            one = jnp.where(lane + 128 * m < CIN, one, 0.0)
            column_ref[degree : degree + 1, 128 * m : 128 * m + 128] = one
    for copy in copies:
        copy.wait()


def gather_rows(length, main, side):
    count = 2 * CHIPS
    return pl.pallas_call(
        partial(gather_kernel, length),
        out_shape=(jax.ShapeDtypeStruct((ALL_ROWS, 640), BF), jax.ShapeDtypeStruct((DEGS, DP), F32)),
        in_specs=[vspec(), vspec()],
        out_specs=(pl.BlockSpec(memory_space=pl.ANY), vspec()),
        scratch_shapes=[
            pltpu.VMEM((count, 64, 640), BF),
            pltpu.VMEM((count, 16, 640), BF),
            pltpu.VMEM((136, 128), F32),
            pltpu.SemaphoreType.DMA((5, 7)),
            pltpu.SemaphoreType.DMA((3, count)),
            pltpu.SemaphoreType.DMA((3, count)),
            pltpu.SemaphoreType.DMA((2 + 2 * count,)),
        ],
        cost_estimate=LIGHT,
        compiler_params=params(30, collective_id=0, has_side_effects=True),
    )(main, side)


def lane_mask():
    return (lax.broadcasted_iota(jnp.int32, (1, DP), 1) < D).astype(F32)


def unit_of(values, mask):
    mean = jnp.sum(values, axis=-1, keepdims=True) * (1.0 / D)
    centred = (values - mean) * mask
    square = jnp.sum(centred * centred, axis=-1, keepdims=True) * (1.0 / D)
    scale = lax.rsqrt(square + 1e-06)
    return centred * scale, scale


def norm_back(upstream, unit, scale, gain):
    scaled = upstream * gain
    mean_one = jnp.sum(scaled, axis=-1, keepdims=True) * (1.0 / D)
    mean_two = jnp.sum(scaled * unit, axis=-1, keepdims=True) * (1.0 / D)
    return scale * (scaled - mean_one * lane_mask() - unit * mean_two)


def modes_kernel(state_ref, noise_ref, vec_ref, table_ref, out_ref):
    unit, scale = unit_of(state_ref[...].astype(F32), lane_mask())
    normed = unit * vec_ref[0:1, :DP] + vec_ref[1:2, :DP]
    joined = jnp.concatenate(
        [normed[:, :640], normed[:, 640:] + noise_ref[...].astype(F32)], axis=1
    )
    for j in range(BLK):
        piece = joined[NLON * j : NLON * j + NLON, :]
        out_ref[j] = split_dot(table_ref[...], piece).astype(BF).reshape(GROUPS, GK, DP)


def modes(state, noise, vectors, table):
    return pl.pallas_call(
        modes_kernel,
        grid=(ROWS // BLK,),
        out_shape=jax.ShapeDtypeStruct((ROWS, GROUPS, GK, DP), BF),
        in_specs=[
            pl.BlockSpec((BC, DP), lambda i: (i, 0)),
            pl.BlockSpec((BC, 128), lambda i: (i, 0)),
            pl.BlockSpec((8, HP), lambda i: (0, 0)),
            pl.BlockSpec((KP, 3 * NLON), lambda i: (0, 0)),
        ],
        out_specs=pl.BlockSpec((BLK, GROUPS, GK, DP), lambda i: (i, 0, 0, 0)),
        cost_estimate=LIGHT,
        compiler_params=params(),
    )(state, noise, vectors, table)


class Swap:
    def __init__(self, own_ref, other, table_ref, table, send, recv, sem):
        dp = lax.axis_index("dp")
        core = dp % 2
        self.partner = (dp + 1 - 2 * core, lax.axis_index("lat"))
        self.table = pltpu.make_async_copy(table_ref.at[core], table, sem)
        self.copies = [
            pltpu.make_async_remote_copy(
                src_ref=own_ref.at[:, group], dst_ref=other.at[:, group], send_sem=send.at[group],
                recv_sem=recv.at[group], device_id=self.partner, device_id_type=pl.DeviceIdType.MESH,
            )
            for group in range(GROUPS)
        ]

    def start(self):
        self.table.start()
        barrier = pltpu.get_barrier_semaphore()
        pl.semaphore_signal(barrier, inc=1, device_id=self.partner, device_id_type=pl.DeviceIdType.MESH)
        pl.semaphore_wait(barrier, 1)
        for copy in self.copies:
            copy.start()

    def finish(self):
        for copy in self.copies:
            copy.wait_send()


def swap_scratch():
    return [
        pltpu.VMEM((24, GROUPS, GK, DP), BF),
        pltpu.VMEM((GROUPS, 192, 384), BF),
        pltpu.SemaphoreType.DMA((GROUPS,)),
        pltpu.SemaphoreType.DMA((GROUPS,)),
        pltpu.SemaphoreType.DMA,
    ]


def legendre(own_ref, table_ref, out_ref, swap_refs):
    other, table, send, recv, sem = swap_refs
    swap = Swap(own_ref, other, table_ref, table, send, recv, sem)
    swap.start()
    swap.table.wait()
    for group in range(GROUPS):
        swap.copies[group].wait_recv()
        both = jnp.concatenate(
            [own_ref[:, group].reshape(192, DP), other[:, group].reshape(192, DP)], axis=0
        )
        total = dot(table[group], both)
        out_ref[:, group] = total.astype(out_ref.dtype).reshape(24, GK, DP)
    swap.finish()


def fetch(w_ref, w_buf, sem, degree):
    slot = degree % DEPTH
    first = pl.multiple_of((CIN * degree) // 16 * 16, 16)
    return pltpu.make_async_copy(w_ref.at[pl.ds(first, WROWS)], w_buf.at[slot], sem.at[slot])


def fetch_next(w_ref, w_buf, sem, degree):
    fetch(w_ref, w_buf, sem, degree).wait()


def fetch_ahead(w_ref, w_buf, sem, degree):
    @pl.when(degree + DEPTH < DEGS)
    def _():
        fetch(w_ref, w_buf, sem, degree + DEPTH).start()


C_TILES = 9
G_TILES = 11
OWNERS = 16


def owner_degrees(owner):
    first = 3 * (owner // 2)
    return first + 2 * (owner % 2), first + 1


def pack_tiles(block_ref, parts_ref, middle_tiles):
    lane = lax.broadcasted_iota(jnp.int32, (KP, 128), 1)
    for owner in range(OWNERS):
        own, middle = owner_degrees(owner)
        for m in range(5):
            at = slice(128 * m, 128 * m + 128)
            parts_ref[owner, m] = block_ref[own, :, :, at].reshape(KP, 128)
        for n, m in enumerate(middle_tiles[owner % 2]):
            at = slice(128 * m, 128 * m + 128)
            parts_ref[owner, 5 + n] = block_ref[middle, :, :, at].reshape(KP, 128)
        one = block_ref[own, :, :, 640:].reshape(KP, 128).astype(F32)
        two = block_ref[middle, :, :, 640:].reshape(KP, 128).astype(F32)
        two = pltpu.roll(two, 16, 1)
        last = parts_ref.shape[1] - 1
        parts_ref[owner, last] = jnp.where(lane < 16, one, two).astype(BF)


def mix_kernel(own_ref, table_ref, column_ref, w_ref, parts_ref, mixed_ref, coeff_ref, w_buf, sem, *swap_refs):
    for degree in range(DEPTH):
        fetch(w_ref, w_buf, sem, degree).start()
    legendre(own_ref, table_ref, coeff_ref, swap_refs)
    pack_tiles(coeff_ref, parts_ref, ((0, 1, 2), (2, 3, 4)))
    lane = lax.broadcasted_iota(jnp.int32, (KP, 128), 1)

    def one(degree, carry):
        fetch_next(w_ref, w_buf, sem, degree)
        coeffs = coeff_ref[degree].reshape(KP, DP).astype(F32)
        moved = pltpu.roll(coeffs, (CIN * degree) % 16, 1)
        mixed = dot(moved[:, :WROWS].astype(BF), w_buf[degree % DEPTH])
        last = jnp.sum(coeffs * column_ref[pl.ds(degree, 1), :], axis=1, keepdims=True)
        mixed = jnp.concatenate([mixed, jnp.where(lane < 1, last, 0.0)], axis=1)
        mixed_ref[degree] = mixed.astype(BF).reshape(GROUPS, GK, DP)
        fetch_ahead(w_ref, w_buf, sem, degree)
        return carry

    lax.fori_loop(0, DEGS, one, 0)


def mix_back_kernel(
    own_ref, table_ref, column_ref, w_ref, parts_ref, out_ref, grad_ref, w_buf, wide, sem, *swap_refs
):
    for degree in range(DEPTH):
        fetch(w_ref, w_buf, sem, degree).start()
    legendre(own_ref, table_ref, grad_ref, swap_refs)
    every = (0, 1, 2, 3, 4)
    pack_tiles(grad_ref, parts_ref, (every, every))
    keep = lax.broadcasted_iota(jnp.int32, (KP, DP), 1) < CIN
    wide[...] = jnp.zeros_like(wide)

    def one(degree, carry):
        fetch_next(w_ref, w_buf, sem, degree)
        grad = grad_ref[degree].reshape(KP, DP)
        wide[:, :WROWS] = dot_nt(grad[:, :640], w_buf[degree % DEPTH])
        back = pltpu.roll(wide[...], DP - (CIN * degree) % 16, 1)
        last = grad[:, 640:].astype(F32)[:, 0:1]
        back = back + last * column_ref[pl.ds(degree, 1), :]
        out_ref[degree] = jnp.where(keep, back, 0.0).astype(BF).reshape(GROUPS, GK, DP)
        fetch_ahead(w_ref, w_buf, sem, degree)
        return carry

    lax.fori_loop(0, DEGS, one, 0)


def anywhere():
    return pl.BlockSpec(memory_space=pl.ANY)


def mix(own, table, weights, column, back):
    tiles = G_TILES if back else C_TILES
    scratch = [pltpu.VMEM((24, GROUPS, GK, DP), BF), pltpu.VMEM((DEPTH, WROWS, 640), BF)]
    if back:
        scratch.append(pltpu.VMEM((KP, DP), F32))
    scratch.append(pltpu.SemaphoreType.DMA((DEPTH,)))
    return pl.pallas_call(
        mix_back_kernel if back else mix_kernel,
        in_specs=[vspec(), anywhere(), vspec(), anywhere()],
        out_specs=(vspec(), vspec()),
        scratch_shapes=scratch + swap_scratch(),
        out_shape=(
            jax.ShapeDtypeStruct((OWNERS, tiles, KP, 128), BF),
            jax.ShapeDtypeStruct((24, GROUPS, GK, DP), BF),
        ),
        cost_estimate=LIGHT,
        compiler_params=params(collective_id=2 if back else 1, has_side_effects=True),
    )(own, table, column, weights)


HID_PARTS = ((0, 256), (256, 256), (512, 256), (768, 256), (1024, 256), (1280, 128))


def feed_kernel(
    mask_ref, own_ref, table_ref, inverse_ref, state_ref, vec_ref, in_ref, out_ref,
    next_ref, middle_ref, hidden_ref, active_ref, slope_ref, lat, *swap_refs
):
    i = pl.program_id(0)

    @pl.when(i == 0)
    def _():
        legendre(own_ref, table_ref, lat, swap_refs)

    mask = mask_ref[0:1, 0:1]
    parts = [split_dot(inverse_ref[...], lat[BLK * i + j].reshape(KP, DP)) for j in range(BLK)]
    middle = state_ref[...].astype(F32) + mask * jnp.concatenate(parts, axis=0)
    middle_ref[...] = middle
    unit, scale = unit_of(middle, lane_mask())
    hidden = (unit * vec_ref[2:3, :DP] + vec_ref[3:4, :DP]).astype(BF)
    hidden_ref[...] = hidden
    for first, width in HID_PARTS:
        at = slice(first, first + width)
        pre = dot(hidden, in_ref[:, at]) + vec_ref[4:5, at]
        bell = 0.5 * (1.0 + lax.erf(pre * (1.0 / math.sqrt(2.0))))
        active_ref[:, at] = (pre * bell).astype(BF)
        slope = bell + pre * (jnp.exp(-0.5 * pre * pre) * (1.0 / math.sqrt(2.0 * math.pi)))
        slope_ref[:, at] = slope.astype(BF)
    result = dot(active_ref[...], out_ref[...]) + vec_ref[5:6, :DP]
    next_ref[...] = (middle + mask * result).astype(next_ref.dtype)


def cell_spec(width):
    return pl.BlockSpec((BC, width), lambda i, *h: (i, 0))


def fixed(*shape):
    return pl.BlockSpec(shape, lambda i, *h: (0,) * len(shape))


def feed(mask, own, table, inverse_t, state, vectors, w_in, w_out, last):
    cells = lambda width, kind: jax.ShapeDtypeStruct((CELLS, width), kind)
    return pl.pallas_call(
        feed_kernel,
        grid=(ROWS // BLK,),
        in_specs=[
            fixed(1, 128), fixed(24, GROUPS, GK, DP), anywhere(), fixed(NLON, 3 * KP), cell_spec(DP),
            fixed(8, HP), fixed(DP, HP), fixed(HP, DP),
        ],
        out_specs=(cell_spec(DP), cell_spec(DP), cell_spec(DP), cell_spec(HP), cell_spec(HP)),
        scratch_shapes=[pltpu.VMEM((24, GROUPS, GK, DP), F32)] + swap_scratch(),
        out_shape=(
            cells(DP, BF if last else F32), cells(DP, F32), cells(DP, BF), cells(HP, BF), cells(HP, BF),
        ),
        cost_estimate=LIGHT,
        compiler_params=params(collective_id=4 if last else 3, has_side_effects=True),
    )(mask, own, table, inverse_t, state, vectors, w_in, w_out)


def feed_back_kernel(
    mask_ref, grad_ref, slope_ref, middle_ref, vec_ref, in_ref, out_ref, inverse_ref,
    result_ref, pre_ref, gm_ref, modes_ref, sums_ref,
):
    i = pl.program_id(0)

    @pl.when(i == 0)
    def _():
        sums_ref[...] = jnp.zeros_like(sums_ref)

    mask = mask_ref[0:1, 0:1]
    grad = grad_ref[...].astype(F32)
    result = (mask * grad).astype(BF)
    result_ref[...] = result
    sums_ref[5:6, :DP] += jnp.sum(result.astype(F32), axis=0, keepdims=True)
    for first, width in HID_PARTS:
        at = slice(first, first + width)
        active = dot_nt(result, out_ref[at, :])
        pre = (active * slope_ref[:, at].astype(F32)).astype(BF)
        pre_ref[:, at] = pre
        sums_ref[4:5, at] += jnp.sum(pre.astype(F32), axis=0, keepdims=True)
    upstream = dot_nt(pre_ref[...], in_ref[...])
    unit, scale = unit_of(middle_ref[...], lane_mask())
    sums_ref[2:3, :DP] += jnp.sum(upstream * unit, axis=0, keepdims=True)
    sums_ref[3:4, :DP] += jnp.sum(upstream, axis=0, keepdims=True)
    total = grad + norm_back(upstream, unit, scale, vec_ref[2:3, :DP])
    gm_ref[...] = total
    total = mask * total
    for j in range(BLK):
        piece = total[NLON * j : NLON * j + NLON, :]
        modes_ref[j] = split_dot(inverse_ref[...], piece).astype(BF).reshape(GROUPS, GK, DP)


def feed_back(mask, grad, slope, middle, vectors, w_in, w_out, inverse):
    cells = lambda width, kind: jax.ShapeDtypeStruct((CELLS, width), kind)
    return pl.pallas_call(
        feed_back_kernel,
        grid=(ROWS // BLK,),
        in_specs=[
            fixed(1, 128), cell_spec(DP), cell_spec(HP), cell_spec(DP), fixed(8, HP), fixed(DP, HP),
            fixed(HP, DP), fixed(KP, 3 * NLON),
        ],
        out_specs=(
            cell_spec(DP), cell_spec(HP), cell_spec(DP),
            pl.BlockSpec((BLK, GROUPS, GK, DP), lambda i: (i, 0, 0, 0)), fixed(8, HP),
        ),
        out_shape=(
            cells(DP, BF), cells(HP, BF), cells(DP, F32), jax.ShapeDtypeStruct((ROWS, GROUPS, GK, DP), BF),
            jax.ShapeDtypeStruct((8, HP), F32),
        ),
        cost_estimate=LIGHT,
        compiler_params=params(),
    )(mask, grad, slope, middle, vectors, w_in, w_out, inverse)


def first_back_kernel(
    own_ref, table_ref, fourier_ref, state_ref, gm_ref, vec_ref, out_ref, sums_ref, lat, *swap_refs
):
    i = pl.program_id(0)

    @pl.when(i == 0)
    def _():
        legendre(own_ref, table_ref, lat, swap_refs)
        sums_ref[...] = jnp.zeros_like(sums_ref)

    parts = [split_dot(fourier_ref[...], lat[BLK * i + j].reshape(KP, DP)) for j in range(BLK)]
    upstream = jnp.concatenate(parts, axis=0)
    unit, scale = unit_of(state_ref[...].astype(F32), lane_mask())
    sums_ref[0:1, :] += jnp.sum(upstream * unit, axis=0, keepdims=True)
    sums_ref[1:2, :] += jnp.sum(upstream, axis=0, keepdims=True)
    total = gm_ref[...] + norm_back(upstream, unit, scale, vec_ref[0:1, :DP])
    out_ref[...] = total.astype(out_ref.dtype)


def first_back(own, table, fourier, state, gm, vectors, last):
    return pl.pallas_call(
        first_back_kernel,
        grid=(ROWS // BLK,),
        in_specs=[
            fixed(24, GROUPS, GK, DP), anywhere(), fixed(NLON, 3 * KP), cell_spec(DP), cell_spec(DP),
            fixed(8, HP),
        ],
        out_specs=(cell_spec(DP), fixed(8, DP)),
        scratch_shapes=[pltpu.VMEM((24, GROUPS, GK, DP), F32)] + swap_scratch(),
        out_shape=(
            jax.ShapeDtypeStruct((CELLS, DP), BF if last else F32), jax.ShapeDtypeStruct((8, DP), F32),
        ),
        cost_estimate=LIGHT,
        compiler_params=params(collective_id=6 if last else 5, has_side_effects=True),
    )(own, table, fourier, state, gm, vectors)


def mlp_grad_kernel(h0, h1, p0, p1, a0, a1, r0, r1, tin, tout, turned):
    for step, ref in enumerate((h0, h1)):
        turned[:, CELLS * step : CELLS * step + CELLS] = ref[...].T
    for first, width in HID_PARTS:
        at = slice(first, first + width)
        part = dot(turned[:, :CELLS], p0[:, at]) + dot(turned[:, CELLS:], p1[:, at])
        for m in range(width // 128):
            tin[first // 128 + m] = part[:, 128 * m : 128 * m + 128]
        part = dot_tn(a0[:, at], r0[...]) + dot_tn(a1[:, at], r1[...])
        for m in range(6):
            tout[m, at, :] = part[:, 128 * m : 128 * m + 128]


def mlp_flat_kernel(gin, gout, feed_sums, first_sums, pack_ref, tin, tout, flat_ref):
    tin[:, :DP, :] = gin[...]
    tout[:, :HP, :] = gout[...]
    tin[:, DP:, :] = jnp.zeros((11, 1024 - DP, 128), F32)
    tout[:, HP:, :] = jnp.zeros((6, 2048 - HP, 128), F32)
    flat_ref[...] = jnp.zeros_like(flat_ref)
    lane = lax.broadcasted_iota(jnp.int32, (1, 128), 1)
    sums = feed_sums[...]
    for row, (place, length) in enumerate(VECTORS):
        first, shift = place // 128, place % 128
        for m in range(-(-length // 128)):
            at = slice(128 * m, 128 * m + 128)
            piece = first_sums[row : row + 1, at] if row < 2 else sums[row : row + 1, at]
            piece = jnp.where(lane + 128 * m < length, piece, 0.0)
            if shift:
                piece = pltpu.roll(piece, shift, 1)
            flat_ref[first + m : first + m + 1, :] += jnp.where(lane >= shift, piece, 0.0)
            flat_ref[first + m + 1 : first + m + 2, :] += jnp.where(lane < shift, piece, 0.0)
    for part in range(2):

        def get_in(m, t, part=part):
            return tin[m, pl.ds(t + 512 * part, 8, stride=64), :]

        rows_in(flat_ref, IN_AT // 128 + 641 * 8 * part, IN_AT % 128, 2, 10, 11, get_in, 64, 1)

    for part in range(2):

        def get_out(m, t, part=part):
            return tout[m, pl.ds(t + 1024 * part, 8, stride=128), :]

        rows_in(flat_ref, OUT_AT // 128 + 641 * 8 * part, OUT_AT % 128, 1, 5, 6, get_out, 128, 2)
    for k in range(32):
        piece = flat_ref[SHARD_ROWS * k : SHARD_ROWS * k + SHARD_ROWS, :]
        piece = jnp.concatenate([piece, jnp.zeros((416 - SHARD_ROWS, 128), F32)], axis=0)
        pack_ref[(k // 2) % 2, (k // 4) * 2 + k % 2] = piece.astype(BF)


FLAT_ROWS = 16784
SHARD_ROWS = 403


def mlp_grads(hidden, pre, active, result, feed_sums, first_sums):
    gin, gout = pl.pallas_call(
        mlp_grad_kernel,
        out_shape=(jax.ShapeDtypeStruct((11, DP, 128), F32), jax.ShapeDtypeStruct((6, HP, 128), F32)),
        in_specs=[vspec()] * 8,
        out_specs=(vspec(), vspec()),
        scratch_shapes=[pltpu.VMEM((DP, 2 * CELLS), BF)],
        cost_estimate=LIGHT,
        compiler_params=params(62),
    )(*hidden, *pre, *active, *result)
    return pl.pallas_call(
        mlp_flat_kernel,
        out_shape=jax.ShapeDtypeStruct((2, 16, 416, 128), BF),
        in_specs=[vspec()] * 4,
        out_specs=vspec(),
        scratch_shapes=[
            pltpu.VMEM((11, 1024, 128), F32),
            pltpu.VMEM((6, 2048, 128), F32),
            pltpu.VMEM((FLAT_ROWS, 128), F32),
        ],
        cost_estimate=LIGHT,
        compiler_params=params(62),
    )(gin, gout, feed_sums, first_sums)


def spectral_grad_kernel(odd_ref, c0, c1, g0, g1, out_ref, head_ref, tiles_ref):
    rows = OWNERS * KP
    lane = lax.broadcasted_iota(jnp.int32, (DP, 128), 1)
    tiles_ref[:, 0:16, :] = jnp.zeros((6, 16, 128), F32)
    tiles_ref[:, 16 + 2 * CIN :, :] = jnp.zeros((6, TROWS - 16 - 2 * CIN, 128), F32)

    def side(ref, first, count):
        take = [ref[:, m].reshape(rows, 128) for m in list(range(first, first + count)) + [ref.shape[1] - 1]]
        return jnp.concatenate(take, axis=1)

    def product(c_first, c_count, g_first):
        total = dot_tn(side(c0, c_first, c_count), side(g0, g_first, 5))
        return total + dot_tn(side(c1, c_first, c_count), side(g1, g_first, 5))

    def save(start, part, first, count, column):
        for m in range(6):
            piece = part[first : first + count, 128 * m : 128 * m + 128]
            if m == 5:
                if column:
                    piece = pltpu.roll(piece, 128 - column, 1)
                piece = jnp.where(lane[:count] < 1, piece, 0.0)
            tiles_ref[m, start : start + count, :] = piece

    own = product(0, 5, 0)
    head = jnp.concatenate([own[0:16, :640], jnp.where(lane[:16] < 1, own[0:16, 640:], 0.0)], axis=1)
    head_ref[...] = head.astype(BF)
    middle = product(5, 3, 5)

    @pl.when(odd_ref[0] == 0)
    def _():
        save(16, own, 0, CIN, 0)
        save(16 + CIN, middle, 0, 384, 16)
        tiles_ref[:, 16 + CIN + 384 : 16 + 2 * CIN, :] = jnp.zeros((6, CIN - 384, 128), F32)

    @pl.when(odd_ref[0] == 1)
    def _():
        tiles_ref[:, 16 : 16 + 256, :] = jnp.zeros((6, 256, 128), F32)
        save(16 + 256, middle, 0, 384, 16)
        save(16 + 640, middle, 400, 9, 16)
        save(16 + CIN, own, 0, CIN, 0)

    out_ref[...] = tiles_ref[...].astype(BF)


def spectral_grads(odd, coeffs, grads):
    return pl.pallas_call(
        spectral_grad_kernel,
        out_shape=(jax.ShapeDtypeStruct((6, TROWS, 128), BF), jax.ShapeDtypeStruct((16, DP), BF)),
        in_specs=[pl.BlockSpec(memory_space=pltpu.SMEM)] + [vspec()] * 4,
        out_specs=(vspec(), vspec()),
        scratch_shapes=[pltpu.VMEM((6, TROWS, 128), F32)],
        cost_estimate=LIGHT,
        compiler_params=params(),
    )(odd, *coeffs, *grads)


def flatten_kernel(length, shard_ref, own_ref, moved_ref, next_ref, out_ref, tiles, flat):
    chunks = length // 128
    shard = shard_ref[0]
    base, start, offset = shard_place(shard, length)
    move = base - CIN * ((3 * shard) // 2) + 16

    @pl.when(shard_ref[1] == 1)
    def _():
        tiles[...] = own_ref[...].astype(F32)

    @pl.when(shard_ref[1] == 0)
    def _():
        tiles[...] = moved_ref[...].astype(F32)

    for m in range(6):
        piece = next_ref[:, 128 * m : 128 * m + 128].astype(F32)
        tiles[m, 16 + 2 * CIN : 24 + 2 * CIN, :] = piece[:8]
    flat[...] = jnp.zeros_like(flat)

    def get(m, t):
        return tiles[m, pl.ds(t + move, 8, stride=128), :]

    rows_in(flat, start, offset, 1, 5, 6, get, 128)

    def save(i, carry):
        piece = flat[pl.ds(pl.multiple_of(88 + 8 * i, 8), 8), :].reshape(1, 1024)
        out_ref[:, pl.ds(pl.multiple_of(1024 * i, 1024), 1024)] = piece
        return carry

    lax.fori_loop(0, chunks // 8, save, 0, unroll=7)
    rest = chunks % 8
    if rest:
        piece = flat[88 + chunks - rest : 88 + chunks, :].reshape(1, 128 * rest)
        out_ref[:, 128 * (chunks - rest) :] = piece


def flatten(shard, own, moved, after, length):
    return pl.pallas_call(
        partial(flatten_kernel, length),
        out_shape=jax.ShapeDtypeStruct((1, length), F32),
        in_specs=[pl.BlockSpec(memory_space=pltpu.SMEM), vspec(), vspec(), vspec()],
        out_specs=vspec(),
        scratch_shapes=[pltpu.VMEM((6, TROWS, 128), F32), pltpu.VMEM((5256, 128), F32)],
        cost_estimate=LIGHT,
        compiler_params=params(),
    )(shard, own, moved, after)


def wide(block):
    flat = block.reshape(CELLS, D)
    return jnp.pad(flat, ((0, 0), (0, DP - D)))


def shards_paired(fields, noise_fields, step_counts, spectral_flat, mlp_flat, cotangent):
    axes = ("dp", "lat")
    dp_count = lax.axis_size("dp")
    dp_index = lax.axis_index("dp")
    core = dp_index % 2
    lat_index = lax.axis_index("lat")
    length = spectral_flat.shape[1]
    places = [(d, y) for d in range(dp_count) for y in range(2)]
    number = lambda d, y: 2 * d + y
    mirror = [(number(d, y), number(d - d % 2 + y, d % 2)) for d, y in places]
    crossing = [pair for pair in mirror if pair[0] != pair[1]]
    other_core = [(number(d, y), number(d + 1 - 2 * (d % 2), y)) for d, y in places]
    same_core = [[number(d, y) for d, y in places if d % 2 == c] for c in range(2)]
    stays = core == lat_index

    def mirrored(block):
        moved = lax.ppermute(block, axes, crossing)
        return jnp.where(stays, block, moved)

    swapped = lambda a: lax.ppermute(a, axes, other_core)
    tables = {name: jnp.asarray(value) for name, value in plan_tables().items()}

    main, side = spectral_window(dp_index.astype(jnp.int32).reshape(1), spectral_flat)
    weights, column = gather_rows(length, main, side)
    mlp_whole = lax.all_gather(mlp_flat.reshape(-1, 128), axes, axis=0, tiled=False)
    moved = lax.ppermute(wide(cotangent), axes, crossing)
    mlp_whole, weights, moved = lax.optimization_barrier((mlp_whole, weights, moved))
    state = mirrored(wide(fields))
    noise = mirrored(noise_fields).reshape(STEPS, CELLS, NOISE)
    noise = jnp.pad(noise, ((0, 0), (0, 0), (1, 128 - 1 - NOISE)))
    counts = mirrored(step_counts)
    w_in, w_out, vectors = mlp_weights(mlp_whole)

    kept = []
    for step in range(STEPS):
        mask = jnp.broadcast_to((step < counts).astype(F32).reshape(1, 1), (1, 128))
        lon_modes = modes(state, noise[step], vectors, tables["fourier_t"])
        parts, mixed = mix(lon_modes, tables["analyse"], weights, column, False)
        following, middle, hidden, active, slope = feed(
            mask, mixed, tables["synthesize"], tables["inverse_t"], state, vectors, w_in, w_out,
            step == STEPS - 1,
        )
        kept.append((mask, state, parts, middle, hidden, active, slope))
        state = following
    output = mirrored(state)
    grad = jnp.where(stays, wide(cotangent), moved)

    def to_owners(parts):
        return lax.all_to_all(
            parts, axes, split_axis=0, concat_axis=0, tiled=True, axis_index_groups=same_core
        )

    received = []

    def to_owners_next(parts):
        if received:
            parts, received[-1] = lax.optimization_barrier((parts, received[-1]))
        received.append(to_owners(parts))

    for step in range(STEPS):
        to_owners_next(kept[step][2])
    results = [None] * STEPS
    pres = [None] * STEPS
    feed_sums = first_sums = 0.0
    for step in reversed(range(STEPS)):
        mask, state, parts, middle, hidden, active, slope = kept[step]
        results[step], pres[step], gm, grad_modes, sums = feed_back(
            mask, grad, slope, middle, vectors, w_in, w_out, tables["inverse"]
        )
        feed_sums = feed_sums + sums
        parts, grad_coeffs = mix(
            grad_modes, tables["synthesize_back"], weights, column, True
        )
        to_owners_next(parts)
        grad, sums = first_back(
            grad_coeffs, tables["analyse_back"], tables["fourier"], state, gm,
            vectors, step == 0,
        )
        first_sums = first_sums + sums
    fields_grad = mirrored(grad)
    mlp_pack = mlp_grads(
        [k[4] for k in kept], pres, [k[5] for k in kept], results, feed_sums, first_sums
    )
    own = lax.dynamic_index_in_dim(mlp_pack, core, 0, keepdims=False)
    give = lax.dynamic_index_in_dim(mlp_pack, 1 - core, 0, keepdims=False)
    pair = (own.astype(F32) + swapped(give).astype(F32)).astype(BF)
    pair = lax.all_to_all(
        pair, axes, split_axis=0, concat_axis=0, tiled=True, axis_index_groups=same_core
    )
    mlp_grad = jnp.sum(pair.astype(F32), axis=0)[: mlp_flat.shape[0] // 128].reshape(-1)

    odd = lat_index.astype(jnp.int32).reshape(1)
    tiles, head = spectral_grads(odd, received[:2], [received[3], received[2]])
    spot = lambda s, c: number(s - s % 2 + c, s % 2)
    earlier = [(spot(s, c), number(s - 1, c)) for s in range(2, dp_count, 2) for c in range(2)]
    after = lax.ppermute(head, axes, earlier)
    moved = lax.ppermute(tiles, axes, crossing)
    place = jnp.stack([dp_index.astype(jnp.int32), stays.astype(jnp.int32)])
    spectral_grad = flatten(place, tiles, moved, after, length)
    narrow = lambda a: a[:, :D].reshape(1, ROWS, NLON, D)
    return narrow(output), narrow(fields_grad), spectral_grad, mlp_grad


def solution(mesh):
    paired = mesh.shape["lat"] == 2 and mesh.shape["dp"] == 16
    return jax.shard_map(
        shards_paired if paired else shards_general,
        mesh=mesh,
        in_specs=(
            P("dp", "lat", None, None),
            P("dp", None, "lat", None),
            P("dp"),
            P("lat", "dp"),
            P(("dp", "lat")),
            P("dp", "lat", None, None),
        ),
        out_specs=(
            P("dp", "lat", None, None),
            P("dp", "lat", None, None),
            P("lat", "dp"),
            P(("dp", "lat")),
        ),
        check_vma=False,
    )
```

```python
from functools import partial
import math

import jax
import jax.numpy as jnp
import numpy as np
from jax import lax
from jax.experimental import pallas as pl
from jax.experimental.pallas import tpu as pltpu
from jax.sharding import PartitionSpec as P

D = 641
HID = 1282
NOISE = 8
NLAT = 48
NLON = 72
LDEG = 48
ORDERS = 36
STEPS = 2
CIN = D + NOISE

HIGHEST = lax.Precision.HIGHEST


def shortened(shard):
    return jax.tree.map(lambda a: a.astype(jnp.bfloat16) if a.dtype == jnp.float32 else a, shard)


def legendre_values(lat_total, degree_total, order_total):
    colatitude = np.pi * (np.arange(lat_total) + 0.5) / lat_total
    cosine = np.cos(colatitude)
    sine_part = np.sin(colatitude)
    legendre = np.zeros((lat_total, degree_total, order_total))
    diagonal = np.full(lat_total, 1.0 / math.sqrt(4.0 * math.pi))
    for column in range(order_total):
        if column > 0:
            diagonal = diagonal * math.sqrt((2.0 * column + 1.0) / (2.0 * column)) * sine_part
        legendre[:, column, column] = diagonal
        legendre[:, column + 1, column] = math.sqrt(2.0 * column + 3.0) * cosine * diagonal
        for degree in range(column + 2, degree_total):
            factor_one = math.sqrt(
                (4.0 * degree * degree - 1.0) / (degree * degree - column * column)
            )
            factor_two = math.sqrt(
                ((degree - 1.0) ** 2 - column * column) / (4.0 * (degree - 1.0) ** 2 - 1.0)
            )
            legendre[:, degree, column] = factor_one * (
                cosine * legendre[:, degree - 1, column]
                - factor_two * legendre[:, degree - 2, column]
            )
    return (colatitude, legendre)


def spectral_tables(lat_total, lon_total, degree_total, order_total):
    colatitude, legendre = legendre_values(lat_total, degree_total, order_total)
    quadrature = np.sin(colatitude) * np.pi / lat_total
    angles = 2.0 * np.pi * np.outer(np.arange(lon_total), np.arange(order_total)) / lon_total
    fourier = np.concatenate([np.cos(angles), -np.sin(angles)], axis=1) * (2.0 * np.pi / lon_total)
    weights = np.where(np.arange(order_total) == 0, 1.0, 2.0)
    inverse = np.concatenate(
        [np.cos(angles).T * weights[:, None], -np.sin(angles).T * weights[:, None]], axis=0
    )
    doubled = np.concatenate([legendre, legendre], axis=2)
    analysis = doubled * quadrature[:, None, None]
    return tuple(
        (np.asarray(member, np.float32) for member in (fourier, inverse, analysis, doubled))
    )


def normalize(values, scale_gain, shift_vec):
    centered = values - jnp.mean(values, axis=-1, keepdims=True)
    inverse_scale = lax.rsqrt(jnp.mean(centered * centered, axis=-1, keepdims=True) + 1e-06)
    unit = centered * inverse_scale
    return (unit * scale_gain + shift_vec, unit, inverse_scale)


def normalize_back(upstream, unit, inverse_scale, scale_gain):
    scaled = upstream * scale_gain
    mean_one = jnp.mean(scaled, axis=-1, keepdims=True)
    mean_two = jnp.mean(scaled * unit, axis=-1, keepdims=True)
    grad_input = inverse_scale * (scaled - mean_one - unit * mean_two)
    return (grad_input, jnp.sum(upstream * unit, axis=(0, 1, 2)), jnp.sum(upstream, axis=(0, 1, 2)))


def unpack_mlp(flat):
    pieces = []
    offset = 0
    for length in (D, D, D, D, HID, D):
        pieces.append(flat[offset : offset + length].astype(jnp.float32))
        offset = offset + length
    w_in = flat[offset : offset + D * HID].reshape(D, HID)
    offset = offset + D * HID
    w_out = flat[offset : offset + HID * D].reshape(HID, D)
    return (tuple(pieces), w_in, w_out)


def build_weights(spectral_whole, mlp_whole, degrees_here):
    count_all = degrees_here * (D + NOISE) * D
    spectral = spectral_whole[0, :count_all].reshape(degrees_here, D + NOISE, D)
    vectors, w_in, w_out = unpack_mlp(mlp_whole)
    return (spectral, vectors, w_in, w_out)


def forward_step(current, noise_step, step_mask, tables, weights):
    (
        fourier,
        inverse,
        analysis_here,
        synthesis_here,
        analysis_rows,
        synthesis_rows,
        analysis_degrees,
        synthesis_degrees,
    ) = tables
    spectral, vectors, w_in, w_out = weights
    gain_one, shift_one, gain_two, shift_two, bias_hidden, bias_out = vectors
    normed, unit_one, scale_one = normalize(current, gain_one, shift_one)
    joined = jnp.concatenate([normed, noise_step], axis=-1)
    grid_modes = jnp.einsum("bjnc,nk->bjkc", joined, fourier, precision=HIGHEST)
    by_order = lax.all_to_all(
        shortened(grid_modes), "lat", split_axis=2, concat_axis=1, tiled=True
    ).astype(grid_modes.dtype)
    coeffs = jnp.einsum("jlk,bjkc->blkc", analysis_here, by_order, precision=HIGHEST).astype(
        jnp.bfloat16
    )
    by_degree = lax.all_to_all(coeffs, "lat", split_axis=1, concat_axis=2, tiled=True)
    mixed_modes = jnp.einsum(
        "blkc,lcd->blkd", by_degree, spectral, preferred_element_type=jnp.float32
    ).astype(jnp.bfloat16)
    mixed_orders = lax.all_to_all(mixed_modes, "lat", split_axis=2, concat_axis=1, tiled=True)
    lat_modes = jnp.einsum(
        "jlk,blkd->bjkd", synthesis_here, mixed_orders.astype(jnp.float32), precision=HIGHEST
    )
    lat_rows = lax.all_to_all(
        shortened(lat_modes), "lat", split_axis=1, concat_axis=2, tiled=True
    ).astype(lat_modes.dtype)
    branch = jnp.einsum("bjkd,kn->bjnd", lat_rows, inverse, precision=HIGHEST)
    middle = current + step_mask * branch
    normed_two, unit_two, scale_two = normalize(middle, gain_two, shift_two)
    hidden_in = normed_two.astype(jnp.bfloat16)
    preactivation = (
        jnp.einsum("bjnd,dh->bjnh", hidden_in, w_in, preferred_element_type=jnp.float32)
        + bias_hidden
    )
    active = jax.nn.gelu(preactivation, approximate=False).astype(jnp.bfloat16)
    result = (
        jnp.einsum("bjnh,hd->bjnd", active, w_out, preferred_element_type=jnp.float32) + bias_out
    )
    kept_values = (
        unit_one,
        scale_one,
        by_degree,
        unit_two,
        scale_two,
        hidden_in,
        preactivation,
        active,
    )
    return (middle + step_mask * result, kept_values)


def backward_step(grad_state, step_mask, kept_values, tables, weights):
    (
        fourier,
        inverse,
        analysis_here,
        synthesis_here,
        analysis_rows,
        synthesis_rows,
        analysis_degrees,
        synthesis_degrees,
    ) = tables
    spectral, vectors, w_in, w_out = weights
    gain_one, shift_one, gain_two, shift_two, bias_hidden, bias_out = vectors
    unit_one, scale_one, by_degree, unit_two, scale_two, hidden_in, preactivation, active = (
        kept_values
    )
    grad_result = (step_mask * grad_state).astype(jnp.bfloat16)
    grad_bias_out = jnp.sum(grad_result.astype(jnp.float32), axis=(0, 1, 2))
    grad_w_out = jnp.einsum(
        "bjnh,bjnd->hd", active, grad_result, preferred_element_type=jnp.float32
    )
    grad_active = jnp.einsum(
        "bjnd,hd->bjnh", grad_result, w_out, preferred_element_type=jnp.float32
    )
    unused, gelu_back = jax.vjp(partial(jax.nn.gelu, approximate=False), preactivation)
    grad_preact = gelu_back(grad_active)[0].astype(jnp.bfloat16)
    grad_bias_hidden = jnp.sum(grad_preact.astype(jnp.float32), axis=(0, 1, 2))
    grad_w_in = jnp.einsum(
        "bjnd,bjnh->dh", hidden_in, grad_preact, preferred_element_type=jnp.float32
    )
    grad_hidden_in = jnp.einsum(
        "bjnh,dh->bjnd", grad_preact, w_in, preferred_element_type=jnp.float32
    )
    grad_norm_two, grad_gain_two, grad_shift_two = normalize_back(
        grad_hidden_in, unit_two, scale_two, gain_two
    )
    grad_middle = grad_state + grad_norm_two
    grad_branch = step_mask * grad_middle
    grad_rows = jnp.einsum("bjnd,kn->bjkd", grad_branch, inverse, precision=HIGHEST)
    grad_modes = lax.all_to_all(
        shortened(grad_rows), "lat", split_axis=2, concat_axis=1, tiled=True
    ).astype(grad_rows.dtype)
    grad_mixed = jnp.einsum("jlk,bjkd->blkd", synthesis_here, grad_modes, precision=HIGHEST).astype(
        jnp.bfloat16
    )
    grad_degree = lax.all_to_all(grad_mixed, "lat", split_axis=1, concat_axis=2, tiled=True)
    grad_spectral = jnp.einsum(
        "blkc,blkd->lcd", by_degree, grad_degree, preferred_element_type=jnp.float32
    )
    grad_coeffs = jnp.einsum(
        "blkd,lcd->blkc", grad_degree, spectral, preferred_element_type=jnp.float32
    ).astype(jnp.bfloat16)
    grad_coeff_orders = lax.all_to_all(grad_coeffs, "lat", split_axis=2, concat_axis=1, tiled=True)
    grad_grid = jnp.einsum(
        "jlk,blkc->bjkc", analysis_here, grad_coeff_orders.astype(jnp.float32), precision=HIGHEST
    )
    grad_lat = lax.all_to_all(
        shortened(grad_grid), "lat", split_axis=1, concat_axis=2, tiled=True
    ).astype(grad_grid.dtype)
    model_width = grad_state.shape[3]
    grad_normed = jnp.einsum(
        "bjkc,nk->bjnc", grad_lat[..., :model_width], fourier, precision=HIGHEST
    )
    grad_norm_one, grad_gain_one, grad_shift_one = normalize_back(
        grad_normed, unit_one, scale_one, gain_one
    )
    vectors_grad = (
        grad_gain_one,
        grad_shift_one,
        grad_gain_two,
        grad_shift_two,
        grad_bias_hidden,
        grad_bias_out,
    )
    return (grad_middle + grad_norm_one, (grad_spectral, vectors_grad, grad_w_in, grad_w_out))


def shards_general(fields, noise_fields, step_counts, spectral_flat, mlp_flat, cotangent):
    lat_count = lax.axis_size("lat")
    lat_index = lax.axis_index("lat")
    dates_here = fields.shape[0]
    rows_here = fields.shape[1]
    degrees_here = LDEG // lat_count
    orders_here = 2 * ORDERS // lat_count
    fourier, inverse, analysis, synthesis = [
        jnp.asarray(member) for member in spectral_tables(NLAT, NLON, LDEG, ORDERS)
    ]
    analysis_here = lax.dynamic_slice_in_dim(analysis, lat_index * orders_here, orders_here, 2)
    synthesis_here = lax.dynamic_slice_in_dim(synthesis, lat_index * orders_here, orders_here, 2)
    analysis_rows = lax.dynamic_slice_in_dim(analysis, lat_index * rows_here, rows_here, 0)
    synthesis_rows = lax.dynamic_slice_in_dim(synthesis, lat_index * rows_here, rows_here, 0)
    analysis_degrees = lax.dynamic_slice_in_dim(analysis, lat_index * degrees_here, degrees_here, 1)
    synthesis_degrees = lax.dynamic_slice_in_dim(
        synthesis, lat_index * degrees_here, degrees_here, 1
    )
    tables = (
        fourier,
        inverse,
        analysis_here,
        synthesis_here,
        analysis_rows,
        synthesis_rows,
        analysis_degrees,
        synthesis_degrees,
    )
    spectral_whole = lax.all_gather(spectral_flat, "dp", axis=1, tiled=True)
    mlp_whole = lax.all_gather(mlp_flat, ("dp", "lat"), axis=0, tiled=True)
    weights = build_weights(spectral_whole, mlp_whole, degrees_here)
    noise_steps = noise_fields.astype(jnp.float32).reshape(
        dates_here, STEPS, rows_here, NLON, NOISE
    )
    current = fields.astype(jnp.float32)
    kept_steps = []
    for step_index in range(STEPS):
        step_mask = (step_index < step_counts).astype(jnp.float32).reshape(dates_here, 1, 1, 1)
        current, kept_values = forward_step(
            current, noise_steps[:, step_index], step_mask, tables, weights
        )
        kept_steps.append((step_mask, kept_values))
    output_fields = current.astype(jnp.bfloat16)
    grad_state = cotangent.astype(jnp.float32)
    totals = None
    for step_index in reversed(range(STEPS)):
        step_mask, kept_values = kept_steps[step_index]
        grad_state, step_totals = backward_step(grad_state, step_mask, kept_values, tables, weights)
        totals = step_totals if totals is None else jax.tree.map(jnp.add, totals, step_totals)
    grad_spectral, grad_vectors, grad_w_in, grad_w_out = totals
    spectral_pad = jnp.zeros((spectral_whole.shape[1] - grad_spectral.size,), jnp.float32)
    spectral_pack = jnp.concatenate([grad_spectral.reshape(-1), spectral_pad]).reshape(1, -1)
    spectral_grad = lax.psum_scatter(
        spectral_pack.astype(jnp.bfloat16), "dp", scatter_dimension=1, tiled=True
    ).astype(jnp.float32)
    mlp_members = list(grad_vectors) + [grad_w_in.reshape(-1), grad_w_out.reshape(-1)]
    used_total = sum((member.size for member in mlp_members))
    mlp_pack = jnp.concatenate(
        mlp_members + [jnp.zeros((mlp_whole.shape[0] - used_total,), jnp.float32)]
    )
    mlp_grad = lax.psum_scatter(mlp_pack, ("dp", "lat"), scatter_dimension=0, tiled=True)
    return (output_fields, grad_state.astype(jnp.bfloat16), spectral_grad, mlp_grad)


ROWS = NLAT // 2
DEGS = LDEG // 2
CELLS = ROWS * NLON
DP = 768
HP = 1408
KP = 72
GROUPS = 9
GK = 8
DEPTH = 8
WROWS = 672
BLK = 4
BC = BLK * NLON
WIN = 992
MAIN = 944
TROWS = 1392
HEAD = 352
BF = jnp.bfloat16
F32 = jnp.float32
MB = 2**20


def params(limit=60, **more):
    return pltpu.CompilerParams(vmem_limit_bytes=limit * MB, **more)


LIGHT = pl.CostEstimate(flops=1, bytes_accessed=1, transcendentals=0)


def vspec():
    return pl.BlockSpec(memory_space=pltpu.VMEM)


def dot(a, b):
    return jnp.dot(a, b, preferred_element_type=F32)


def split_table(table):
    high = table.astype(BF).astype(np.float32)
    return np.concatenate([high, table - high, high], axis=1).astype(BF)


def split_dot(table, value):
    high = value.astype(BF).astype(F32)
    return dot(table, jnp.concatenate([high, high, value - high], axis=0).astype(BF))


def dot_nt(a, b):
    return lax.dot_general(a, b, (((1,), (1,)), ((), ())), preferred_element_type=F32)


def dot_tn(a, b):
    return lax.dot_general(a, b, (((0,), (0,)), ((), ())), preferred_element_type=F32)


def column_order():
    places = np.zeros(KP, np.int64)
    for group in range(GROUPS):
        for i in range(4):
            places[GK * group + i] = 4 * group + i
            places[GK * group + 4 + i] = ORDERS + 4 * group + i
    return places


def plan_tables():
    fourier, inverse, analysis, synthesis = spectral_tables(NLAT, NLON, LDEG, ORDERS)
    take = column_order()
    fourier = fourier[:, take]
    inverse = inverse[take, :]
    analysis = analysis[:, :, take]
    synthesis = synthesis[:, :, take]
    eye = np.eye(GK, dtype=np.float32)

    def blocks(table):
        out = np.zeros((2, GROUPS, 192, 384), np.float32)
        for own in range(2):
            for which in range(2):
                half = own if which == 0 else 1 - own
                for group in range(GROUPS):
                    part = table[24 * own : 24 * own + 24, 24 * half : 24 * half + 24]
                    part = part[:, :, GK * group : GK * group + GK]
                    full = np.einsum("pqi,ij->piqj", part, eye)
                    out[own, group, :, 192 * which : 192 * which + 192] = full.reshape(192, 192)
        return out.astype(BF)

    by_degree = np.transpose
    return dict(
        fourier_t=split_table(fourier.T),
        fourier=split_table(fourier),
        inverse_t=split_table(inverse.T),
        inverse=split_table(inverse),
        analyse=blocks(by_degree(analysis, (1, 0, 2))),
        synthesize=blocks(synthesis),
        analyse_back=blocks(analysis),
        synthesize_back=blocks(by_degree(synthesis, (1, 0, 2))),
    )


def rows_out(flat_ref, start, offset, step, wide, tiles, tail, put, count, unroll=4):
    lane = lax.broadcasted_iota(jnp.int32, (8, 128), 1)

    def one(t, carry):
        shift = offset + step * t
        jump = shift // 128
        shift = shift - 128 * jump
        amount = (128 - shift) % 128
        low = lane + shift < 128
        pieces = [
            pltpu.roll(flat_ref[pl.ds(start + wide * t + jump + m, 8, stride=641), :], amount, 1)
            for m in range(tiles + 1)
        ]
        for m in range(tiles):
            piece = jnp.where(low, pieces[m], pieces[m + 1])
            if m == tiles - 1:
                piece = jnp.where(lane < tail, piece, 0.0)
            put(m, t, piece)
        return carry

    lax.fori_loop(0, count, one, 0, unroll=unroll)


def rows_in(flat_ref, start, offset, step, wide, tiles, get, count, unroll=2):
    lane = lax.broadcasted_iota(jnp.int32, (8, 128), 1)

    def one(t, carry):
        shift = offset + step * t
        jump = shift // 128
        shift = shift - 128 * jump
        high = lane >= shift
        pieces = [pltpu.roll(get(m, t), shift, 1) for m in range(tiles)]
        last = tiles + (1 if step > 1 else 0)
        for m in range(last):
            here = pieces[m] if m < tiles else jnp.zeros((8, 128), F32)
            before = pieces[m - 1] if m > 0 else jnp.zeros((8, 128), F32)
            piece = jnp.where(high, here, before)
            where = pl.ds(start + wide * t + jump + m, 8, stride=641)
            if m == 0 or m >= tiles - 1:
                flat_ref[where, :] = flat_ref[where, :] + piece
            else:
                flat_ref[where, :] = piece
        return carry

    lax.fori_loop(0, count, one, 0, unroll=unroll)


def shard_place(shard, length):
    first = (shard * length) // D
    base = (first // 16) * 16
    start = D * base - length * shard + 128 * 88
    return base, start // 128, start % 128


def window_kernel(length, shard_ref, flat_ref, main_ref, side_ref, flat, tiles, extra):
    chunks = length // 128
    base, start, offset = shard_place(shard_ref[0], length)
    flat[0:88, :] = jnp.zeros((88, 128), F32)
    flat[88 + chunks :, :] = jnp.zeros((flat.shape[0] - 88 - chunks, 128), F32)

    def load(i, carry):
        piece = flat_ref[:, pl.ds(pl.multiple_of(1024 * i, 1024), 1024)]
        flat[pl.ds(pl.multiple_of(88 + 8 * i, 8), 8), :] = piece.astype(F32).reshape(8, 128)
        return carry

    lax.fori_loop(0, chunks // 8, load, 0, unroll=7)
    rest = chunks % 8
    if rest:
        piece = flat_ref[:, 128 * (chunks - rest) :].astype(F32).reshape(rest, 128)
        flat[88 + chunks - rest : 88 + chunks, :] = piece
    lane = lax.broadcasted_iota(jnp.int32, (8, 128), 1)
    extra[...] = jnp.zeros_like(extra)

    def put(m, t, piece):
        if m < 5:
            tiles[m, pl.ds(t, 8, stride=128), :] = piece
        else:
            extra[...] = jnp.where(lane == t, piece[:, 0:1], extra[...])

    rows_out(flat, start, offset, 1, 5, 6, 1, put, 128)
    side_ref[48:64, :] = jnp.zeros((16, 640), BF)
    side_ref[48:64, 0:128] = jnp.concatenate([extra[...], jnp.zeros((8, 128), F32)], axis=0).astype(BF)
    for m in range(5):
        at = slice(128 * m, 128 * m + 128)
        main_ref[:, at] = tiles[m, 16 : 16 + MAIN, :].astype(BF)
        side_ref[0:16, at] = tiles[m, 0:16, :].astype(BF)
        side_ref[16:48, at] = tiles[m, 16 + MAIN : WIN, :].astype(BF)


def spectral_window(shard, flat):
    length = flat.shape[1]
    return pl.pallas_call(
        partial(window_kernel, length),
        out_shape=(jax.ShapeDtypeStruct((MAIN, 640), BF), jax.ShapeDtypeStruct((64, 640), BF)),
        in_specs=[pl.BlockSpec(memory_space=pltpu.SMEM), vspec()],
        out_specs=(vspec(), vspec()),
        scratch_shapes=[
            pltpu.VMEM((5256, 128), F32),
            pltpu.VMEM((5, 1024, 128), F32),
            pltpu.VMEM((8, 128), F32),
        ],
        cost_estimate=LIGHT,
        compiler_params=params(),
    )(shard, flat)


VECTORS = ((0, D), (D, D), (2 * D, D), (3 * D, D), (4 * D, HID), (4 * D + HID, D))
IN_AT = 5 * D + HID
OUT_AT = IN_AT + D * HID


def mlp_kernel(flat_ref, in_ref, out_ref, vec_ref, flat, tin, tout):
    count, rows, _ = flat_ref.shape
    for k in range(count):
        flat[rows * k : rows * k + rows, :] = flat_ref[k].astype(F32)
    lane = lax.broadcasted_iota(jnp.int32, (1, 128), 1)
    vec_ref[...] = jnp.zeros_like(vec_ref)
    for row, (place, length) in enumerate(VECTORS):
        first, shift = place // 128, place % 128
        for m in range(-(-length // 128)):
            one = flat[first + m : first + m + 1, :]
            two = flat[first + m + 1 : first + m + 2, :]
            if shift:
                one = pltpu.roll(one, 128 - shift, 1)
                two = pltpu.roll(two, 128 - shift, 1)
            piece = jnp.where(lane + shift < 128, one, two)
            piece = jnp.where(lane + 128 * m < length, piece, 0.0)
            vec_ref[row : row + 1, 128 * m : 128 * m + 128] = piece
    for part in range(2):

        def put_in(m, t, piece, part=part):
            tin[m, pl.ds(t + 512 * part, 8, stride=64), :] = piece

        rows_out(flat, IN_AT // 128 + 641 * 8 * part, IN_AT % 128, 2, 10, 11, 2, put_in, 64, 4)

        def put_out(m, t, piece, part=part):
            tout[m, pl.ds(t + 1024 * part, 8, stride=128), :] = piece

        rows_out(flat, OUT_AT // 128 + 641 * 8 * part, OUT_AT % 128, 1, 5, 6, 1, put_out, 128, 8)
    keep = lax.broadcasted_iota(jnp.int32, (DP, 128), 0) < D
    for m in range(11):
        in_ref[:, 128 * m : 128 * m + 128] = jnp.where(keep, tin[m, :DP, :], 0.0).astype(BF)
    keep = lax.broadcasted_iota(jnp.int32, (HP, 128), 0) < HID
    for m in range(6):
        out_ref[:, 128 * m : 128 * m + 128] = jnp.where(keep, tout[m, :HP, :], 0.0).astype(BF)


def mlp_weights(flat):
    return pl.pallas_call(
        mlp_kernel,
        out_shape=(
            jax.ShapeDtypeStruct((DP, HP), BF),
            jax.ShapeDtypeStruct((HP, DP), BF),
            jax.ShapeDtypeStruct((8, HP), F32),
        ),
        in_specs=[vspec()],
        out_specs=(vspec(), vspec(), vspec()),
        scratch_shapes=[
            pltpu.VMEM((16776, 128), F32),
            pltpu.VMEM((11, 1024, 128), F32),
            pltpu.VMEM((6, 2048, 128), F32),
        ],
        cost_estimate=LIGHT,
        compiler_params=params(),
    )(flat)


ALL_ROWS = 15584
CHIPS = 8


def cuts(length, count):
    return [((s * length) // D) // 16 * 16 for s in range(count)] + [ALL_ROWS]


def gather_kernel(length, main_ref, side_ref, w_ref, column_ref, sides, edges, line, ring, over, arrive, local):
    dp = lax.axis_index("dp")
    lat = lax.axis_index("lat")
    core = dp % 2
    chip = dp // 2
    z = chip // 2
    x = chip % 2
    place = z + x * (7 - 2 * z)
    home = lat == core
    count = 2 * CHIPS

    def chip_at(p):
        p = (p + CHIPS) % CHIPS
        back = p // 4
        return ((1 - back) * p + back * (7 - p)) * 2 + back

    def device(p, which):
        return (chip_at(p) * 2 + which, lat)

    def shard(p, which):
        return chip_at(p) * 2 + which

    across = (dp, 1 - lat)
    partner = (dp + 1 - 2 * core, lat)
    barrier = pltpu.get_barrier_semaphore()
    for who in (device(place + 1, core), device(place - 1, core), across, partner):
        pl.semaphore_signal(barrier, inc=1, device_id=who, device_id_type=pl.DeviceIdType.MESH)
    pl.semaphore_wait(barrier, 4)

    def rows_of(s, first, size):
        start = ((s * length) // D) // 16 * 16 + 16 + first
        return w_ref.at[pl.ds(pl.multiple_of(start, 16), size)]

    def remote(src, dst, send, recv, who):
        return pltpu.make_async_remote_copy(
            src_ref=src, dst_ref=dst, send_sem=send, recv_sem=recv, device_id=who,
            device_id_type=pl.DeviceIdType.MESH,
        )

    first = core
    second = 1 - core
    hops = {1: [(0, 0), (0, 1), (1, 0), (1, 1), (2, 0), (2, 1), (3, 0)],
            -1: [(0, 0), (0, 1), (1, 0), (1, 1), (2, 0), (2, 1), (3, 1)]}
    coming = [(way, d, w) for d in (1, 2, 3) for w in (0, 1) for way in (1, -1)] + [(1, 4, 0), (-1, 4, 1)]

    def named(way, d, w):
        which = first if w == 0 else second
        return shard(place - way * d, which)

    def wait_part(kind, s, size):
        remote(rows_of(s, 0, size), rows_of(s, 0, size), local.at[0], arrive.at[kind, s], across).wait_recv()

    def wait_side(s):
        remote(sides.at[s], sides.at[s], local.at[0], arrive.at[2, s], across).wait_recv()

    own = dp

    @pl.when(home)
    def _():
        keep = pltpu.make_async_copy(main_ref, rows_of(own, 0, MAIN), local.at[0])
        keep.start()
        keep_side = pltpu.make_async_copy(side_ref, sides.at[own], local.at[1])
        keep_side.start()
        sent = []

        def send(way, hop, s, main, side):
            to = device(place + way, core)
            lane = 0 if way == 1 else 1
            copies = (
                remote(main, rows_of(s, 0, MAIN), ring.at[lane, hop], arrive.at[0, s], to),
                remote(side, sides.at[s], ring.at[lane + 2, hop], arrive.at[2, s], to),
            )
            for copy in copies:
                copy.start()
                sent.append(copy)

        def cross(index, s, main, side):
            copies = [remote(main(0, HEAD), rows_of(s, 0, HEAD), over.at[0, index], arrive.at[1, s], across)]
            copies.append(remote(side, sides.at[s], over.at[1, index], arrive.at[2, s], across))
            if index < 2:
                copies.insert(
                    0,
                    remote(
                        main(HEAD, MAIN - HEAD), rows_of(s, HEAD, MAIN - HEAD), over.at[2, index],
                        arrive.at[0, s], across,
                    ),
                )
            for copy in copies:
                copy.start()
                sent.append(copy)

        send(1, 0, own, main_ref, side_ref)
        send(-1, 0, own, main_ref, side_ref)
        cross(0, own, lambda at, size: main_ref.at[pl.ds(at, size)], side_ref)
        mate = dp + 1 - 2 * core
        wait_part(0, mate, MAIN)
        wait_side(mate)
        held = lambda s: (lambda at, size: rows_of(s, at, size))
        send(1, 1, mate, rows_of(mate, 0, MAIN), sides.at[mate])
        send(-1, 1, mate, rows_of(mate, 0, MAIN), sides.at[mate])
        cross(1, mate, held(mate), sides.at[mate])
        for index, (way, d, w) in enumerate(coming):
            s = named(way, d, w)
            wait_part(0, s, MAIN)
            wait_side(s)
            if (d, w) in hops[way]:
                send(way, hops[way].index((d, w)), s, rows_of(s, 0, MAIN), sides.at[s])
            cross(2 + index, s, held(s), sides.at[s])
        for copy in sent:
            copy.wait_send()
        keep.wait()
        keep_side.wait()

    @pl.when(jnp.logical_not(home))
    def _():
        sent = [
            remote(main_ref, rows_of(own, 0, MAIN), ring.at[4, 0], arrive.at[0, own], partner),
            remote(side_ref, sides.at[own], ring.at[4, 1], arrive.at[2, own], partner),
        ]
        for copy in sent:
            copy.start()
        size = MAIN - HEAD

        def send(way, hop, s):
            lane = 0 if way == 1 else 1
            copy = remote(
                rows_of(s, HEAD, size), rows_of(s, HEAD, size), ring.at[lane, hop], arrive.at[0, s],
                device(place + way, core),
            )
            copy.start()
            sent.append(copy)

        mate = dp + 1 - 2 * core
        wait_part(0, own, size)
        send(1, 0, own)
        send(-1, 0, own)
        wait_part(0, mate, size)
        send(1, 1, mate)
        send(-1, 1, mate)
        for way, d, w in coming:
            s = named(way, d, w)
            wait_part(0, s, size)
            if (d, w) in hops[way]:
                send(way, hops[way].index((d, w)), s)
        for s in [own, mate] + [named(*one) for one in coming]:
            wait_part(1, s, HEAD)
            wait_side(s)
        for copy in sent:
            copy.wait_send()

    places = cuts(length, count)
    copies = []
    for s in range(count):
        span = places[s + 1] - places[s]
        edge = sides[s, 0:16, :]
        if s:
            before = places[s] - places[s - 1] - 16 - MAIN
            edge = edge + sides[s - 1, 16 + before : 32 + before, :]
        edges[s] = edge
        copies.append(pltpu.make_async_copy(edges.at[s], w_ref.at[pl.ds(places[s], 16)], local.at[2 + s]))
        left = span - 16 - MAIN
        if left:
            copies.append(
                pltpu.make_async_copy(
                    sides.at[s, pl.ds(16, left)], w_ref.at[pl.ds(places[s] + 16 + MAIN, left)],
                    local.at[2 + count + s],
                )
            )
    for copy in copies:
        copy.start()
    lane = lax.broadcasted_iota(jnp.int32, (8, 128), 1)
    line[...] = jnp.zeros_like(line)
    for s in range(count):
        a, b = places[s] // 128, places[s] % 128
        piece = sides[s, 48:64, 0:128].astype(F32)[:8]
        if b:
            piece = pltpu.roll(piece, b, 1)
        line[a : a + 8, :] += jnp.where(lane >= b, piece, 0.0)
        line[a + 1 : a + 9, :] += jnp.where(lane < b, piece, 0.0)
    lane = lax.broadcasted_iota(jnp.int32, (1, 128), 1)
    for degree in range(DEGS):
        a, b = CIN * degree // 128, CIN * degree % 128
        piece = line[a : a + 8, :]
        if b:
            piece = pltpu.roll(piece, 128 - b, 1)
        for m in range(6):
            one = jnp.where(lane + b < 128, piece[m : m + 1], piece[m + 1 : m + 2])
            one = jnp.where(lane + 128 * m < CIN, one, 0.0)
            column_ref[degree : degree + 1, 128 * m : 128 * m + 128] = one
    for copy in copies:
        copy.wait()


def gather_rows(length, main, side):
    count = 2 * CHIPS
    return pl.pallas_call(
        partial(gather_kernel, length),
        out_shape=(jax.ShapeDtypeStruct((ALL_ROWS, 640), BF), jax.ShapeDtypeStruct((DEGS, DP), F32)),
        in_specs=[vspec(), vspec()],
        out_specs=(pl.BlockSpec(memory_space=pl.ANY), vspec()),
        scratch_shapes=[
            pltpu.VMEM((count, 64, 640), BF),
            pltpu.VMEM((count, 16, 640), BF),
            pltpu.VMEM((136, 128), F32),
            pltpu.SemaphoreType.DMA((5, 7)),
            pltpu.SemaphoreType.DMA((3, count)),
            pltpu.SemaphoreType.DMA((3, count)),
            pltpu.SemaphoreType.DMA((2 + 2 * count,)),
        ],
        cost_estimate=LIGHT,
        compiler_params=params(30, collective_id=0, has_side_effects=True),
    )(main, side)


def lane_mask():
    return (lax.broadcasted_iota(jnp.int32, (1, DP), 1) < D).astype(F32)


def unit_of(values, mask):
    mean = jnp.sum(values, axis=-1, keepdims=True) * (1.0 / D)
    centred = (values - mean) * mask
    square = jnp.sum(centred * centred, axis=-1, keepdims=True) * (1.0 / D)
    scale = lax.rsqrt(square + 1e-06)
    return centred * scale, scale


def norm_back(upstream, unit, scale, gain):
    scaled = upstream * gain
    mean_one = jnp.sum(scaled, axis=-1, keepdims=True) * (1.0 / D)
    mean_two = jnp.sum(scaled * unit, axis=-1, keepdims=True) * (1.0 / D)
    return scale * (scaled - mean_one * lane_mask() - unit * mean_two)


def modes_kernel(state_ref, noise_ref, vec_ref, table_ref, out_ref):
    unit, scale = unit_of(state_ref[...].astype(F32), lane_mask())
    normed = unit * vec_ref[0:1, :DP] + vec_ref[1:2, :DP]
    joined = jnp.concatenate(
        [normed[:, :640], normed[:, 640:] + noise_ref[...].astype(F32)], axis=1
    )
    for j in range(BLK):
        piece = joined[NLON * j : NLON * j + NLON, :]
        out_ref[j] = split_dot(table_ref[...], piece).astype(BF).reshape(GROUPS, GK, DP)


def modes(state, noise, vectors, table):
    return pl.pallas_call(
        modes_kernel,
        grid=(ROWS // BLK,),
        out_shape=jax.ShapeDtypeStruct((ROWS, GROUPS, GK, DP), BF),
        in_specs=[
            pl.BlockSpec((BC, DP), lambda i: (i, 0)),
            pl.BlockSpec((BC, 128), lambda i: (i, 0)),
            pl.BlockSpec((8, HP), lambda i: (0, 0)),
            pl.BlockSpec((KP, 3 * NLON), lambda i: (0, 0)),
        ],
        out_specs=pl.BlockSpec((BLK, GROUPS, GK, DP), lambda i: (i, 0, 0, 0)),
        cost_estimate=LIGHT,
        compiler_params=params(),
    )(state, noise, vectors, table)


class Swap:
    def __init__(self, own_ref, other, table_ref, table, send, recv, sem):
        dp = lax.axis_index("dp")
        core = dp % 2
        self.partner = (dp + 1 - 2 * core, lax.axis_index("lat"))
        self.table = pltpu.make_async_copy(table_ref.at[core], table, sem)
        self.copies = [
            pltpu.make_async_remote_copy(
                src_ref=own_ref.at[:, group], dst_ref=other.at[:, group], send_sem=send.at[group],
                recv_sem=recv.at[group], device_id=self.partner, device_id_type=pl.DeviceIdType.MESH,
            )
            for group in range(GROUPS)
        ]

    def start(self):
        self.table.start()
        barrier = pltpu.get_barrier_semaphore()
        pl.semaphore_signal(barrier, inc=1, device_id=self.partner, device_id_type=pl.DeviceIdType.MESH)
        pl.semaphore_wait(barrier, 1)
        for copy in self.copies:
            copy.start()

    def finish(self):
        for copy in self.copies:
            copy.wait_send()


def swap_scratch():
    return [
        pltpu.VMEM((24, GROUPS, GK, DP), BF),
        pltpu.VMEM((GROUPS, 192, 384), BF),
        pltpu.SemaphoreType.DMA((GROUPS,)),
        pltpu.SemaphoreType.DMA((GROUPS,)),
        pltpu.SemaphoreType.DMA,
    ]


def legendre(own_ref, table_ref, out_ref, swap_refs):
    other, table, send, recv, sem = swap_refs
    swap = Swap(own_ref, other, table_ref, table, send, recv, sem)
    swap.start()
    swap.table.wait()
    for group in range(GROUPS):
        swap.copies[group].wait_recv()
        both = jnp.concatenate(
            [own_ref[:, group].reshape(192, DP), other[:, group].reshape(192, DP)], axis=0
        )
        total = dot(table[group], both)
        out_ref[:, group] = total.astype(out_ref.dtype).reshape(24, GK, DP)
    swap.finish()


def fetch(w_ref, w_buf, sem, degree):
    slot = degree % DEPTH
    first = pl.multiple_of((CIN * degree) // 16 * 16, 16)
    return pltpu.make_async_copy(w_ref.at[pl.ds(first, WROWS)], w_buf.at[slot], sem.at[slot])


def fetch_next(w_ref, w_buf, sem, degree):
    fetch(w_ref, w_buf, sem, degree).wait()


def fetch_ahead(w_ref, w_buf, sem, degree):
    @pl.when(degree + DEPTH < DEGS)
    def _():
        fetch(w_ref, w_buf, sem, degree + DEPTH).start()


C_TILES = 9
G_TILES = 11
OWNERS = 16


def owner_degrees(owner):
    first = 3 * (owner // 2)
    return first + 2 * (owner % 2), first + 1


def pack_tiles(block_ref, parts_ref, middle_tiles):
    lane = lax.broadcasted_iota(jnp.int32, (KP, 128), 1)
    for owner in range(OWNERS):
        own, middle = owner_degrees(owner)
        for m in range(5):
            at = slice(128 * m, 128 * m + 128)
            parts_ref[owner, m] = block_ref[own, :, :, at].reshape(KP, 128)
        for n, m in enumerate(middle_tiles[owner % 2]):
            at = slice(128 * m, 128 * m + 128)
            parts_ref[owner, 5 + n] = block_ref[middle, :, :, at].reshape(KP, 128)
        one = block_ref[own, :, :, 640:].reshape(KP, 128).astype(F32)
        two = block_ref[middle, :, :, 640:].reshape(KP, 128).astype(F32)
        two = pltpu.roll(two, 16, 1)
        last = parts_ref.shape[1] - 1
        parts_ref[owner, last] = jnp.where(lane < 16, one, two).astype(BF)


def mix_kernel(own_ref, table_ref, column_ref, w_ref, parts_ref, mixed_ref, coeff_ref, w_buf, sem, *swap_refs):
    for degree in range(DEPTH):
        fetch(w_ref, w_buf, sem, degree).start()
    legendre(own_ref, table_ref, coeff_ref, swap_refs)
    pack_tiles(coeff_ref, parts_ref, ((0, 1, 2), (2, 3, 4)))
    lane = lax.broadcasted_iota(jnp.int32, (KP, 128), 1)

    def one(degree, carry):
        fetch_next(w_ref, w_buf, sem, degree)
        coeffs = coeff_ref[degree].reshape(KP, DP).astype(F32)
        moved = pltpu.roll(coeffs, (CIN * degree) % 16, 1)
        mixed = dot(moved[:, :WROWS].astype(BF), w_buf[degree % DEPTH])
        last = jnp.sum(coeffs * column_ref[pl.ds(degree, 1), :], axis=1, keepdims=True)
        mixed = jnp.concatenate([mixed, jnp.where(lane < 1, last, 0.0)], axis=1)
        mixed_ref[degree] = mixed.astype(BF).reshape(GROUPS, GK, DP)
        fetch_ahead(w_ref, w_buf, sem, degree)
        return carry

    lax.fori_loop(0, DEGS, one, 0)


def mix_back_kernel(
    own_ref, table_ref, column_ref, w_ref, parts_ref, out_ref, grad_ref, w_buf, wide, sem, *swap_refs
):
    for degree in range(DEPTH):
        fetch(w_ref, w_buf, sem, degree).start()
    legendre(own_ref, table_ref, grad_ref, swap_refs)
    every = (0, 1, 2, 3, 4)
    pack_tiles(grad_ref, parts_ref, (every, every))
    keep = lax.broadcasted_iota(jnp.int32, (KP, DP), 1) < CIN
    wide[...] = jnp.zeros_like(wide)

    def one(degree, carry):
        fetch_next(w_ref, w_buf, sem, degree)
        grad = grad_ref[degree].reshape(KP, DP)
        wide[:, :WROWS] = dot_nt(grad[:, :640], w_buf[degree % DEPTH])
        back = pltpu.roll(wide[...], DP - (CIN * degree) % 16, 1)
        last = grad[:, 640:].astype(F32)[:, 0:1]
        back = back + last * column_ref[pl.ds(degree, 1), :]
        out_ref[degree] = jnp.where(keep, back, 0.0).astype(BF).reshape(GROUPS, GK, DP)
        fetch_ahead(w_ref, w_buf, sem, degree)
        return carry

    lax.fori_loop(0, DEGS, one, 0)


def anywhere():
    return pl.BlockSpec(memory_space=pl.ANY)


def mix(own, table, weights, column, back):
    tiles = G_TILES if back else C_TILES
    scratch = [pltpu.VMEM((24, GROUPS, GK, DP), BF), pltpu.VMEM((DEPTH, WROWS, 640), BF)]
    if back:
        scratch.append(pltpu.VMEM((KP, DP), F32))
    scratch.append(pltpu.SemaphoreType.DMA((DEPTH,)))
    return pl.pallas_call(
        mix_back_kernel if back else mix_kernel,
        in_specs=[vspec(), anywhere(), vspec(), anywhere()],
        out_specs=(vspec(), vspec()),
        scratch_shapes=scratch + swap_scratch(),
        out_shape=(
            jax.ShapeDtypeStruct((OWNERS, tiles, KP, 128), BF),
            jax.ShapeDtypeStruct((24, GROUPS, GK, DP), BF),
        ),
        cost_estimate=LIGHT,
        compiler_params=params(collective_id=2 if back else 1, has_side_effects=True),
    )(own, table, column, weights)


HID_PARTS = ((0, 256), (256, 256), (512, 256), (768, 256), (1024, 256), (1280, 128))


def feed_kernel(
    mask_ref, own_ref, table_ref, inverse_ref, state_ref, vec_ref, in_ref, out_ref,
    next_ref, middle_ref, hidden_ref, active_ref, slope_ref, lat, *swap_refs
):
    i = pl.program_id(0)

    @pl.when(i == 0)
    def _():
        legendre(own_ref, table_ref, lat, swap_refs)

    mask = mask_ref[0:1, 0:1]
    parts = [split_dot(inverse_ref[...], lat[BLK * i + j].reshape(KP, DP)) for j in range(BLK)]
    middle = state_ref[...].astype(F32) + mask * jnp.concatenate(parts, axis=0)
    middle_ref[...] = middle
    unit, scale = unit_of(middle, lane_mask())
    hidden = (unit * vec_ref[2:3, :DP] + vec_ref[3:4, :DP]).astype(BF)
    hidden_ref[...] = hidden
    for first, width in HID_PARTS:
        at = slice(first, first + width)
        pre = dot(hidden, in_ref[:, at]) + vec_ref[4:5, at]
        bell = 0.5 * (1.0 + lax.erf(pre * (1.0 / math.sqrt(2.0))))
        active_ref[:, at] = (pre * bell).astype(BF)
        slope = bell + pre * (jnp.exp(-0.5 * pre * pre) * (1.0 / math.sqrt(2.0 * math.pi)))
        slope_ref[:, at] = slope.astype(BF)
    result = dot(active_ref[...], out_ref[...]) + vec_ref[5:6, :DP]
    next_ref[...] = (middle + mask * result).astype(next_ref.dtype)


def cell_spec(width):
    return pl.BlockSpec((BC, width), lambda i, *h: (i, 0))


def fixed(*shape):
    return pl.BlockSpec(shape, lambda i, *h: (0,) * len(shape))


def feed(mask, own, table, inverse_t, state, vectors, w_in, w_out, last):
    cells = lambda width, kind: jax.ShapeDtypeStruct((CELLS, width), kind)
    return pl.pallas_call(
        feed_kernel,
        grid=(ROWS // BLK,),
        in_specs=[
            fixed(1, 128), fixed(24, GROUPS, GK, DP), anywhere(), fixed(NLON, 3 * KP), cell_spec(DP),
            fixed(8, HP), fixed(DP, HP), fixed(HP, DP),
        ],
        out_specs=(cell_spec(DP), cell_spec(DP), cell_spec(DP), cell_spec(HP), cell_spec(HP)),
        scratch_shapes=[pltpu.VMEM((24, GROUPS, GK, DP), F32)] + swap_scratch(),
        out_shape=(
            cells(DP, BF if last else F32), cells(DP, F32), cells(DP, BF), cells(HP, BF), cells(HP, BF),
        ),
        cost_estimate=LIGHT,
        compiler_params=params(collective_id=4 if last else 3, has_side_effects=True),
    )(mask, own, table, inverse_t, state, vectors, w_in, w_out)


def feed_back_kernel(
    mask_ref, grad_ref, slope_ref, middle_ref, vec_ref, in_ref, out_ref, inverse_ref,
    result_ref, pre_ref, gm_ref, modes_ref, sums_ref,
):
    i = pl.program_id(0)

    @pl.when(i == 0)
    def _():
        sums_ref[...] = jnp.zeros_like(sums_ref)

    mask = mask_ref[0:1, 0:1]
    grad = grad_ref[...].astype(F32)
    result = (mask * grad).astype(BF)
    result_ref[...] = result
    sums_ref[5:6, :DP] += jnp.sum(result.astype(F32), axis=0, keepdims=True)
    for first, width in HID_PARTS:
        at = slice(first, first + width)
        active = dot_nt(result, out_ref[at, :])
        pre = (active * slope_ref[:, at].astype(F32)).astype(BF)
        pre_ref[:, at] = pre
        sums_ref[4:5, at] += jnp.sum(pre.astype(F32), axis=0, keepdims=True)
    upstream = dot_nt(pre_ref[...], in_ref[...])
    unit, scale = unit_of(middle_ref[...], lane_mask())
    sums_ref[2:3, :DP] += jnp.sum(upstream * unit, axis=0, keepdims=True)
    sums_ref[3:4, :DP] += jnp.sum(upstream, axis=0, keepdims=True)
    total = grad + norm_back(upstream, unit, scale, vec_ref[2:3, :DP])
    gm_ref[...] = total
    total = mask * total
    for j in range(BLK):
        piece = total[NLON * j : NLON * j + NLON, :]
        modes_ref[j] = split_dot(inverse_ref[...], piece).astype(BF).reshape(GROUPS, GK, DP)


def feed_back(mask, grad, slope, middle, vectors, w_in, w_out, inverse):
    cells = lambda width, kind: jax.ShapeDtypeStruct((CELLS, width), kind)
    return pl.pallas_call(
        feed_back_kernel,
        grid=(ROWS // BLK,),
        in_specs=[
            fixed(1, 128), cell_spec(DP), cell_spec(HP), cell_spec(DP), fixed(8, HP), fixed(DP, HP),
            fixed(HP, DP), fixed(KP, 3 * NLON),
        ],
        out_specs=(
            cell_spec(DP), cell_spec(HP), cell_spec(DP),
            pl.BlockSpec((BLK, GROUPS, GK, DP), lambda i: (i, 0, 0, 0)), fixed(8, HP),
        ),
        out_shape=(
            cells(DP, BF), cells(HP, BF), cells(DP, F32), jax.ShapeDtypeStruct((ROWS, GROUPS, GK, DP), BF),
            jax.ShapeDtypeStruct((8, HP), F32),
        ),
        cost_estimate=LIGHT,
        compiler_params=params(),
    )(mask, grad, slope, middle, vectors, w_in, w_out, inverse)


def first_back_kernel(
    own_ref, table_ref, fourier_ref, state_ref, gm_ref, vec_ref, out_ref, sums_ref, lat, *swap_refs
):
    i = pl.program_id(0)

    @pl.when(i == 0)
    def _():
        legendre(own_ref, table_ref, lat, swap_refs)
        sums_ref[...] = jnp.zeros_like(sums_ref)

    parts = [split_dot(fourier_ref[...], lat[BLK * i + j].reshape(KP, DP)) for j in range(BLK)]
    upstream = jnp.concatenate(parts, axis=0)
    unit, scale = unit_of(state_ref[...].astype(F32), lane_mask())
    sums_ref[0:1, :] += jnp.sum(upstream * unit, axis=0, keepdims=True)
    sums_ref[1:2, :] += jnp.sum(upstream, axis=0, keepdims=True)
    total = gm_ref[...] + norm_back(upstream, unit, scale, vec_ref[0:1, :DP])
    out_ref[...] = total.astype(out_ref.dtype)


def first_back(own, table, fourier, state, gm, vectors, last):
    return pl.pallas_call(
        first_back_kernel,
        grid=(ROWS // BLK,),
        in_specs=[
            fixed(24, GROUPS, GK, DP), anywhere(), fixed(NLON, 3 * KP), cell_spec(DP), cell_spec(DP),
            fixed(8, HP),
        ],
        out_specs=(cell_spec(DP), fixed(8, DP)),
        scratch_shapes=[pltpu.VMEM((24, GROUPS, GK, DP), F32)] + swap_scratch(),
        out_shape=(
            jax.ShapeDtypeStruct((CELLS, DP), BF if last else F32), jax.ShapeDtypeStruct((8, DP), F32),
        ),
        cost_estimate=LIGHT,
        compiler_params=params(collective_id=6 if last else 5, has_side_effects=True),
    )(own, table, fourier, state, gm, vectors)


def mlp_grad_kernel(h0, h1, p0, p1, a0, a1, r0, r1, tin, tout, turned):
    for step, ref in enumerate((h0, h1)):
        turned[:, CELLS * step : CELLS * step + CELLS] = ref[...].T
    for first, width in HID_PARTS:
        at = slice(first, first + width)
        part = dot(turned[:, :CELLS], p0[:, at]) + dot(turned[:, CELLS:], p1[:, at])
        for m in range(width // 128):
            tin[first // 128 + m] = part[:, 128 * m : 128 * m + 128]
        part = dot_tn(a0[:, at], r0[...]) + dot_tn(a1[:, at], r1[...])
        for m in range(6):
            tout[m, at, :] = part[:, 128 * m : 128 * m + 128]


def mlp_flat_kernel(gin, gout, feed_sums, first_sums, pack_ref, tin, tout, flat_ref):
    tin[:, :DP, :] = gin[...]
    tout[:, :HP, :] = gout[...]
    tin[:, DP:, :] = jnp.zeros((11, 1024 - DP, 128), F32)
    tout[:, HP:, :] = jnp.zeros((6, 2048 - HP, 128), F32)
    flat_ref[...] = jnp.zeros_like(flat_ref)
    lane = lax.broadcasted_iota(jnp.int32, (1, 128), 1)
    sums = feed_sums[...]
    for row, (place, length) in enumerate(VECTORS):
        first, shift = place // 128, place % 128
        for m in range(-(-length // 128)):
            at = slice(128 * m, 128 * m + 128)
            piece = first_sums[row : row + 1, at] if row < 2 else sums[row : row + 1, at]
            piece = jnp.where(lane + 128 * m < length, piece, 0.0)
            if shift:
                piece = pltpu.roll(piece, shift, 1)
            flat_ref[first + m : first + m + 1, :] += jnp.where(lane >= shift, piece, 0.0)
            flat_ref[first + m + 1 : first + m + 2, :] += jnp.where(lane < shift, piece, 0.0)
    for part in range(2):

        def get_in(m, t, part=part):
            return tin[m, pl.ds(t + 512 * part, 8, stride=64), :]

        rows_in(flat_ref, IN_AT // 128 + 641 * 8 * part, IN_AT % 128, 2, 10, 11, get_in, 64, 4)

    for part in range(2):

        def get_out(m, t, part=part):
            return tout[m, pl.ds(t + 1024 * part, 8, stride=128), :]

        rows_in(flat_ref, OUT_AT // 128 + 641 * 8 * part, OUT_AT % 128, 1, 5, 6, get_out, 128, 8)
    for k in range(32):
        piece = flat_ref[SHARD_ROWS * k : SHARD_ROWS * k + SHARD_ROWS, :]
        piece = jnp.concatenate([piece, jnp.zeros((416 - SHARD_ROWS, 128), F32)], axis=0)
        pack_ref[(k // 2) % 2, (k // 4) * 2 + k % 2] = piece.astype(BF)


FLAT_ROWS = 16784
SHARD_ROWS = 403


def mlp_grads(hidden, pre, active, result, feed_sums, first_sums):
    gin, gout = pl.pallas_call(
        mlp_grad_kernel,
        out_shape=(jax.ShapeDtypeStruct((11, DP, 128), F32), jax.ShapeDtypeStruct((6, HP, 128), F32)),
        in_specs=[vspec()] * 8,
        out_specs=(vspec(), vspec()),
        scratch_shapes=[pltpu.VMEM((DP, 2 * CELLS), BF)],
        cost_estimate=LIGHT,
        compiler_params=params(62),
    )(*hidden, *pre, *active, *result)
    return pl.pallas_call(
        mlp_flat_kernel,
        out_shape=jax.ShapeDtypeStruct((2, 16, 416, 128), BF),
        in_specs=[vspec()] * 4,
        out_specs=vspec(),
        scratch_shapes=[
            pltpu.VMEM((11, 1024, 128), F32),
            pltpu.VMEM((6, 2048, 128), F32),
            pltpu.VMEM((FLAT_ROWS, 128), F32),
        ],
        cost_estimate=LIGHT,
        compiler_params=params(62),
    )(gin, gout, feed_sums, first_sums)


def spectral_grad_kernel(odd_ref, c0, c1, g0, g1, out_ref, head_ref, tiles_ref):
    rows = OWNERS * KP
    lane = lax.broadcasted_iota(jnp.int32, (DP, 128), 1)
    tiles_ref[:, 0:16, :] = jnp.zeros((6, 16, 128), F32)
    tiles_ref[:, 16 + 2 * CIN :, :] = jnp.zeros((6, TROWS - 16 - 2 * CIN, 128), F32)

    def side(ref, first, count):
        take = [ref[:, m].reshape(rows, 128) for m in list(range(first, first + count)) + [ref.shape[1] - 1]]
        return jnp.concatenate(take, axis=1)

    def product(c_first, c_count, g_first):
        total = dot_tn(side(c0, c_first, c_count), side(g0, g_first, 5))
        return total + dot_tn(side(c1, c_first, c_count), side(g1, g_first, 5))

    def save(start, part, first, count, column):
        for m in range(6):
            piece = part[first : first + count, 128 * m : 128 * m + 128]
            if m == 5:
                if column:
                    piece = pltpu.roll(piece, 128 - column, 1)
                piece = jnp.where(lane[:count] < 1, piece, 0.0)
            tiles_ref[m, start : start + count, :] = piece

    own = product(0, 5, 0)
    head = jnp.concatenate([own[0:16, :640], jnp.where(lane[:16] < 1, own[0:16, 640:], 0.0)], axis=1)
    head_ref[...] = head.astype(BF)
    middle = product(5, 3, 5)

    @pl.when(odd_ref[0] == 0)
    def _():
        save(16, own, 0, CIN, 0)
        save(16 + CIN, middle, 0, 384, 16)
        tiles_ref[:, 16 + CIN + 384 : 16 + 2 * CIN, :] = jnp.zeros((6, CIN - 384, 128), F32)

    @pl.when(odd_ref[0] == 1)
    def _():
        tiles_ref[:, 16 : 16 + 256, :] = jnp.zeros((6, 256, 128), F32)
        save(16 + 256, middle, 0, 384, 16)
        save(16 + 640, middle, 400, 9, 16)
        save(16 + CIN, own, 0, CIN, 0)

    out_ref[...] = tiles_ref[...].astype(BF)


def spectral_grads(odd, coeffs, grads):
    return pl.pallas_call(
        spectral_grad_kernel,
        out_shape=(jax.ShapeDtypeStruct((6, TROWS, 128), BF), jax.ShapeDtypeStruct((16, DP), BF)),
        in_specs=[pl.BlockSpec(memory_space=pltpu.SMEM)] + [vspec()] * 4,
        out_specs=(vspec(), vspec()),
        scratch_shapes=[pltpu.VMEM((6, TROWS, 128), F32)],
        cost_estimate=LIGHT,
        compiler_params=params(),
    )(odd, *coeffs, *grads)


def flatten_kernel(length, shard_ref, own_ref, moved_ref, next_ref, out_ref, tiles, flat):
    chunks = length // 128
    shard = shard_ref[0]
    base, start, offset = shard_place(shard, length)
    move = base - CIN * ((3 * shard) // 2) + 16

    @pl.when(shard_ref[1] == 1)
    def _():
        tiles[...] = own_ref[...].astype(F32)

    @pl.when(shard_ref[1] == 0)
    def _():
        tiles[...] = moved_ref[...].astype(F32)

    for m in range(6):
        piece = next_ref[:, 128 * m : 128 * m + 128].astype(F32)
        tiles[m, 16 + 2 * CIN : 24 + 2 * CIN, :] = piece[:8]
    flat[...] = jnp.zeros_like(flat)

    def get(m, t):
        return tiles[m, pl.ds(t + move, 8, stride=128), :]

    rows_in(flat, start, offset, 1, 5, 6, get, 128, 8)

    def save(i, carry):
        piece = flat[pl.ds(pl.multiple_of(88 + 8 * i, 8), 8), :].reshape(1, 1024)
        out_ref[:, pl.ds(pl.multiple_of(1024 * i, 1024), 1024)] = piece
        return carry

    lax.fori_loop(0, chunks // 8, save, 0, unroll=7)
    rest = chunks % 8
    if rest:
        piece = flat[88 + chunks - rest : 88 + chunks, :].reshape(1, 128 * rest)
        out_ref[:, 128 * (chunks - rest) :] = piece


def flatten(shard, own, moved, after, length):
    return pl.pallas_call(
        partial(flatten_kernel, length),
        out_shape=jax.ShapeDtypeStruct((1, length), F32),
        in_specs=[pl.BlockSpec(memory_space=pltpu.SMEM), vspec(), vspec(), vspec()],
        out_specs=vspec(),
        scratch_shapes=[pltpu.VMEM((6, TROWS, 128), F32), pltpu.VMEM((5256, 128), F32)],
        cost_estimate=LIGHT,
        compiler_params=params(),
    )(shard, own, moved, after)


def wide(block):
    flat = block.reshape(CELLS, D)
    return jnp.pad(flat, ((0, 0), (0, DP - D)))


def shards_paired(fields, noise_fields, step_counts, spectral_flat, mlp_flat, cotangent):
    axes = ("dp", "lat")
    dp_count = lax.axis_size("dp")
    dp_index = lax.axis_index("dp")
    core = dp_index % 2
    lat_index = lax.axis_index("lat")
    length = spectral_flat.shape[1]
    places = [(d, y) for d in range(dp_count) for y in range(2)]
    number = lambda d, y: 2 * d + y
    mirror = [(number(d, y), number(d - d % 2 + y, d % 2)) for d, y in places]
    crossing = [pair for pair in mirror if pair[0] != pair[1]]
    other_core = [(number(d, y), number(d + 1 - 2 * (d % 2), y)) for d, y in places]
    same_core = [[number(d, y) for d, y in places if d % 2 == c] for c in range(2)]
    stays = core == lat_index

    def mirrored(block):
        moved = lax.ppermute(block, axes, crossing)
        return jnp.where(stays, block, moved)

    swapped = lambda a: lax.ppermute(a, axes, other_core)
    tables = {name: jnp.asarray(value) for name, value in plan_tables().items()}

    main, side = spectral_window(dp_index.astype(jnp.int32).reshape(1), spectral_flat)
    weights, column = gather_rows(length, main, side)
    mlp_whole = lax.all_gather(mlp_flat.reshape(-1, 128), axes, axis=0, tiled=False)
    moved = lax.ppermute(wide(cotangent), axes, crossing)
    mlp_whole, weights, moved = lax.optimization_barrier((mlp_whole, weights, moved))
    state = mirrored(wide(fields))
    noise = mirrored(noise_fields).reshape(STEPS, CELLS, NOISE)
    noise = jnp.pad(noise, ((0, 0), (0, 0), (1, 128 - 1 - NOISE)))
    counts = mirrored(step_counts)
    w_in, w_out, vectors = mlp_weights(mlp_whole)

    kept = []
    for step in range(STEPS):
        mask = jnp.broadcast_to((step < counts).astype(F32).reshape(1, 1), (1, 128))
        lon_modes = modes(state, noise[step], vectors, tables["fourier_t"])
        parts, mixed = mix(lon_modes, tables["analyse"], weights, column, False)
        following, middle, hidden, active, slope = feed(
            mask, mixed, tables["synthesize"], tables["inverse_t"], state, vectors, w_in, w_out,
            step == STEPS - 1,
        )
        kept.append((mask, state, parts, middle, hidden, active, slope))
        state = following
    output = mirrored(state)
    grad = jnp.where(stays, wide(cotangent), moved)

    def to_owners(parts):
        return lax.all_to_all(
            parts, axes, split_axis=0, concat_axis=0, tiled=True, axis_index_groups=same_core
        )

    received = []

    def to_owners_next(parts):
        if received:
            parts, received[-1] = lax.optimization_barrier((parts, received[-1]))
        received.append(to_owners(parts))

    for step in range(STEPS):
        to_owners_next(kept[step][2])
    results = [None] * STEPS
    pres = [None] * STEPS
    feed_sums = first_sums = 0.0
    for step in reversed(range(STEPS)):
        mask, state, parts, middle, hidden, active, slope = kept[step]
        results[step], pres[step], gm, grad_modes, sums = feed_back(
            mask, grad, slope, middle, vectors, w_in, w_out, tables["inverse"]
        )
        feed_sums = feed_sums + sums
        parts, grad_coeffs = mix(
            grad_modes, tables["synthesize_back"], weights, column, True
        )
        to_owners_next(parts)
        grad, sums = first_back(
            grad_coeffs, tables["analyse_back"], tables["fourier"], state, gm,
            vectors, step == 0,
        )
        first_sums = first_sums + sums
    fields_grad = mirrored(grad)
    mlp_pack = mlp_grads(
        [k[4] for k in kept], pres, [k[5] for k in kept], results, feed_sums, first_sums
    )
    own = lax.dynamic_index_in_dim(mlp_pack, core, 0, keepdims=False)
    give = lax.dynamic_index_in_dim(mlp_pack, 1 - core, 0, keepdims=False)
    pair = (own.astype(F32) + swapped(give).astype(F32)).astype(BF)
    pair = lax.all_to_all(
        pair, axes, split_axis=0, concat_axis=0, tiled=True, axis_index_groups=same_core
    )
    mlp_grad = jnp.sum(pair.astype(F32), axis=0)[: mlp_flat.shape[0] // 128].reshape(-1)

    odd = lat_index.astype(jnp.int32).reshape(1)
    tiles, head = spectral_grads(odd, received[:2], [received[3], received[2]])
    spot = lambda s, c: number(s - s % 2 + c, s % 2)
    earlier = [(spot(s, c), number(s - 1, c)) for s in range(2, dp_count, 2) for c in range(2)]
    after = lax.ppermute(head, axes, earlier)
    moved = lax.ppermute(tiles, axes, crossing)
    place = jnp.stack([dp_index.astype(jnp.int32), stays.astype(jnp.int32)])
    spectral_grad = flatten(place, tiles, moved, after, length)
    narrow = lambda a: a[:, :D].reshape(1, ROWS, NLON, D)
    return narrow(output), narrow(fields_grad), spectral_grad, mlp_grad


def solution(mesh):
    paired = mesh.shape["lat"] == 2 and mesh.shape["dp"] == 16
    return jax.shard_map(
        shards_paired if paired else shards_general,
        mesh=mesh,
        in_specs=(
            P("dp", "lat", None, None),
            P("dp", None, "lat", None),
            P("dp"),
            P("lat", "dp"),
            P(("dp", "lat")),
            P("dp", "lat", None, None),
        ),
        out_specs=(
            P("dp", "lat", None, None),
            P("dp", "lat", None, None),
            P("lat", "dp"),
            P(("dp", "lat")),
        ),
        check_vma=False,
    )
```
